32 devices in a mesh: grp: 2 (over core), wide: 16 (over z, y, x).
Axes of the slice: x: 2, y: 2, z: 4, core: 2. Of those that a mesh axis runs over, the one named last changes fastest.
Arguments:
- hidden_in: bfloat16 [32768, 768], P(('grp', 'wide')), may hold values from -6 to 6
- valid_mask: int32 [32768], P(('grp', 'wide')), may hold values from 0 to 1, as said below
- bucket: int32 [64], P(('grp', 'wide')), may hold values from 0 to 1, as said below
- in_weight: bfloat16 [768, 1536], replicated, may hold values from -0.21875 to 0.21875
- in_bias: float32 [4, 384], replicated, may hold values from -3 to 3
- depth_weight: float32 [9, 768], replicated, may hold values from -2 to 2
- point_weight: bfloat16 [768, 384], replicated, may hold values from -0.21875 to 0.21875
- kernel_weight: bfloat16 [384, 54], replicated, may hold values from -0.3125 to 0.3125
- kernel_bias: float32 [54], replicated, may hold values from -3 to 3
- out_weight: bfloat16 [768, 768], replicated, may hold values from -0.875 to 0.875
- out_bias: float32 [768], replicated, may hold values from -2 to 2
- norm_gain: float32 [2, 768], replicated, may hold values from 0.5 to 1.5
- norm_bias: float32 [2, 768], replicated, may hold values from -2 to 2
- ffn_in: bfloat16 [2, 1536, 384], P('grp', 'wide'), may hold values from -0.3125 to 0.3125
- ffn_in_bias: bfloat16 [2, 1536], P('grp', 'wide'), may hold values from -3 to 3
- ffn_out: bfloat16 [2, 1536, 384], P('grp', 'wide'), may hold values from -0.15625 to 0.15625
- ffn_out_bias: float32 [2, 384], P('grp'), may hold values from -2 to 2
- out_grad: bfloat16 [32768, 768], P(('grp', 'wide')), may hold values from -6 to 6
Outputs:
- output: bfloat16 [32768, 768], P(('grp', 'wide'))
- hidden_grad: float32 [32768, 768], P(('grp', 'wide'))
- in_weight_grad: float32 [768, 1536], replicated
- in_bias_grad: float32 [4, 384], replicated
- depth_weight_grad: float32 [9, 768], replicated
- point_weight_grad: float32 [768, 384], replicated
- kernel_weight_grad: float32 [384, 54], replicated
- kernel_bias_grad: float32 [54], replicated
- out_weight_grad: float32 [768, 768], replicated
- out_bias_grad: float32 [768], replicated
- norm_gain_grad: float32 [2, 768], replicated
- norm_bias_grad: float32 [2, 768], replicated
- ffn_in_grad: float32 [2, 1536, 384], P('grp', 'wide')
- ffn_in_bias_grad: float32 [2, 1536], P('grp', 'wide')
- ffn_out_grad: float32 [2, 1536, 384], P('grp', 'wide')
- ffn_out_bias_grad: float32 [2, 384], P('grp')
The draws below stay inside these ranges and needn't reach their ends.
Inputs may be any that keep to these rules, and one draw needn't show every extreme that they name: `valid_mask`: 1 marks a real token, 0 padding. Every sequence (one slot of 512 rows in a block of bucket 0, each of 4 slots of 128 rows in a block of bucket 1) has its real tokens first and at least one of them; some slot of each kind has no padding. `bucket`: 0: the block holds one sequence of 512 rows; 1: 4 sequences of 128 rows. Both kinds occur.
All inputs are finite; a program needn't handle non-finite values.
Results may differ from the reference program's by a relative error of at most 0.017.
Values may be sent and summed in bfloat16 or wider, within the bound.
No kernel may reach another device: no remote copies, remote signals or barrier semaphores. Data moves between devices by JAX's collectives and lax.ppermute only.
A program may use at most 256 MiB of HBM per device.

```python
import math
import jax
import jax.numpy as jnp
from jax import lax

D = 768
HEADS = 6
HEAD = 64
KERNEL = 9
GROUPS = 2
FF_G = 1536
AH = 384
GW = 384
BLOCK = 512
SHORT = 128
SLOTS = 4
NBLOCKS = 64
TOKENS = 32768


def block_layout(key):
    key_kind, key_order, key_long, key_short = jax.random.split(key, 4)
    bucket_kind = (jax.random.randint(key_kind, (NBLOCKS,), 0, 5) == 0).astype(jnp.int32)
    block_order = jax.random.permutation(key_order, NBLOCKS)
    bucket_kind = bucket_kind.at[block_order[0]].set(0).at[block_order[1]].set(1)
    long_length = jax.random.randint(key_long, (NBLOCKS,), BLOCK // 2, BLOCK + 1)
    long_length = long_length.at[block_order[0]].set(BLOCK)
    short_length = jax.random.randint(key_short, (NBLOCKS, SLOTS), SHORT // 4, SHORT + 1)
    short_length = short_length.at[block_order[1], 0].set(SHORT).at[block_order[1], 1].set(SHORT // 4)
    places = jnp.arange(BLOCK, dtype=jnp.int32)
    long_mask = places[None, :] < long_length[:, None]
    short_bound = jnp.repeat(short_length, SHORT, axis=1)
    short_mask = (places % SHORT)[None, :] < short_bound
    padding = jnp.where(bucket_kind[:, None] == 0, long_mask, short_mask).astype(jnp.int32)
    return (bucket_kind, padding.reshape(TOKENS))


def draw_valid_mask(key, part):
    layout = block_layout(key)
    return layout[1]


def draw_bucket(key, part):
    layout = block_layout(key)
    return layout[0]


def steps_of(rng, extent, shards, least, largest):
    factor_of = 1.0
    for dim, shards_of in shards:
        draws = jax.random.uniform(jax.random.fold_in(jax.random.fold_in(rng, 6), dim), (shards_of,), jnp.float32, least / len(shards), largest / len(shards))
        factor_of = factor_of * jnp.repeat(jnp.exp(draws), extent[dim] // shards_of).reshape((-1,) + (1,) * (len(extent) - 1 - dim))
    return factor_of


def gaussian(own_key, dims, scale, reach, cuts=(), kind=jnp.bfloat16):
    gain = steps_of(own_key, dims, cuts, -0.22, 0.18) if cuts else 1.0
    entries = jax.random.normal(own_key, dims, jnp.float32) * scale * gain
    return jnp.minimum(jnp.maximum(entries, -reach), reach).astype(kind)


def setup_inputs(seed: int = 0) -> dict:
    splits = jax.random.split(jax.random.key(seed), 19)
    hidden_in = gaussian(splits[0], (TOKENS, D), 1.0, 6.0, ((0, 32),))
    valid_mask = draw_valid_mask(jax.random.fold_in(splits[18], 71), 0)
    bucket = draw_bucket(jax.random.fold_in(splits[18], 71), 0)
    in_weight = gaussian(splits[3], (D, 4 * AH), D ** -0.5, 0.21875)
    in_bias = gaussian(splits[4], (4, AH), 0.5, 3.0, (), jnp.float32)
    depth_weight = gaussian(splits[5], (KERNEL, D), KERNEL ** -0.5, 2.0, (), jnp.float32)
    point_weight = gaussian(splits[6], (D, AH), D ** -0.5, 0.21875)
    kernel_weight = gaussian(splits[7], (AH, HEADS * KERNEL), AH ** -0.5, 0.3125)
    kernel_bias = gaussian(splits[8], (HEADS * KERNEL,), 0.5, 3.0, (), jnp.float32)
    out_weight = gaussian(splits[9], (D, D), (D // 16) ** -0.5, 0.875)
    out_bias = gaussian(splits[10], (D,), 0.3, 2.0, (), jnp.float32)
    norm_gain = jnp.clip(1.0 + 0.1 * jax.random.normal(splits[11], (2, D), jnp.float32), 0.5, 1.5)
    norm_bias = gaussian(splits[12], (2, D), 0.3, 2.0, (), jnp.float32)
    ffn_in = gaussian(splits[13], (GROUPS, FF_G, GW), GW ** -0.5, 0.3125, ((0, 2), (1, 16)))
    ffn_in_bias = gaussian(splits[14], (GROUPS, FF_G), 0.5, 3.0, ((0, 2), (1, 16)))
    ffn_out = gaussian(splits[15], (GROUPS, FF_G, GW), FF_G ** -0.5, 0.15625, ((0, 2), (1, 16)))
    ffn_out_bias = gaussian(splits[16], (GROUPS, GW), 0.3, 2.0, ((0, 2),), jnp.float32)
    out_grad = gaussian(splits[17], (TOKENS, D), 1.0, 6.0, ((0, 32),))
    return {"hidden_in": hidden_in, "valid_mask": valid_mask, "bucket": bucket, "in_weight": in_weight, "in_bias": in_bias, "depth_weight": depth_weight, "point_weight": point_weight, "kernel_weight": kernel_weight, "kernel_bias": kernel_bias, "out_weight": out_weight, "out_bias": out_bias, "norm_gain": norm_gain, "norm_bias": norm_bias, "ffn_in": ffn_in, "ffn_in_bias": ffn_in_bias, "ffn_out": ffn_out, "ffn_out_bias": ffn_out_bias, "out_grad": out_grad}


@jax.custom_vjp
def low(v):
    return lax.optimization_barrier(v.astype(jnp.bfloat16)).astype(jnp.float32)

@jax.custom_vjp
def low_back(v):
    return v

def low_keep(v):
    return (low(v), None)

def low_pass(kept, grad):
    return (grad,)

def back_keep(v):
    return (v, None)

def back_low(kept, grad):
    return (low(grad),)
low.defvjp(low_keep, low_pass)
low_back.defvjp(back_keep, back_low)
PRECISE = lax.Precision.HIGHEST
EPSILON = 1e-12

def norm_rows(values, scale_row, shift_row):
    row_mean = lax.optimization_barrier(jnp.mean(values, axis=-1, keepdims=True))
    centred = values - row_mean
    row_var = lax.optimization_barrier(jnp.mean(centred * centred, axis=-1, keepdims=True))
    return centred * lax.rsqrt(row_var + EPSILON) * scale_row + shift_row

def gelu_exact(values):
    return 0.5 * values * (1.0 + jax.scipy.special.erf(values * 0.7071067811865476))

def softmax_last(values):
    row_max = lax.optimization_barrier(jnp.max(values, axis=-1, keepdims=True))
    exp_values = jnp.exp(values - row_max)
    return exp_values / lax.optimization_barrier(jnp.sum(exp_values, axis=-1, keepdims=True))

def slot_geometry(bucket):
    positions = jnp.arange(BLOCK, dtype=jnp.int32)
    slot_span = jnp.where(bucket[:, None] == 0, BLOCK, SHORT).astype(jnp.int32)
    slot_place = positions[None, :] % slot_span
    slot_index = positions[None, :] // slot_span
    return (slot_place, slot_span, slot_index)

def shifted(source, offset, slot_place, slot_span):
    edge = (KERNEL - 1) // 2
    padded = jnp.pad(source, ((0, 0), (edge, edge), (0, 0)))
    moved = lax.slice_in_dim(padded, edge + offset, edge + offset + BLOCK, axis=1)
    inside = (slot_place + offset >= 0) & (slot_place + offset < slot_span)
    return jnp.where(inside[:, :, None], moved, 0.0)

def layer_blocks(inputs, valid_mask, bucket, weights):
    in_weight, in_bias, depth_weight, point_weight, kernel_weight, kernel_bias, out_weight, out_bias, norm_gain, norm_bias, ffn_in, ffn_in_bias, ffn_out, ffn_out_bias = weights
    count = inputs.shape[0]
    edge = (KERNEL - 1) // 2
    slot_place, slot_span, slot_index = slot_geometry(bucket)
    projected = low_back(jnp.einsum('cti,ij->ctj', inputs, in_weight, precision=PRECISE))
    queries = low(projected[..., :AH] + in_bias[0])
    keys_low = low(projected[..., AH:2 * AH])
    values_low = low(projected[..., 2 * AH:3 * AH] + in_bias[1])
    conv_values = low(projected[..., 3 * AH:] + in_bias[2])
    depthwise = sum((shifted(inputs, j - edge, slot_place, slot_span) * depth_weight[j] for j in range(KERNEL)))
    key_conv = low_back(jnp.einsum('cti,ij->ctj', low(depthwise), point_weight, precision=PRECISE)) + in_bias[3]
    conv_in = low(key_conv * queries)
    logits = low_back(jnp.einsum('cti,ij->ctj', conv_in, kernel_weight, precision=PRECISE)) + kernel_bias
    conv_kernel = softmax_last(logits.reshape(count, BLOCK, HEADS, KERNEL))
    conv_out = sum((shifted(conv_values, j - edge, slot_place, slot_span).reshape(count, BLOCK, HEADS, HEAD) * conv_kernel[..., j:j + 1] for j in range(KERNEL)))
    conv_out = conv_out.reshape(count, BLOCK, AH)
    query_heads = queries.reshape(count, BLOCK, HEADS, HEAD)
    key_heads = keys_low.reshape(count, BLOCK, HEADS, HEAD)
    value_heads = values_low.reshape(count, BLOCK, HEADS, HEAD)
    raw_scores = low_back(jnp.einsum('cqhd,ckhd->chqk', query_heads, key_heads, precision=PRECISE))
    allowed = (slot_index[:, :, None] == slot_index[:, None, :]) & (valid_mask[:, None, :] > 0)
    scores = jnp.where(allowed[:, None], raw_scores * HEAD ** (-0.5), -1e+30)
    attn_probs = softmax_last(scores)
    context = jnp.einsum('chqk,ckhd->cqhd', low(attn_probs), value_heads, precision=PRECISE)
    context = context.reshape(count, BLOCK, AH)
    mixed = low(low_back(jnp.concatenate([context, conv_out], axis=-1)))
    attended = low_back(jnp.einsum('cti,ij->ctj', mixed, out_weight, precision=PRECISE)) + out_bias + inputs
    normed = norm_rows(attended, norm_gain[0], norm_bias[0])
    ffn_input = low(low_back(normed)).reshape(count, BLOCK, GROUPS, GW)
    ffn_pre = low_back(jnp.einsum('btgi,gfi->btgf', ffn_input, ffn_in, precision=PRECISE)) + ffn_in_bias
    ffn_act = low(gelu_exact(ffn_pre))
    ffn_output = low(low_back(jnp.einsum('btgf,gfi->btgi', ffn_act, ffn_out, precision=PRECISE) + ffn_out_bias))
    summed = ffn_output.reshape(count, BLOCK, D) + normed
    return norm_rows(summed, norm_gain[1], norm_bias[1])

def reference(hidden_in, valid_mask, bucket, in_weight, in_bias, depth_weight, point_weight, kernel_weight, kernel_bias, out_weight, out_bias, norm_gain, norm_bias, ffn_in, ffn_in_bias, ffn_out, ffn_out_bias, out_grad):
    per_step = math.gcd(NBLOCKS, 8)
    steps_count = NBLOCKS // per_step
    params = tuple((item.astype(jnp.float32) for item in (in_weight, in_bias, depth_weight, point_weight, kernel_weight, kernel_bias, out_weight, out_bias, norm_gain, norm_bias, ffn_in, ffn_in_bias, ffn_out, ffn_out_bias)))
    inputs = hidden_in.astype(jnp.float32).reshape(steps_count, per_step, BLOCK, D)
    mask_steps = valid_mask.reshape(steps_count, per_step, BLOCK)
    bucket_steps = bucket.reshape(steps_count, per_step)

    def forward(inputs_all, weights):

        def one_step(pieces):
            return layer_blocks(pieces[0], pieces[1], pieces[2], weights)
        return lax.map(jax.checkpoint(one_step), (inputs_all, mask_steps, bucket_steps))
    result_out, pullback = jax.vjp(forward, inputs, params)
    grad_inputs, weight_grads = pullback(out_grad.astype(jnp.float32).reshape(result_out.shape))
    output = result_out.reshape(TOKENS, D).astype(jnp.bfloat16)
    hidden_grad = grad_inputs.reshape(TOKENS, D)
    return (output, hidden_grad, weight_grads[0], weight_grads[1], weight_grads[2], weight_grads[3], weight_grads[4], weight_grads[5], weight_grads[6], weight_grads[7], weight_grads[8], weight_grads[9], weight_grads[10], weight_grads[11], weight_grads[12], weight_grads[13])
```

```python
import functools
import jax
import jax.numpy as jnp
from jax import lax
from jax.experimental import pallas as pl
from jax.experimental.pallas import tpu as pltpu
from jax.sharding import PartitionSpec as P

HEADS = 6
HEAD = 64
KERNEL = 9
EDGE = 4
BLOCK = 512
SHORT = 128
CHUNKS = BLOCK // SHORT
WIDTH = HEADS * HEAD
DIM = 2 * WIDTH
SLAB = 128
TAPS = KERNEL * SLAB
HALO = 8
PADDED = SHORT + 2 * HALO
EPSILON = 1e-12
BF = jnp.bfloat16
F32 = jnp.float32
VMEM_LIMIT = 60 * 1024 * 1024


def mm(a, b):
    return lax.dot_general(a, b, (((1,), (0,)), ((), ())), preferred_element_type=F32)


def mm_nt(a, b):
    return lax.dot_general(a, b, (((1,), (1,)), ((), ())), preferred_element_type=F32)


def mm_tn(a, b):
    return lax.dot_general(a, b, (((0,), (0,)), ((), ())), preferred_element_type=F32)


def col_sum(v):
    return jnp.sum(v, axis=0, keepdims=True)


def params(limit=VMEM_LIMIT):
    return pltpu.CompilerParams(vmem_limit_bytes=limit)


def whole(shape):
    return pl.BlockSpec(shape, lambda *_: (0,) * len(shape))


def rows(tile, width, lane=0):
    return pl.BlockSpec((tile, width), lambda i, *_: (i, lane))


def sds(shape, dtype):
    return jax.ShapeDtypeStruct(shape, dtype)


def fill_padded(pad_ref, values, joined):
    n = values.shape[1]
    zero = jnp.zeros((HALO, n), F32)
    for s in range(CHUNKS):
        lo, hi = s * SHORT, (s + 1) * SHORT
        pad_ref[s, HALO : HALO + SHORT, :] = values[lo:hi]
        pad_ref[s, 0:HALO, :] = values[lo - HALO : lo] * joined if s else zero
        pad_ref[s, HALO + SHORT :, :] = (
            values[hi : hi + HALO] * joined if s < CHUNKS - 1 else zero
        )


def tap(pad_ref, s, offset, lo, hi):
    return pad_ref[s, HALO + offset : HALO + offset + SHORT, lo:hi]


def slab_select(rows_of):
    source = lax.broadcasted_iota(jnp.int32, (rows_of, TAPS), 0)
    target = lax.broadcasted_iota(jnp.int32, (rows_of, TAPS), 1)
    head = target % SLAB
    hit = (head < HEADS) & (source == head * KERNEL + target // SLAB)
    return hit.astype(F32)


def head_spread():
    source = lax.broadcasted_iota(jnp.int32, (SLAB, WIDTH), 0)
    target = lax.broadcasted_iota(jnp.int32, (SLAB, WIDTH), 1)
    return (source == target // HEAD).astype(BF)


def norm_stats(v):
    mean = jnp.mean(v, axis=-1, keepdims=True)
    centred = v - mean
    var = jnp.mean(centred * centred, axis=-1, keepdims=True)
    inv = lax.rsqrt(var + EPSILON)
    return centred * inv, inv


def norm_back(d_scaled, hat, inv):
    first = jnp.mean(d_scaled, axis=-1, keepdims=True)
    second = jnp.mean(d_scaled * hat, axis=-1, keepdims=True)
    return inv * (d_scaled - first - hat * second)


def normal_cdf(v):
    bell = jnp.exp(v * v * -0.5)
    den = 1.0 + 0.23164189 * jnp.abs(v)
    t = pl.reciprocal(den, approx=True)
    t = t * (2.0 - den * t)
    poly = 0.5 * 1.061405429
    poly = poly * t + 0.5 * -1.453152027
    poly = poly * t + 0.5 * 1.421413741
    poly = poly * t + 0.5 * -0.284496736
    poly = poly * t + 0.5 * 0.254829592
    tail = poly * t * bell
    return jnp.where(v < 0.0, tail, 1.0 - tail), bell


def project_kernel(
    bucket, x, w, bias, dw, pw, kw, kb, qkvc, dep, kc, ks, co, xpad, cvpad
):
    joined = jnp.where(bucket[pl.program_id(0)] == 0, 1.0, 0.0).astype(F32)
    xb = x[...]
    proj = mm(xb, w[...])
    q = (proj[:, :WIDTH] + bias[0:1, :]).astype(BF)
    qkvc[:, 0:WIDTH] = q
    qkvc[:, WIDTH : 2 * WIDTH] = proj[:, WIDTH : 2 * WIDTH].astype(BF)
    qkvc[:, 2 * WIDTH : 3 * WIDTH] = (
        proj[:, 2 * WIDTH : 3 * WIDTH] + bias[1:2, :]
    ).astype(BF)
    cv = (proj[:, 3 * WIDTH :] + bias[2:3, :]).astype(BF)
    qkvc[:, 3 * WIDTH :] = cv
    fill_padded(xpad, xb.astype(F32), joined)
    fill_padded(cvpad, cv.astype(F32), joined)
    for s in range(CHUNKS):
        for lo in range(0, DIM, 256):
            acc = tap(xpad, s, -EDGE, lo, lo + 256) * dw[0:1, lo : lo + 256]
            for j in range(1, KERNEL):
                acc += tap(xpad, s, j - EDGE, lo, lo + 256) * dw[j : j + 1, lo : lo + 256]
            dep[s * SHORT : (s + 1) * SHORT, lo : lo + 256] = acc.astype(BF)
    key_conv = mm(dep[...], pw[...]) + bias[3:4, :]
    kc[...] = key_conv
    conv_in = (key_conv * q.astype(F32)).astype(BF)
    select = slab_select(HEADS * KERNEL)
    kw_slab = mm(kw[...], select.astype(BF)).astype(BF)
    kb_slab = jnp.dot(
        jnp.broadcast_to(kb[...], (8, HEADS * KERNEL)),
        select,
        precision=lax.Precision.HIGHEST,
        preferred_element_type=F32,
    )[0:1]
    logits = mm(conv_in, kw_slab) + kb_slab
    slabs = [logits[:, j * SLAB : (j + 1) * SLAB] for j in range(KERNEL)]
    top = functools.reduce(jnp.maximum, slabs)
    slabs = [jnp.exp(v - top) for v in slabs]
    inv = 1.0 / functools.reduce(jnp.add, slabs)
    for j in range(KERNEL):
        ks[:, j * SLAB : (j + 1) * SLAB] = (slabs[j] * inv).astype(BF)
    spread = head_spread()
    acc = None
    for j in range(KERNEL):
        weight = mm(ks[:, j * SLAB : (j + 1) * SLAB], spread)
        moved = cvpad[:, HALO + j - EDGE : HALO + j - EDGE + SHORT, :].reshape(BLOCK, WIDTH)
        acc = weight * moved if acc is None else acc + weight * moved
    co[...] = acc.astype(BF)


def project(bucket, x, in_weight, in_bias, depth_weight, point_weight, kernel_weight, kernel_bias):
    count = x.shape[0]
    blocks = count // BLOCK
    taps = HEADS * KERNEL
    return pl.pallas_call(
        project_kernel,
        grid_spec=pltpu.PrefetchScalarGridSpec(
            num_scalar_prefetch=1,
            grid=(blocks,),
            in_specs=[
                rows(BLOCK, DIM),
                whole((DIM, 4 * WIDTH)),
                whole((4, WIDTH)),
                whole((KERNEL, DIM)),
                whole((DIM, WIDTH)),
                whole((WIDTH, taps)),
                whole((1, taps)),
            ],
            out_specs=[
                rows(BLOCK, 4 * WIDTH),
                rows(BLOCK, DIM),
                rows(BLOCK, WIDTH),
                rows(BLOCK, TAPS),
                rows(BLOCK, WIDTH),
            ],
            scratch_shapes=[
                pltpu.VMEM((CHUNKS, PADDED, DIM), F32),
                pltpu.VMEM((CHUNKS, PADDED, WIDTH), F32),
            ],
        ),
        out_shape=[
            sds((count, 4 * WIDTH), BF),
            sds((count, DIM), BF),
            sds((count, WIDTH), F32),
            sds((count, TAPS), BF),
            sds((count, WIDTH), BF),
        ],
        compiler_params=params(),
        cost_estimate=pl.CostEstimate(
            flops=2 * count * DIM * 6 * WIDTH, bytes_accessed=20 << 20, transcendentals=0
        ),
        name="project",
    )(bucket, x, in_weight, in_bias, depth_weight, point_weight, kernel_weight, kernel_bias)


def mask_bias(is_short, valid_row):
    column = jnp.transpose(jnp.broadcast_to(valid_row.astype(F32), (SLAB, BLOCK)))
    column = jnp.concatenate([column] * (BLOCK // SLAB), axis=1)
    key_slot = (lax.broadcasted_iota(jnp.int32, (BLOCK, BLOCK), 0) // SHORT) * is_short
    query_slot = (lax.broadcasted_iota(jnp.int32, (BLOCK, BLOCK), 1) // SHORT) * is_short
    return jnp.where((key_slot == query_slot) & (column > 0.0), 0.0, -1e30)


def half_mask(v, h):
    lane = lax.broadcasted_iota(jnp.int32, v.shape, 1)
    keep = lane < HEAD if h % 2 == 0 else lane >= HEAD
    return jnp.where(keep, v, jnp.zeros_like(v))


def attend_kernel(bucket, valid, q, k, v, co, mixed, logs, bias, context):
    bias[...] = mask_bias(bucket[pl.program_id(0)], valid[...].reshape(1, BLOCK))
    vt = jnp.transpose(v[...])
    logs[...] = jnp.zeros_like(logs)
    for h in range(HEADS):
        lo = (h // 2) * SLAB
        qm = half_mask(q[:, lo : lo + SLAB], h) * jnp.asarray(HEAD**-0.5, BF)
        scores = mm_nt(k[:, lo : lo + SLAB], qm) + bias[...]
        top = jnp.max(scores, axis=0, keepdims=True)
        e = jnp.exp(scores - top)
        total = jnp.sum(e, axis=0, keepdims=True)
        part = mm(vt[h * HEAD : (h + 1) * HEAD], e.astype(BF))
        context[h * HEAD : (h + 1) * HEAD, :] = part / total
        logs[0, h : h + 1, :] = top + jnp.log(total)
    mixed[:, :WIDTH] = jnp.transpose(context[...]).astype(BF)
    mixed[:, WIDTH:] = co[...]


def attend(bucket, valid, qkvc, conv_out):
    count = qkvc.shape[0]
    blocks = count // BLOCK
    return pl.pallas_call(
        attend_kernel,
        grid_spec=pltpu.PrefetchScalarGridSpec(
            num_scalar_prefetch=1,
            grid=(blocks,),
            in_specs=[
                pl.BlockSpec((1, 1, BLOCK), lambda i, *_: (i, 0, 0)),
                rows(BLOCK, WIDTH, 0),
                rows(BLOCK, WIDTH, 1),
                rows(BLOCK, WIDTH, 2),
                rows(BLOCK, WIDTH),
            ],
            out_specs=[
                rows(BLOCK, DIM),
                pl.BlockSpec((1, 8, BLOCK), lambda i, *_: (i, 0, 0)),
            ],
            scratch_shapes=[
                pltpu.VMEM((BLOCK, BLOCK), F32),
                pltpu.VMEM((WIDTH, BLOCK), F32),
            ],
        ),
        out_shape=[sds((count, DIM), BF), sds((blocks, 8, BLOCK), F32)],
        compiler_params=params(),
        cost_estimate=pl.CostEstimate(
            flops=8 * count * BLOCK * WIDTH, bytes_accessed=8 << 20, transcendentals=0
        ),
        name="attend",
    )(bucket, valid, qkvc, qkvc, qkvc, conv_out)


def middle_kernel(
    group, x, mixed, grad, w_out, b_out, gain, shift, b2, w1a, w2a, w1b, w2b, b1a, b1b,
    output, d_att, d_mixed, xin, dback, act_a, act_b, dpre_a, dpre_b, sums, sums_a, sums_b,
    normed, hat1, ffn_out, d_summed, slope, datt_low,
):
    tile = x.shape[0]
    hidden = w1a.shape[0]
    part = 512
    own = pl.multiple_of(group[0] * WIDTH, SLAB)
    other = pl.multiple_of((1 - group[0]) * WIDTH, SLAB)

    @pl.when(pl.program_id(0) == 0)
    def _():
        sums[...] = jnp.zeros_like(sums)
        sums_a[...] = jnp.zeros_like(sums_a)
        sums_b[...] = jnp.zeros_like(sums_b)

    att = mm(mixed[...], w_out[...]) + b_out[...] + x[...].astype(F32)
    hat, inv1 = norm_stats(att)
    hat1[...] = hat
    y = hat * gain[0:1, :] + shift[0:1, :]
    normed[...] = y
    xin[...] = y.astype(BF)
    for base, w1, w2, b1, act, at in (
        (own, w1a, w2a, b1a, act_a, 0),
        (other, w1b, w2b, b1b, act_b, hidden),
    ):
        xg = xin[:, pl.ds(base, WIDTH)]
        for lo in range(0, hidden, part):
            pre = mm_nt(xg, w1[lo : lo + part, :]) + b1[:, lo : lo + part]
            cdf, bell = normal_cdf(pre)
            act[:, lo : lo + part] = (pre * cdf).astype(BF)
            slope[:, at + lo : at + lo + part] = cdf + pre * bell * 0.3989422804014327
        ffn_out[:, pl.ds(base, WIDTH)] = mm(act[...], w2[...])
    result = (ffn_out[...] + b2[...]).astype(BF).astype(F32)
    hat2, inv2 = norm_stats(result + normed[...])
    output[...] = (hat2 * gain[1:2, :] + shift[1:2, :]).astype(BF)
    dy = grad[...].astype(F32)
    sums[1:2, :] += col_sum(dy * hat2)
    sums[3:4, :] += col_sum(dy)
    ds = norm_back(dy * gain[1:2, :], hat2, inv2)
    d_summed[...] = ds
    low = ds.astype(BF)
    dback[...] = low
    sums[5:6, :] += col_sum(low.astype(F32))
    for base, w1, w2, dpre, bsum, at in (
        (own, w1a, w2a, dpre_a, sums_a, 0),
        (other, w1b, w2b, dpre_b, sums_b, hidden),
    ):
        dg = dback[:, pl.ds(base, WIDTH)]
        for lo in range(0, hidden, part):
            dp = mm_nt(dg, w2[lo : lo + part, :]) * slope[:, at + lo : at + lo + part]
            bsum[:, lo : lo + part] += col_sum(dp)
            dpre[:, lo : lo + part] = dp.astype(BF)
        ffn_out[:, pl.ds(base, WIDTH)] = mm(dpre[...], w1[...])
    dn = d_summed[...] + ffn_out[...].astype(BF).astype(F32)
    hat = hat1[...]
    sums[0:1, :] += col_sum(dn * hat)
    sums[2:3, :] += col_sum(dn)
    da = norm_back(dn * gain[0:1, :], hat, inv1)
    d_att[...] = da
    sums[4:5, :] += col_sum(da)
    datt_low[...] = da.astype(BF)
    d_mixed[...] = mm_nt(datt_low[...], w_out[...]).astype(BF)


def middle(group, x, mixed, grad, out_weight, out_bias, norm_gain, norm_bias, b2, w1a, w2a, w1b, w2b, b1a, b1b):
    count = x.shape[0]
    hidden = w1a.shape[0]
    tile = BLOCK
    return pl.pallas_call(
        middle_kernel,
        grid_spec=pltpu.PrefetchScalarGridSpec(
            num_scalar_prefetch=1,
            grid=(count // tile,),
            in_specs=[
                rows(tile, DIM),
                rows(tile, DIM),
                rows(tile, DIM),
                whole((DIM, DIM)),
                whole((1, DIM)),
                whole((2, DIM)),
                whole((2, DIM)),
                whole((1, DIM)),
                whole((hidden, WIDTH)),
                whole((hidden, WIDTH)),
                whole((hidden, WIDTH)),
                whole((hidden, WIDTH)),
                whole((1, hidden)),
                whole((1, hidden)),
            ],
            out_specs=[
                rows(tile, DIM),
                rows(tile, DIM),
                rows(tile, DIM),
                rows(tile, DIM),
                rows(tile, DIM),
                rows(tile, hidden),
                rows(tile, hidden),
                rows(tile, hidden),
                rows(tile, hidden),
                whole((8, DIM)),
                whole((1, hidden)),
                whole((1, hidden)),
                ],
            scratch_shapes=[
                pltpu.VMEM((tile, DIM), F32),
                pltpu.VMEM((tile, DIM), F32),
                pltpu.VMEM((tile, DIM), F32),
                pltpu.VMEM((tile, DIM), F32),
                pltpu.VMEM((tile, 2 * hidden), F32),
                pltpu.VMEM((tile, DIM), BF),
            ],
        ),
        out_shape=[
            sds((count, DIM), BF),
            sds((count, DIM), F32),
            sds((count, DIM), BF),
            sds((count, DIM), BF),
            sds((count, DIM), BF),
            sds((count, hidden), BF),
            sds((count, hidden), BF),
            sds((count, hidden), BF),
            sds((count, hidden), BF),
            sds((8, DIM), F32),
            sds((1, hidden), F32),
            sds((1, hidden), F32),
        ],
        compiler_params=params(),
        cost_estimate=pl.CostEstimate(
            flops=18 * count * hidden * DIM, bytes_accessed=40 << 20, transcendentals=0
        ),
        name="middle",
    )(group, x, mixed, grad, out_weight, out_bias, norm_gain, norm_bias, b2, w1a, w2a, w1b, w2b, b1a, b1b)


def ffn_grad_kernel(group, dpre, act, xin, dback, first, second):
    first[...] = mm_tn(dpre[...], xin[...]).astype(BF)
    second[...] = mm_tn(act[...], dback[...]).astype(BF)


def ffn_grad(group, dpre, act, xin, dback):
    count, hidden = dpre.shape
    tile = 384
    lanes = pl.BlockSpec((count, tile), lambda i, g: (0, i))
    side = pl.BlockSpec((count, WIDTH), lambda i, g: (0, g[0]))
    out = pl.BlockSpec((tile, WIDTH), lambda i, g: (i, 0))
    return pl.pallas_call(
        ffn_grad_kernel,
        grid_spec=pltpu.PrefetchScalarGridSpec(
            num_scalar_prefetch=1,
            grid=(hidden // tile,),
            in_specs=[lanes, lanes, side, side],
            out_specs=[out, out],
        ),
        out_shape=[sds((hidden, WIDTH), BF)] * 2,
        compiler_params=params(),
        cost_estimate=pl.CostEstimate(
            flops=4 * count * hidden * WIDTH, bytes_accessed=10 << 20, transcendentals=0
        ),
        name="ffn_grad",
    )(group, dpre, act, xin, dback)


def tn_kernel(a, b, out):
    out[...] = mm_tn(a[...], b[...].astype(BF)).astype(out.dtype)


def tn_matmul(a, b, name, tile=384):
    count, m = a.shape
    n = b.shape[1]
    return pl.pallas_call(
        tn_kernel,
        grid=(m // tile,),
        in_specs=[pl.BlockSpec((count, tile), lambda i: (0, i)), whole((count, n))],
        out_specs=pl.BlockSpec((tile, n), lambda i: (i, 0)),
        out_shape=sds((m, n), BF),
        compiler_params=params(),
        cost_estimate=pl.CostEstimate(
            flops=2 * count * m * n, bytes_accessed=6 << 20, transcendentals=0
        ),
        name=name,
    )(a, b)


def attend_back_kernel(bucket, valid, q, k, v, dctx, logs, dq, dkv, sums, bias, dqt):
    @pl.when(pl.program_id(0) == 0)
    def _():
        sums[...] = jnp.zeros_like(sums)

    bias[...] = mask_bias(bucket[pl.program_id(0)], valid[...].reshape(1, BLOCK))
    scale = jnp.asarray(HEAD**-0.5, BF)
    kt = jnp.transpose(k[...] * scale)
    for pair in range(HEADS // 2):
        lo = pair * SLAB
        kp = k[:, lo : lo + SLAB]
        vp = v[:, lo : lo + SLAB]
        dk = dv = None
        for h in (2 * pair, 2 * pair + 1):
            qm = half_mask(q[:, lo : lo + SLAB], h) * scale
            cm = half_mask(dctx[:, lo : lo + SLAB], h)
            probs = jnp.exp(mm_nt(kp, qm) + bias[...] - logs[0, h : h + 1, :])
            d_probs = mm_nt(vp, cm)
            delta = col_sum(probs * d_probs)
            d_scores = (probs * (d_probs - delta)).astype(BF)
            probs = probs.astype(BF)
            dv = mm(probs, cm) if dv is None else dv + mm(probs, cm)
            dk = mm(d_scores, qm) if dk is None else dk + mm(d_scores, qm)
            dqt[h * HEAD : (h + 1) * HEAD, :] = mm(kt[h * HEAD : (h + 1) * HEAD], d_scores)
        dkv[:, lo : lo + SLAB] = dk.astype(BF)
        dkv[:, WIDTH + lo : WIDTH + lo + SLAB] = dv.astype(BF)
        sums[0:1, lo : lo + SLAB] += col_sum(dv)
    dq[...] = jnp.transpose(dqt[...])


def attend_back(bucket, valid, qkvc, d_mixed, logs):
    count = qkvc.shape[0]
    blocks = count // BLOCK
    return pl.pallas_call(
        attend_back_kernel,
        grid_spec=pltpu.PrefetchScalarGridSpec(
            num_scalar_prefetch=1,
            grid=(blocks,),
            in_specs=[
                pl.BlockSpec((1, 1, BLOCK), lambda i, *_: (i, 0, 0)),
                rows(BLOCK, WIDTH, 0),
                rows(BLOCK, WIDTH, 1),
                rows(BLOCK, WIDTH, 2),
                rows(BLOCK, WIDTH, 0),
                pl.BlockSpec((1, 8, BLOCK), lambda i, *_: (i, 0, 0)),
            ],
            out_specs=[rows(BLOCK, WIDTH), rows(BLOCK, DIM), whole((8, WIDTH))],
            scratch_shapes=[
                pltpu.VMEM((BLOCK, BLOCK), F32),
                pltpu.VMEM((WIDTH, BLOCK), F32),
            ],
        ),
        out_shape=[sds((count, WIDTH), F32), sds((count, DIM), BF), sds((8, WIDTH), F32)],
        compiler_params=params(),
        cost_estimate=pl.CostEstimate(
            flops=20 * count * BLOCK * WIDTH, bytes_accessed=8 << 20, transcendentals=0
        ),
        name="attend_back",
    )(bucket, valid, qkvc, qkvc, qkvc, d_mixed, logs)


def conv_back_kernel(
    bucket, q, cv, dconv, kc, ks, dq, kw, dqc, dkc, sums, kw_sum, kb_sum, cvpad, dcpad, kspad, dk_slab, dlog
):
    @pl.when(pl.program_id(0) == 0)
    def _():
        sums[...] = jnp.zeros_like(sums)
        kw_sum[...] = jnp.zeros_like(kw_sum)
        kb_sum[...] = jnp.zeros_like(kb_sum)

    joined = jnp.where(bucket[pl.program_id(0)] == 0, 1.0, 0.0).astype(F32)
    dc = dconv[...].astype(F32)
    fill_padded(cvpad, cv[...].astype(F32), joined)
    fill_padded(dcpad, dc, joined)
    fill_padded(kspad, ks[...].astype(F32), joined)
    spread = head_spread()
    total = None
    for j in range(KERNEL):
        at = HALO + j - EDGE
        moved = cvpad[:, at : at + SHORT, :].reshape(BLOCK, WIDTH)
        part = mm_nt((dc * moved).astype(BF), spread)
        dk_slab[:, j * SLAB : (j + 1) * SLAB] = part
        part = part * ks[:, j * SLAB : (j + 1) * SLAB].astype(F32)
        total = part if total is None else total + part
    for j in range(KERNEL):
        lanes = slice(j * SLAB, (j + 1) * SLAB)
        grad = ks[:, lanes].astype(F32) * (dk_slab[:, lanes] - total)
        kb_sum[0:1, lanes] += col_sum(grad)
        dlog[:, lanes] = grad.astype(BF)
    acc = None
    for j in range(KERNEL):
        at = HALO - (j - EDGE)
        weight = mm(
            kspad[:, at : at + SHORT, j * SLAB : (j + 1) * SLAB].reshape(BLOCK, SLAB).astype(BF),
            spread,
        )
        moved = dcpad[:, at : at + SHORT, :].reshape(BLOCK, WIDTH)
        acc = weight * moved if acc is None else acc + weight * moved
    dqc[:, WIDTH:] = acc.astype(BF)
    sums[1:2, :] += col_sum(acc)
    select = slab_select(HEADS * KERNEL).astype(BF)
    compact = mm_nt(dlog[...], select).astype(BF)
    qf = q[...].astype(F32)
    key_conv = kc[...]
    conv_in = (key_conv * qf).astype(BF)
    kw_sum[...] += mm_tn(conv_in, compact)
    d_conv_in = mm_nt(compact, kw[...])
    d_key = d_conv_in * qf
    sums[2:3, :] += col_sum(d_key)
    dkc[...] = d_key.astype(BF)
    dq_all = dq[...] + d_conv_in * key_conv
    sums[0:1, :] += col_sum(dq_all)
    dqc[:, :WIDTH] = dq_all.astype(BF)


def conv_back(bucket, qkvc, d_mixed, kc, ks, dq, kernel_weight):
    count = qkvc.shape[0]
    blocks = count // BLOCK
    taps = HEADS * KERNEL
    return pl.pallas_call(
        conv_back_kernel,
        grid_spec=pltpu.PrefetchScalarGridSpec(
            num_scalar_prefetch=1,
            grid=(blocks,),
            in_specs=[
                rows(BLOCK, WIDTH, 0),
                rows(BLOCK, WIDTH, 3),
                rows(BLOCK, WIDTH, 1),
                rows(BLOCK, WIDTH),
                rows(BLOCK, TAPS),
                rows(BLOCK, WIDTH),
                whole((WIDTH, taps)),
            ],
            out_specs=[
                rows(BLOCK, DIM),
                rows(BLOCK, WIDTH),
                whole((8, WIDTH)),
                whole((WIDTH, taps)),
                whole((8, TAPS)),
            ],
            scratch_shapes=[
                pltpu.VMEM((CHUNKS, PADDED, WIDTH), F32),
                pltpu.VMEM((CHUNKS, PADDED, WIDTH), F32),
                pltpu.VMEM((CHUNKS, PADDED, TAPS), F32),
                pltpu.VMEM((BLOCK, TAPS), F32),
                pltpu.VMEM((BLOCK, TAPS), BF),
            ],
        ),
        out_shape=[
            sds((count, DIM), BF),
            sds((count, WIDTH), BF),
            sds((8, WIDTH), F32),
            sds((WIDTH, taps), F32),
            sds((8, TAPS), F32),
        ],
        compiler_params=params(),
        cost_estimate=pl.CostEstimate(
            flops=30 * count * DIM * WIDTH, bytes_accessed=16 << 20, transcendentals=0
        ),
        name="conv_back",
    )(bucket, qkvc, qkvc, d_mixed, kc, ks, dq, kernel_weight)


def hidden_kernel(bucket, x, dkc, d_att, dqc, dkv, dw, pw, w, hidden, dw_sum, xpad, ddpad):
    @pl.when(pl.program_id(0) == 0)
    def _():
        dw_sum[...] = jnp.zeros_like(dw_sum)

    joined = jnp.where(bucket[pl.program_id(0)] == 0, 1.0, 0.0).astype(F32)
    fill_padded(xpad, x[...].astype(F32), joined)
    fill_padded(ddpad, mm_nt(dkc[...], pw[...]), joined)
    hidden[...] = (
        d_att[...]
        + mm_nt(dkv[...], w[:, WIDTH : 3 * WIDTH])
        + mm_nt(dqc[:, :WIDTH], w[:, :WIDTH])
        + mm_nt(dqc[:, WIDTH:], w[:, 3 * WIDTH :])
    )
    for s in range(CHUNKS):
        for lo in range(0, DIM, 256):
            hi = lo + 256
            here = tap(ddpad, s, 0, lo, hi)
            acc = None
            for j in range(KERNEL):
                dw_sum[j : j + 1, lo:hi] += col_sum(tap(xpad, s, j - EDGE, lo, hi) * here)
                part = tap(ddpad, s, EDGE - j, lo, hi) * dw[j : j + 1, lo:hi]
                acc = part if acc is None else acc + part
            hidden[s * SHORT : (s + 1) * SHORT, lo:hi] += acc


def hidden_back(bucket, x, dkc, d_att, dqc, dkv, depth_weight, point_weight, in_weight):
    count = x.shape[0]
    blocks = count // BLOCK
    return pl.pallas_call(
        hidden_kernel,
        grid_spec=pltpu.PrefetchScalarGridSpec(
            num_scalar_prefetch=1,
            grid=(blocks,),
            in_specs=[
                rows(BLOCK, DIM),
                rows(BLOCK, WIDTH),
                rows(BLOCK, DIM),
                rows(BLOCK, DIM),
                rows(BLOCK, DIM),
                whole((KERNEL, DIM)),
                whole((DIM, WIDTH)),
                whole((DIM, 4 * WIDTH)),
            ],
            out_specs=[rows(BLOCK, DIM), whole((16, DIM))],
            scratch_shapes=[
                pltpu.VMEM((CHUNKS, PADDED, DIM), F32),
                pltpu.VMEM((CHUNKS, PADDED, DIM), F32),
            ],
        ),
        out_shape=[sds((count, DIM), F32), sds((16, DIM), F32)],
        compiler_params=params(),
        cost_estimate=pl.CostEstimate(
            flops=10 * count * DIM * WIDTH, bytes_accessed=20 << 20, transcendentals=0
        ),
        name="hidden_back",
    )(bucket, x, dkc, d_att, dqc, dkv, depth_weight, point_weight, in_weight)


def digit_groups(size):
    groups, shift = [], 0
    while (1 << shift) < size:
        bits = 2 if (4 << shift) <= size else 1
        groups.append((shift, 1 << bits))
        shift += bits
    return groups


def partner(value, size, distance):
    return lax.ppermute(value, "wide", [(i, i ^ distance) for i in range(size)])


def swap_core(value):
    return lax.ppermute(value, "grp", [(0, 1), (1, 0)])


def gather_relative(block, size):
    buf = block[None]
    for shift, count in reversed(digit_groups(size)):
        parts = [buf] + [partner(buf, size, k << shift) for k in range(1, count)]
        buf = jnp.concatenate(parts, axis=0)
    return buf


def scatter_relative(blocks, size):
    buf = blocks
    groups = digit_groups(size)
    for n, (shift, count) in enumerate(groups):
        parts = buf.reshape((count, buf.shape[0] // count) + buf.shape[1:])
        total = parts[0].astype(F32)
        for k in range(1, count):
            total = total + partner(parts[k], size, k << shift).astype(F32)
        buf = total if n == len(groups) - 1 else total.astype(BF)
    return buf[0]


def take(array, index):
    return lax.dynamic_index_in_dim(array, index, 0, keepdims=False)


def sum_everywhere(rows_in, size):
    core = lax.axis_index("grp")
    place = lax.axis_index("wide")
    groups = digit_groups(size)
    n, width = rows_in.shape
    unit = n // (2 * size)
    halves = rows_in.reshape(2, n // 2, width)
    buf = take(halves, core).astype(F32) + swap_core(take(halves, 1 - core)).astype(F32)
    buf = buf.astype(BF)
    for shift, count in groups:
        digit = (place >> shift) & (count - 1)
        parts = buf.reshape(count, buf.shape[0] // count, width)
        total = take(parts, digit).astype(F32)
        for k in range(1, count):
            total = total + partner(take(parts, digit ^ k), size, k << shift).astype(F32)
        buf = total.astype(BF)
    for shift, count in reversed(groups):
        digit = (place >> shift) & (count - 1)
        out = jnp.zeros((count,) + buf.shape, BF)
        out = lax.dynamic_update_index_in_dim(out, buf, digit, 0)
        for k in range(1, count):
            out = lax.dynamic_update_index_in_dim(out, partner(buf, size, k << shift), digit ^ k, 0)
        buf = out.reshape(count * buf.shape[0], width)
    out = jnp.zeros((2,) + buf.shape, BF)
    out = lax.dynamic_update_index_in_dim(out, buf, core, 0)
    out = lax.dynamic_update_index_in_dim(out, swap_core(buf), 1 - core, 0)
    return out.reshape(n, width)


def pad_rows(array, multiple):
    return jnp.pad(array, ((0, -array.shape[0] % multiple), (0, 0)))


def wide_rows(array):
    flat = array.reshape(-1)
    return jnp.pad(flat, (0, -flat.shape[0] % DIM)).reshape(-1, DIM)


def body(
    size,
    hidden_in,
    valid_mask,
    bucket,
    in_weight,
    in_bias,
    depth_weight,
    point_weight,
    kernel_weight,
    kernel_bias,
    out_weight,
    out_bias,
    norm_gain,
    norm_bias,
    ffn_in,
    ffn_in_bias,
    ffn_out,
    ffn_out_bias,
    out_grad,
):
    count = hidden_in.shape[0]
    blocks = count // BLOCK
    shard = ffn_in.shape[1]
    hidden = shard * size
    core = lax.axis_index("grp")
    group = jnp.reshape(core, (1,)).astype(jnp.int32)
    valid = valid_mask.reshape(blocks, 1, BLOCK)

    bias_rows = jnp.pad(ffn_in_bias, ((0, 15), (0, WIDTH - shard)))
    pack = jnp.concatenate([ffn_in[0], ffn_out[0], bias_rows], axis=0)
    own = gather_relative(pack, size)
    other = swap_core(own)

    def unpack(blocks_of):
        return (
            blocks_of[:, :shard].reshape(hidden, WIDTH),
            blocks_of[:, shard : 2 * shard].reshape(hidden, WIDTH),
            blocks_of[:, 2 * shard, :shard].reshape(1, hidden).astype(F32),
        )

    w1a, w2a, b1a = unpack(own)
    w1b, w2b, b1b = unpack(other)
    out_bias_pair = jnp.concatenate([ffn_out_bias, swap_core(ffn_out_bias)], axis=1)
    out_bias_pair = jnp.where(core == 0, out_bias_pair, jnp.roll(out_bias_pair, WIDTH, axis=1))

    qkvc, dep, kc, ks, conv_out = project(
        bucket, hidden_in, in_weight, in_bias, depth_weight, point_weight, kernel_weight,
        kernel_bias[None],
    )
    mixed, logs = attend(bucket, valid, qkvc, conv_out)
    (
        output, d_att, d_mixed, xin, dback, act_a, act_b, dpre_a, dpre_b, sums, sums_a, sums_b,
    ) = middle(
        group, hidden_in, mixed, out_grad, out_weight, out_bias[None], norm_gain, norm_bias,
        out_bias_pair, w1a, w2a, w1b, w2b, b1a, b1b,
    )

    def grad_blocks(first, second, bias_sum):
        bias_part = jnp.pad(bias_sum.reshape(size, 1, shard), ((0, 0), (0, 15), (0, WIDTH - shard)))
        return jnp.concatenate(
            [
                first.reshape(size, shard, WIDTH),
                second.reshape(size, shard, WIDTH),
                bias_part.astype(BF),
            ],
            axis=1,
        )

    first_b, second_b = ffn_grad(1 - group, dpre_b, act_b, xin, dback)
    from_core = swap_core(grad_blocks(first_b, second_b, sums_b))
    first_a, second_a = ffn_grad(group, dpre_a, act_a, xin, dback)
    pair = grad_blocks(first_a, second_a, sums_a).astype(F32) + from_core.astype(F32)
    ffn_grads = scatter_relative(pair.astype(BF), size)

    out_weight_part = tn_matmul(mixed, d_att, "out_weight_grad")
    dq, dkv, sums_v = attend_back(bucket, valid, qkvc, d_mixed, logs)
    kv_part = tn_matmul(hidden_in, dkv, "key_value_grad")
    early = sum_everywhere(
        pad_rows(jnp.concatenate([out_weight_part, kv_part], axis=0), 16 * size), size
    )
    dqc, dkc, sums_c, kw_part, kb_part = conv_back(
        bucket, qkvc, d_mixed, kc, ks, dq, kernel_weight
    )
    qc_part = tn_matmul(hidden_in, dqc, "query_conv_grad")
    point_part = tn_matmul(dep, dkc, "point_grad")
    hidden_grad, dw_sum = hidden_back(
        bucket, hidden_in, dkc, d_att, dqc, dkv, depth_weight, point_weight, in_weight
    )
    kb_sum = kb_part[0].reshape(KERNEL, SLAB)[:, :HEADS].T.reshape(-1)
    small = [
        sums[:6],
        wide_rows(jnp.concatenate([sums_c[0:1], sums_v[0:1], sums_c[1:3]], axis=0)),
        dw_sum[:KERNEL],
        wide_rows(kw_part),
        wide_rows(kb_sum),
    ]
    late_parts = [qc_part, point_part.reshape(-1, DIM)] + [v.astype(BF) for v in small]
    late = sum_everywhere(pad_rows(jnp.concatenate(late_parts, axis=0), 16 * size), size)

    out_weight_grad = early[:DIM].astype(F32)
    kv = early[DIM : 2 * DIM].astype(F32)
    late = late.astype(F32)
    qc = late[:DIM]
    in_weight_grad = jnp.concatenate([qc[:, :WIDTH], kv, qc[:, WIDTH:]], axis=1)
    at = DIM
    point_weight_grad = late[at : at + WIDTH].reshape(DIM, WIDTH)
    at += WIDTH
    norms = late[at : at + 6]
    at += 6
    in_bias_grad = late[at : at + 2].reshape(4, WIDTH)
    at += 2
    depth_weight_grad = late[at : at + KERNEL]
    at += KERNEL
    taps = HEADS * KERNEL
    kw_rows = WIDTH * taps // DIM
    kernel_weight_grad = late[at : at + kw_rows].reshape(WIDTH, taps)
    at += kw_rows
    kernel_bias_grad = late[at, :taps]
    ffn_out_bias_grad = lax.dynamic_slice(norms, (5, core * WIDTH), (1, WIDTH))
    return (
        output,
        hidden_grad,
        in_weight_grad,
        in_bias_grad,
        depth_weight_grad,
        point_weight_grad,
        kernel_weight_grad,
        kernel_bias_grad,
        out_weight_grad,
        norms[4],
        norms[0:2],
        norms[2:4],
        ffn_grads[None, :shard],
        ffn_grads[None, 2 * shard, :shard],
        ffn_grads[None, shard : 2 * shard],
        ffn_out_bias_grad,
    )


def solution(mesh):
    both = ("grp", "wide")
    return jax.shard_map(
        functools.partial(body, mesh.shape["wide"]),
        mesh=mesh,
        in_specs=(
            P(both, None),
            P(both),
            P(both),
            P(),
            P(),
            P(),
            P(),
            P(),
            P(),
            P(),
            P(),
            P(),
            P(),
            P("grp", "wide", None),
            P("grp", "wide"),
            P("grp", "wide", None),
            P("grp", None),
            P(both, None),
        ),
        out_specs=(
            P(both, None),
            P(both, None),
            P(),
            P(),
            P(),
            P(),
            P(),
            P(),
            P(),
            P(),
            P(),
            P(),
            P("grp", "wide", None),
            P("grp", "wide"),
            P("grp", "wide", None),
            P("grp", None),
        ),
        check_vma=False,
    )
```

```python
import functools
import jax
import jax.numpy as jnp
from jax import lax
from jax.experimental import pallas as pl
from jax.experimental.pallas import tpu as pltpu
from jax.sharding import PartitionSpec as P

HEADS = 6
HEAD = 64
KERNEL = 9
EDGE = 4
BLOCK = 512
SHORT = 128
CHUNKS = BLOCK // SHORT
WIDTH = HEADS * HEAD
DIM = 2 * WIDTH
SLAB = 128
TAPS = KERNEL * SLAB
HALO = 8
PADDED = SHORT + 2 * HALO
EPSILON = 1e-12
BF = jnp.bfloat16
F32 = jnp.float32
VMEM_LIMIT = 60 * 1024 * 1024


def mm(a, b):
    return lax.dot_general(a, b, (((1,), (0,)), ((), ())), preferred_element_type=F32)


def mm_nt(a, b):
    return lax.dot_general(a, b, (((1,), (1,)), ((), ())), preferred_element_type=F32)


def mm_tn(a, b):
    return lax.dot_general(a, b, (((0,), (0,)), ((), ())), preferred_element_type=F32)


def col_sum(v):
    return jnp.sum(v, axis=0, keepdims=True)


def params(limit=VMEM_LIMIT):
    return pltpu.CompilerParams(vmem_limit_bytes=limit)


def whole(shape):
    return pl.BlockSpec(shape, lambda *_: (0,) * len(shape))


def rows(tile, width, lane=0):
    return pl.BlockSpec((tile, width), lambda i, *_: (i, lane))


def cost(micros):
    return pl.CostEstimate(flops=int(micros * 1e7), bytes_accessed=int(micros * 3e4), transcendentals=0)


def sds(shape, dtype):
    return jax.ShapeDtypeStruct(shape, dtype)


def fill_padded(pad_ref, values, joined):
    n = values.shape[1]
    zero = jnp.zeros((HALO, n), F32)
    for s in range(CHUNKS):
        lo, hi = s * SHORT, (s + 1) * SHORT
        pad_ref[s, HALO : HALO + SHORT, :] = values[lo:hi]
        pad_ref[s, 0:HALO, :] = values[lo - HALO : lo] * joined if s else zero
        pad_ref[s, HALO + SHORT :, :] = (
            values[hi : hi + HALO] * joined if s < CHUNKS - 1 else zero
        )


def tap(pad_ref, s, offset, lo, hi):
    return pad_ref[s, HALO + offset : HALO + offset + SHORT, lo:hi]


def slab_select(rows_of):
    source = lax.broadcasted_iota(jnp.int32, (rows_of, TAPS), 0)
    target = lax.broadcasted_iota(jnp.int32, (rows_of, TAPS), 1)
    head = target % SLAB
    hit = (head < HEADS) & (source == head * KERNEL + target // SLAB)
    return hit.astype(F32)


def head_spread():
    source = lax.broadcasted_iota(jnp.int32, (SLAB, WIDTH), 0)
    target = lax.broadcasted_iota(jnp.int32, (SLAB, WIDTH), 1)
    return (source == target // HEAD).astype(BF)


def norm_stats(v):
    mean = jnp.mean(v, axis=-1, keepdims=True)
    centred = v - mean
    var = jnp.mean(centred * centred, axis=-1, keepdims=True)
    inv = lax.rsqrt(var + EPSILON)
    return centred * inv, inv


def norm_back(d_scaled, hat, inv):
    first = jnp.mean(d_scaled, axis=-1, keepdims=True)
    second = jnp.mean(d_scaled * hat, axis=-1, keepdims=True)
    return inv * (d_scaled - first - hat * second)


def normal_cdf(v):
    density = jnp.exp2(v * v * -0.7213475204444817 - 1.3257480647361595)
    den = 1.0 + 0.23164189 * jnp.abs(v)
    t = pl.reciprocal(den, approx=True)
    t = t * (2.0 - den * t)
    poly = 1.3302745
    poly = poly * t - 1.8212560
    poly = poly * t + 1.7814779
    poly = poly * t - 0.35656378
    poly = poly * t + 0.31938153
    tail = poly * t * density
    return jnp.where(v < 0.0, tail, 1.0 - tail), density


def project_kernel(
    bucket, x, w, bias, dw, pw, kw, kb, qkvc, dep, kc, ks, co, xpad, cvpad
):
    joined = jnp.where(bucket[pl.program_id(0)] == 0, 1.0, 0.0).astype(F32)
    xb = x[...]
    proj = mm(xb, w[...])
    q = (proj[:, :WIDTH] + bias[0:1, :]).astype(BF)
    qkvc[:, 0:WIDTH] = q
    qkvc[:, WIDTH : 2 * WIDTH] = proj[:, WIDTH : 2 * WIDTH].astype(BF)
    qkvc[:, 2 * WIDTH : 3 * WIDTH] = (
        proj[:, 2 * WIDTH : 3 * WIDTH] + bias[1:2, :]
    ).astype(BF)
    cv = (proj[:, 3 * WIDTH :] + bias[2:3, :]).astype(BF)
    qkvc[:, 3 * WIDTH :] = cv
    fill_padded(xpad, xb.astype(F32), joined)
    fill_padded(cvpad, cv.astype(F32), joined)
    for s in range(CHUNKS):
        for lo in range(0, DIM, 256):
            acc = tap(xpad, s, -EDGE, lo, lo + 256) * dw[0:1, lo : lo + 256]
            for j in range(1, KERNEL):
                acc += tap(xpad, s, j - EDGE, lo, lo + 256) * dw[j : j + 1, lo : lo + 256]
            dep[s * SHORT : (s + 1) * SHORT, lo : lo + 256] = acc.astype(BF)
    key_conv = mm(dep[...], pw[...]) + bias[3:4, :]
    kc[...] = key_conv
    conv_in = (key_conv * q.astype(F32)).astype(BF)
    select = slab_select(HEADS * KERNEL)
    kw_slab = mm(kw[...], select.astype(BF)).astype(BF)
    kb_slab = jnp.dot(
        jnp.broadcast_to(kb[...], (8, HEADS * KERNEL)),
        select,
        precision=lax.Precision.HIGHEST,
        preferred_element_type=F32,
    )[0:1]
    logits = mm(conv_in, kw_slab) + kb_slab
    slabs = [logits[:, j * SLAB : (j + 1) * SLAB] for j in range(KERNEL)]
    top = functools.reduce(jnp.maximum, slabs)
    slabs = [jnp.exp(v - top) for v in slabs]
    inv = 1.0 / functools.reduce(jnp.add, slabs)
    for j in range(KERNEL):
        ks[:, j * SLAB : (j + 1) * SLAB] = (slabs[j] * inv).astype(BF)
    spread = head_spread()
    acc = None
    for j in range(KERNEL):
        weight = mm(ks[:, j * SLAB : (j + 1) * SLAB], spread)
        moved = cvpad[:, HALO + j - EDGE : HALO + j - EDGE + SHORT, :].reshape(BLOCK, WIDTH)
        acc = weight * moved if acc is None else acc + weight * moved
    co[...] = acc.astype(BF)


def project(bucket, x, in_weight, in_bias, depth_weight, point_weight, kernel_weight, kernel_bias):
    count = x.shape[0]
    blocks = count // BLOCK
    taps = HEADS * KERNEL
    return pl.pallas_call(
        project_kernel,
        grid_spec=pltpu.PrefetchScalarGridSpec(
            num_scalar_prefetch=1,
            grid=(blocks,),
            in_specs=[
                rows(BLOCK, DIM),
                whole((DIM, 4 * WIDTH)),
                whole((4, WIDTH)),
                whole((KERNEL, DIM)),
                whole((DIM, WIDTH)),
                whole((WIDTH, taps)),
                whole((1, taps)),
            ],
            out_specs=[
                rows(BLOCK, 4 * WIDTH),
                rows(BLOCK, DIM),
                rows(BLOCK, WIDTH),
                rows(BLOCK, TAPS),
                rows(BLOCK, WIDTH),
            ],
            scratch_shapes=[
                pltpu.VMEM((CHUNKS, PADDED, DIM), F32),
                pltpu.VMEM((CHUNKS, PADDED, WIDTH), F32),
            ],
        ),
        out_shape=[
            sds((count, 4 * WIDTH), BF),
            sds((count, DIM), BF),
            sds((count, WIDTH), F32),
            sds((count, TAPS), BF),
            sds((count, WIDTH), BF),
        ],
        compiler_params=params(),
        cost_estimate=cost(17),
        name="project",
    )(bucket, x, in_weight, in_bias, depth_weight, point_weight, kernel_weight, kernel_bias)


def mask_bias(is_short, valid_row):
    column = jnp.transpose(jnp.broadcast_to(valid_row.astype(F32), (SLAB, BLOCK)))
    column = jnp.concatenate([column] * (BLOCK // SLAB), axis=1)
    key_slot = (lax.broadcasted_iota(jnp.int32, (BLOCK, BLOCK), 0) // SHORT) * is_short
    query_slot = (lax.broadcasted_iota(jnp.int32, (BLOCK, BLOCK), 1) // SHORT) * is_short
    return jnp.where((key_slot == query_slot) & (column > 0.0), 0.0, -1e30)


def half_mask(v, h):
    lane = lax.broadcasted_iota(jnp.int32, v.shape, 1)
    keep = lane < HEAD if h % 2 == 0 else lane >= HEAD
    return jnp.where(keep, v, jnp.zeros_like(v))


def attend_kernel(
    bucket, valid, q, k, v, co, x, w_out, b_out, gain, shift,
    mixed, logs, hat, inv, xin, bias, context,
):
    bias[...] = mask_bias(bucket[pl.program_id(0)], valid[...].reshape(1, BLOCK))
    vt = jnp.transpose(v[...])
    logs[...] = jnp.zeros_like(logs)
    for h in range(HEADS):
        lo = (h // 2) * SLAB
        qm = half_mask(q[:, lo : lo + SLAB], h) * jnp.asarray(HEAD**-0.5, BF)
        scores = mm_nt(k[:, lo : lo + SLAB], qm) + bias[...]
        top = jnp.max(scores, axis=0, keepdims=True)
        e = jnp.exp(scores - top)
        total = jnp.sum(e, axis=0, keepdims=True)
        part = mm(vt[h * HEAD : (h + 1) * HEAD], e.astype(BF))
        context[h * HEAD : (h + 1) * HEAD, :] = part / total
        logs[0, h : h + 1, :] = top + jnp.log(total)
    mixed[:, :WIDTH] = jnp.transpose(context[...]).astype(BF)
    mixed[:, WIDTH:] = co[...]
    att = mm(mixed[...], w_out[...]) + b_out[...] + x[...].astype(F32)
    scaled, stat = norm_stats(att)
    hat[...] = scaled
    inv[...] = jnp.broadcast_to(stat, inv.shape)
    xin[...] = (scaled * gain[0:1, :] + shift[0:1, :]).astype(BF)


def attend(bucket, valid, qkvc, conv_out, x, out_weight, out_bias, gain, shift):
    count = qkvc.shape[0]
    blocks = count // BLOCK
    return pl.pallas_call(
        attend_kernel,
        grid_spec=pltpu.PrefetchScalarGridSpec(
            num_scalar_prefetch=1,
            grid=(blocks,),
            in_specs=[
                pl.BlockSpec((1, 1, BLOCK), lambda i, *_: (i, 0, 0)),
                rows(BLOCK, WIDTH, 0),
                rows(BLOCK, WIDTH, 1),
                rows(BLOCK, WIDTH, 2),
                rows(BLOCK, WIDTH),
                rows(BLOCK, DIM),
                whole((DIM, DIM)),
                whole((1, DIM)),
                whole((2, DIM)),
                whole((2, DIM)),
            ],
            out_specs=[
                rows(BLOCK, DIM),
                pl.BlockSpec((1, 8, BLOCK), lambda i, *_: (i, 0, 0)),
                rows(BLOCK, DIM),
                rows(BLOCK, SLAB),
                rows(BLOCK, DIM),
            ],
            scratch_shapes=[
                pltpu.VMEM((BLOCK, BLOCK), F32),
                pltpu.VMEM((WIDTH, BLOCK), F32),
            ],
        ),
        out_shape=[
            sds((count, DIM), BF),
            sds((blocks, 8, BLOCK), F32),
            sds((count, DIM), F32),
            sds((count, SLAB), F32),
            sds((count, DIM), BF),
        ],
        compiler_params=params(),
        cost_estimate=cost(14),
        name="attend",
    )(bucket, valid, qkvc, qkvc, qkvc, conv_out, x, out_weight, out_bias, gain, shift)


PARTS = 4


def unpack_weights(packs, w1, w2, bias_blocks, sems, g, shard, per):
    copies = []
    for k, pack in enumerate(packs):
        at = pl.ds(k * per, per)
        for n, (lo, size, dst) in enumerate(
            ((0, shard, w1), (shard, shard, w2), (2 * shard, 16, bias_blocks))
        ):
            copies.append(
                pltpu.make_async_copy(
                    pack.at[:, pl.ds(lo, size), :], dst.at[g, at], sems.at[g, k, n]
                )
            )
    return copies


def middle_kernel(
    group, *refs, shard, size
):
    hidden = shard * size
    packs, refs = refs[: 2 * PARTS], refs[2 * PARTS :]
    (
        hat1, inv1, xin, mixed, grad, w_out, gain, shift, b2,
        output, d_att, d_mixed, dback, act_a, act_b, dpre_a, dpre_b, sums, sums_a, sums_b, out_grad,
        ffn_out, d_summed, slope, datt_low, bias_sum, out_acc, w1s, w2s, blocks_s, b1s, sems,
    ) = refs
    own = pl.multiple_of(group[0] * WIDTH, SLAB)
    other = pl.multiple_of((1 - group[0]) * WIDTH, SLAB)
    part = 512
    step = pl.program_id(0)
    copies = [
        unpack_weights(
            packs[g * PARTS : (g + 1) * PARTS], w1s, w2s, blocks_s, sems, g, shard, size // PARTS
        )
        for g in range(2)
    ]

    @pl.when(step == 0)
    def _():
        for c in copies[0] + copies[1]:
            c.start()

    @pl.when(step == 0)
    def _():
        sums[...] = jnp.zeros_like(sums)
        bias_sum[...] = jnp.zeros_like(bias_sum)
        out_acc[...] = jnp.zeros_like(out_acc)

    def weights(g):
        return (
            w1s.at[g].reshape(hidden, WIDTH),
            w2s.at[g].reshape(hidden, WIDTH),
            b1s.at[g],
        )

    for g, base, act, at in ((0, own, act_a, 0), (1, other, act_b, hidden)):

        @pl.when(step == 0)
        def _():
            for c in copies[g]:
                c.wait()
            for r in range(size):
                row = blocks_s[g, r].astype(F32)[0:1, :shard]
                b1s[g, 0:1, r * shard : (r + 1) * shard] = row

        w1, w2, b1 = weights(g)
        xg = xin[:, pl.ds(base, WIDTH)]
        for lo in range(0, hidden, part):
            pre = mm_nt(xg, w1[lo : lo + part, :]) + b1[0:1, lo : lo + part]
            cdf, bell = normal_cdf(pre)
            act[:, lo : lo + part] = (pre * cdf).astype(BF)
            slope[:, at + lo : at + lo + part] = (cdf + pre * bell).astype(BF)
        ffn_out[:, pl.ds(base, WIDTH)] = mm(act[...], w2[...])
    result = (ffn_out[...] + b2[...]).astype(BF).astype(F32)
    hat2, inv2 = norm_stats(result + (hat1[...] * gain[0:1, :] + shift[0:1, :]))
    output[...] = (hat2 * gain[1:2, :] + shift[1:2, :]).astype(BF)
    dy = grad[...].astype(F32)
    sums[1:2, :] += col_sum(dy * hat2)
    sums[3:4, :] += col_sum(dy)
    ds = norm_back(dy * gain[1:2, :], hat2, inv2)
    d_summed[...] = ds
    low = ds.astype(BF)
    dback[...] = low
    sums[5:6, :] += col_sum(low.astype(F32))
    for g, base, dpre, at in ((0, own, dpre_a, 0), (1, other, dpre_b, hidden)):
        w1, w2, b1 = weights(g)
        dg = dback[:, pl.ds(base, WIDTH)]
        for lo in range(0, hidden, part):
            dp = mm_nt(dg, w2[lo : lo + part, :]) * slope[:, at + lo : at + lo + part].astype(F32)
            bias_sum[g : g + 1, lo : lo + part] += col_sum(dp)
            dpre[:, lo : lo + part] = dp.astype(BF)
        ffn_out[:, pl.ds(base, WIDTH)] = mm(dpre[...], w1[...])
    dn = d_summed[...] + ffn_out[...].astype(BF).astype(F32)
    hat = hat1[...]
    sums[0:1, :] += col_sum(dn * hat)
    sums[2:3, :] += col_sum(dn)
    da = norm_back(dn * gain[0:1, :], hat, inv1[:, 0:1])
    d_att[...] = da
    sums[4:5, :] += col_sum(da)
    datt_low[...] = da.astype(BF)
    d_mixed[...] = mm_nt(datt_low[...], w_out[...]).astype(BF)
    out_acc[...] += mm_tn(mixed[...], datt_low[...])

    @pl.when(step == pl.num_programs(0) - 1)
    def _():
        out_grad[...] = out_acc[...].astype(BF)
        for g, dst in ((0, sums_a), (1, sums_b)):
            dst[...] = jnp.zeros_like(dst)
            for r in range(size):
                dst[r, 0:1, 0:shard] = bias_sum[g : g + 1, r * shard : (r + 1) * shard]


def middle(group, packs, shard, size, hat, inv, xin, mixed, grad, out_weight, gain, shift, b2):
    count = xin.shape[0]
    hidden = shard * size
    tile = BLOCK
    sum_shape = (size, 8, WIDTH)
    return pl.pallas_call(
        functools.partial(middle_kernel, shard=shard, size=size),
        grid_spec=pltpu.PrefetchScalarGridSpec(
            num_scalar_prefetch=1,
            grid=(count // tile,),
            in_specs=[pl.BlockSpec(memory_space=pl.ANY)] * (2 * PARTS)
            + [
                rows(tile, DIM),
                rows(tile, SLAB),
                rows(tile, DIM),
                rows(tile, DIM),
                rows(tile, DIM),
                whole((DIM, DIM)),
                whole((2, DIM)),
                whole((2, DIM)),
                whole((1, DIM)),
            ],
            out_specs=[
                rows(tile, DIM),
                rows(tile, DIM),
                rows(tile, DIM),
                rows(tile, DIM),
                rows(tile, hidden),
                rows(tile, hidden),
                rows(tile, hidden),
                rows(tile, hidden),
                whole((8, DIM)),
                whole(sum_shape),
                whole(sum_shape),
                whole((DIM, DIM)),
            ],
            scratch_shapes=[
                pltpu.VMEM((tile, DIM), F32),
                pltpu.VMEM((tile, DIM), F32),
                pltpu.VMEM((tile, 2 * hidden), BF),
                pltpu.VMEM((tile, DIM), BF),
                pltpu.VMEM((8, hidden), F32),
                pltpu.VMEM((DIM, DIM), F32),
                pltpu.VMEM((2, size, shard, WIDTH), BF),
                pltpu.VMEM((2, size, shard, WIDTH), BF),
                pltpu.VMEM((2, size, 16, WIDTH), BF),
                pltpu.VMEM((2, 8, hidden), F32),
                pltpu.SemaphoreType.DMA((2, PARTS, 3)),
            ],
        ),
        out_shape=[
            sds((count, DIM), BF),
            sds((count, DIM), F32),
            sds((count, DIM), BF),
            sds((count, DIM), BF),
            sds((count, hidden), BF),
            sds((count, hidden), BF),
            sds((count, hidden), BF),
            sds((count, hidden), BF),
            sds((8, DIM), F32),
            sds(sum_shape, F32),
            sds(sum_shape, F32),
            sds((DIM, DIM), BF),
        ],
        compiler_params=params(),
        cost_estimate=cost(38),
        name="middle",
    )(group, *packs, hat, inv, xin, mixed, grad, out_weight, gain, shift, b2)


def ffn_grad_kernel(group, dpre, act, xin, dback, sums, out, *, shard):
    first = mm_tn(dpre[...], xin[...]).astype(BF)
    second = mm_tn(act[...], dback[...]).astype(BF)
    for z in range(out.shape[0]):
        out[z, 0:shard, :] = first[z * shard : (z + 1) * shard]
        out[z, shard : 2 * shard, :] = second[z * shard : (z + 1) * shard]
        row = jnp.concatenate([sums[z], jnp.zeros((8, WIDTH), F32)], axis=0)
        out[z, 2 * shard :, :] = row.astype(BF)


def ffn_grad(group, dpre, act, xin, dback, sums, shard, size):
    count, hidden = dpre.shape
    tile = hidden // PARTS
    per = size // PARTS
    lanes = pl.BlockSpec((count, tile), lambda i, g: (0, i))
    side = pl.BlockSpec((count, WIDTH), lambda i, g: (0, g[0]))
    return pl.pallas_call(
        functools.partial(ffn_grad_kernel, shard=shard),
        grid_spec=pltpu.PrefetchScalarGridSpec(
            num_scalar_prefetch=1,
            grid=(PARTS,),
            in_specs=[
                lanes, lanes, side, side, pl.BlockSpec((per, 8, WIDTH), lambda i, g: (i, 0, 0)),
            ],
            out_specs=pl.BlockSpec((per, 2 * shard + 16, WIDTH), lambda i, g: (i, 0, 0)),
        ),
        out_shape=sds((size, 2 * shard + 16, WIDTH), BF),
        compiler_params=params(),
        cost_estimate=cost(7),
        name="ffn_grad",
    )(group, dpre, act, xin, dback, sums)


def repack(packs, size, shard):
    old = (packs.shape[1] - 16) // 2
    first = packs[:, :old].reshape(size, shard, WIDTH)
    second = packs[:, old : 2 * old].reshape(size, shard, WIDTH)
    bias = packs[:, 2 * old, :old].reshape(size, 1, shard)
    bias = jnp.pad(bias, ((0, 0), (0, 15), (0, WIDTH - shard)))
    return jnp.concatenate([first, second, bias], axis=1)


def attend_back_kernel(
    info, valid, q, k, v, dctx, logs, x, out_part, dq, dkv, sums, keep, send, bias, dqt, acc
):
    step = pl.program_id(0)

    @pl.when(step == 0)
    def _():
        sums[...] = jnp.zeros_like(sums)
        acc[...] = jnp.zeros_like(acc)

    bias[...] = mask_bias(info[1 + step], valid[...].reshape(1, BLOCK))
    scale = jnp.asarray(HEAD**-0.5, BF)
    kt = jnp.transpose(k[...] * scale)
    for pair in range(HEADS // 2):
        lo = pair * SLAB
        kp = k[:, lo : lo + SLAB]
        vp = v[:, lo : lo + SLAB]
        dk = dv = None
        for h in (2 * pair, 2 * pair + 1):
            qm = half_mask(q[:, lo : lo + SLAB], h) * scale
            cm = half_mask(dctx[:, lo : lo + SLAB], h)
            probs = jnp.exp(mm_nt(kp, qm) + bias[...] - logs[0, h : h + 1, :])
            d_probs = mm_nt(vp, cm)
            delta = col_sum(probs * d_probs)
            d_scores = (probs * (d_probs - delta)).astype(BF)
            probs = probs.astype(BF)
            dv = mm(probs, cm) if dv is None else dv + mm(probs, cm)
            dk = mm(d_scores, qm) if dk is None else dk + mm(d_scores, qm)
            dqt[h * HEAD : (h + 1) * HEAD, :] = mm(kt[h * HEAD : (h + 1) * HEAD], d_scores)
        dkv[:, lo : lo + SLAB] = dk.astype(BF)
        dkv[:, WIDTH + lo : WIDTH + lo + SLAB] = dv.astype(BF)
        sums[0:1, lo : lo + SLAB] += col_sum(dv)
    dq[...] = jnp.transpose(dqt[...])
    acc[...] += mm_tn(x[...], dkv[...])

    @pl.when((step == pl.num_programs(0) - 1) & (info[0] == 0))
    def _():
        keep[...] = out_part[...]
        send[...] = acc[...].astype(BF)

    @pl.when((step == pl.num_programs(0) - 1) & (info[0] != 0))
    def _():
        keep[...] = acc[...].astype(BF)
        send[...] = out_part[...]


def attend_back(info, valid, qkvc, d_mixed, logs, x, out_part):
    count = qkvc.shape[0]
    blocks = count // BLOCK
    return pl.pallas_call(
        attend_back_kernel,
        grid_spec=pltpu.PrefetchScalarGridSpec(
            num_scalar_prefetch=1,
            grid=(blocks,),
            in_specs=[
                pl.BlockSpec((1, 1, BLOCK), lambda i, *_: (i, 0, 0)),
                rows(BLOCK, WIDTH, 0),
                rows(BLOCK, WIDTH, 1),
                rows(BLOCK, WIDTH, 2),
                rows(BLOCK, WIDTH, 0),
                pl.BlockSpec((1, 8, BLOCK), lambda i, *_: (i, 0, 0)),
                rows(BLOCK, DIM),
                whole((DIM, DIM)),
            ],
            out_specs=[
                rows(BLOCK, WIDTH),
                rows(BLOCK, DIM),
                whole((8, WIDTH)),
                whole((DIM, DIM)),
                whole((DIM, DIM)),
            ],
            scratch_shapes=[
                pltpu.VMEM((BLOCK, BLOCK), F32),
                pltpu.VMEM((WIDTH, BLOCK), F32),
                pltpu.VMEM((DIM, DIM), F32),
            ],
        ),
        out_shape=[
            sds((count, WIDTH), F32),
            sds((count, DIM), BF),
            sds((8, WIDTH), F32),
            sds((DIM, DIM), BF),
            sds((DIM, DIM), BF),
        ],
        compiler_params=params(),
        cost_estimate=cost(16),
        name="attend_back",
    )(info, valid, qkvc, qkvc, qkvc, d_mixed, logs, x, out_part)


POINT_ROW = DIM
SMALL_ROW = DIM + WIDTH
LATE_ROWS = DIM + WIDTH + 128
NORM_ROW = SMALL_ROW + 64
TAP_ROW = SMALL_ROW + 72


def conv_back_kernel(
    info, q, cv, dconv, kc, ks, dq, x, dep, kw, pw, sums_mid, sums_v, dqc, dkc, keep, send,
    cvpad, dcpad, kspad, xpad, dk_slab, dlog, qc_acc, pt_acc, kw_acc, kb_acc, dw_acc, sums, flat
):
    step = pl.program_id(0)
    taps = HEADS * KERNEL

    @pl.when(step == 0)
    def _():
        for ref in (qc_acc, pt_acc, kw_acc, kb_acc, dw_acc, sums):
            ref[...] = jnp.zeros_like(ref)

    joined = jnp.where(info[1 + step] == 0, 1.0, 0.0).astype(F32)
    dc = dconv[...].astype(F32)
    fill_padded(cvpad, cv[...].astype(F32), joined)
    fill_padded(dcpad, dc, joined)
    fill_padded(kspad, ks[...].astype(F32), joined)
    fill_padded(xpad, x[...].astype(F32), joined)
    spread = head_spread()
    total = None
    for j in range(KERNEL):
        at = HALO + j - EDGE
        moved = cvpad[:, at : at + SHORT, :].reshape(BLOCK, WIDTH)
        part = mm_nt((dc * moved).astype(BF), spread)
        dk_slab[:, j * SLAB : (j + 1) * SLAB] = part
        part = part * ks[:, j * SLAB : (j + 1) * SLAB].astype(F32)
        total = part if total is None else total + part
    for j in range(KERNEL):
        lanes = slice(j * SLAB, (j + 1) * SLAB)
        grad = ks[:, lanes].astype(F32) * (dk_slab[:, lanes] - total)
        kb_acc[0:1, lanes] += col_sum(grad)
        dlog[:, lanes] = grad.astype(BF)
    acc = None
    for j in range(KERNEL):
        at = HALO - (j - EDGE)
        weight = mm(
            kspad[:, at : at + SHORT, j * SLAB : (j + 1) * SLAB].reshape(BLOCK, SLAB).astype(BF),
            spread,
        )
        moved = dcpad[:, at : at + SHORT, :].reshape(BLOCK, WIDTH)
        acc = weight * moved if acc is None else acc + weight * moved
    dqc[:, WIDTH:] = acc.astype(BF)
    sums[1:2, :] += col_sum(acc)
    select = slab_select(taps)
    compact = mm_nt(dlog[...], select.astype(BF)).astype(BF)
    qf = q[...].astype(F32)
    key_conv = kc[...]
    conv_in = (key_conv * qf).astype(BF)
    kw_acc[0:taps, :] += mm_tn(compact, conv_in)
    d_conv_in = mm_nt(compact, kw[...])
    d_key = d_conv_in * qf
    sums[2:3, :] += col_sum(d_key)
    dkc[...] = d_key.astype(BF)
    dq_all = dq[...] + d_conv_in * key_conv
    sums[0:1, :] += col_sum(dq_all)
    dqc[:, :WIDTH] = dq_all.astype(BF)
    qc_acc[...] += mm_tn(x[...], dqc[...])
    pt_acc[...] += mm_tn(dep[...], dkc[...])
    d_depth = mm_nt(dkc[...], pw[...])
    for lo in range(0, DIM, SLAB):
        here = d_depth[:, lo : lo + SLAB]
        for j in range(KERNEL):
            at = HALO + j - EDGE
            moved = xpad[:, at : at + SHORT, lo : lo + SLAB].reshape(BLOCK, SLAB)
            dw_acc[j : j + 1, lo : lo + SLAB] += col_sum(moved * here)

    @pl.when(step == pl.num_programs(0) - 1)
    def _():
        flat[0:DIM, :] = qc_acc[...].astype(BF)
        flat[POINT_ROW:SMALL_ROW, 0:WIDTH] = pt_acc[0:WIDTH, :].astype(BF)
        flat[POINT_ROW:SMALL_ROW, WIDTH:] = pt_acc[WIDTH:, :].astype(BF)
        flat[SMALL_ROW : SMALL_ROW + 64, 0:WIDTH] = kw_acc[...].astype(BF)
        kb = lax.dot_general(
            kb_acc[...],
            select,
            (((1,), (1,)), ((), ())),
            precision=lax.Precision.HIGHEST,
            preferred_element_type=F32,
        )
        blank = jnp.zeros((4, WIDTH), F32)
        rows_of = jnp.concatenate([sums[0:1], sums_v[0:1], sums[1:3], blank], axis=0)
        kb = jnp.concatenate([kb, jnp.zeros((8, WIDTH - taps), F32)], axis=1)
        flat[SMALL_ROW : SMALL_ROW + 16, WIDTH:] = jnp.concatenate([rows_of, kb], axis=0).astype(BF)
        flat[SMALL_ROW + 16 : NORM_ROW, WIDTH:] = jnp.zeros((48, WIDTH), BF)
        flat[NORM_ROW : NORM_ROW + 32, :] = jnp.concatenate(
            [sums_mid[...], dw_acc[...], jnp.zeros((8, DIM), F32)], axis=0
        ).astype(BF)
        flat[NORM_ROW + 32 :, :] = jnp.zeros((32, DIM), BF)
        half = LATE_ROWS // 2
        core = info[0]
        keep[...] = flat[pl.ds(pl.multiple_of(core * half, 16), half), :]
        send[...] = flat[pl.ds(pl.multiple_of((1 - core) * half, 16), half), :]


def conv_back(info, qkvc, d_mixed, kc, ks, dq, x, dep, kernel_weight, point_weight, sums_mid, sums_v):
    count = qkvc.shape[0]
    blocks = count // BLOCK
    taps = HEADS * KERNEL
    half = LATE_ROWS // 2
    return pl.pallas_call(
        conv_back_kernel,
        grid_spec=pltpu.PrefetchScalarGridSpec(
            num_scalar_prefetch=1,
            grid=(blocks,),
            in_specs=[
                rows(BLOCK, WIDTH, 0),
                rows(BLOCK, WIDTH, 3),
                rows(BLOCK, WIDTH, 1),
                rows(BLOCK, WIDTH),
                rows(BLOCK, TAPS),
                rows(BLOCK, WIDTH),
                rows(BLOCK, DIM),
                rows(BLOCK, DIM),
                whole((WIDTH, taps)),
                whole((DIM, WIDTH)),
                whole((8, DIM)),
                whole((8, WIDTH)),
            ],
            out_specs=[
                rows(BLOCK, DIM),
                rows(BLOCK, WIDTH),
                whole((half, DIM)),
                whole((half, DIM)),
            ],
            scratch_shapes=[
                pltpu.VMEM((CHUNKS, PADDED, WIDTH), F32),
                pltpu.VMEM((CHUNKS, PADDED, WIDTH), F32),
                pltpu.VMEM((CHUNKS, PADDED, TAPS), F32),
                pltpu.VMEM((CHUNKS, PADDED, DIM), F32),
                pltpu.VMEM((BLOCK, TAPS), F32),
                pltpu.VMEM((BLOCK, TAPS), BF),
                pltpu.VMEM((DIM, DIM), F32),
                pltpu.VMEM((DIM, WIDTH), F32),
                pltpu.VMEM((64, WIDTH), F32),
                pltpu.VMEM((8, TAPS), F32),
                pltpu.VMEM((16, DIM), F32),
                pltpu.VMEM((8, WIDTH), F32),
                pltpu.VMEM((LATE_ROWS, DIM), BF),
            ],
        ),
        out_shape=[
            sds((count, DIM), BF),
            sds((count, WIDTH), BF),
            sds((half, DIM), BF),
            sds((half, DIM), BF),
        ],
        compiler_params=params(),
        cost_estimate=cost(22),
        name="conv_back",
    )(info, qkvc, qkvc, d_mixed, kc, ks, dq, x, dep, kernel_weight, point_weight, sums_mid, sums_v)


def hidden_kernel(info, dkc, d_att, dqc, dkv, dw, pw, w, hidden, ddpad):
    joined = jnp.where(info[1 + pl.program_id(0)] == 0, 1.0, 0.0).astype(F32)
    fill_padded(ddpad, mm_nt(dkc[...], pw[...]), joined)
    hidden[...] = (
        d_att[...]
        + mm_nt(dkv[...], w[:, WIDTH : 3 * WIDTH])
        + mm_nt(dqc[:, :WIDTH], w[:, :WIDTH])
        + mm_nt(dqc[:, WIDTH:], w[:, 3 * WIDTH :])
    )
    for lo in range(0, DIM, SLAB):
        acc = hidden[:, lo : lo + SLAB]
        for j in range(KERNEL):
            at = HALO + EDGE - j
            moved = ddpad[:, at : at + SHORT, lo : lo + SLAB].reshape(BLOCK, SLAB)
            acc += moved * dw[j : j + 1, lo : lo + SLAB]
        hidden[:, lo : lo + SLAB] = acc


def hidden_back(info, dkc, d_att, dqc, dkv, depth_weight, point_weight, in_weight):
    count = d_att.shape[0]
    return pl.pallas_call(
        hidden_kernel,
        grid_spec=pltpu.PrefetchScalarGridSpec(
            num_scalar_prefetch=1,
            grid=(count // BLOCK,),
            in_specs=[
                rows(BLOCK, WIDTH),
                rows(BLOCK, DIM),
                rows(BLOCK, DIM),
                rows(BLOCK, DIM),
                whole((KERNEL, DIM)),
                whole((DIM, WIDTH)),
                whole((DIM, 4 * WIDTH)),
            ],
            out_specs=rows(BLOCK, DIM),
            scratch_shapes=[pltpu.VMEM((CHUNKS, PADDED, DIM), F32)],
        ),
        out_shape=sds((count, DIM), F32),
        compiler_params=params(),
        cost_estimate=cost(12),
        name="hidden_back",
    )(info, dkc, d_att, dqc, dkv, depth_weight, point_weight, in_weight)


def spread_out_kernel(info, *refs, early_rows, late_rows):
    early_in, late_in, refs = refs[:2], refs[2 : 2 + 2 * PARTS], refs[2 + 2 * PARTS :]
    in_w, in_b, dw, point, kw, kb, out_w, out_b, gain, shift, b2, early, late, sems = refs
    core, digit = info[0], info[1]
    half, late_half = early_rows // 2, late_rows // 2
    quarter = late_half // PARTS
    copies = []
    for c in range(2):
        at = pl.ds(pl.multiple_of((core ^ c) * half, 16), half)
        copies.append(pltpu.make_async_copy(early_in[c], early.at[at, :], sems.at[c, PARTS]))
        for k in range(PARTS):
            row = (core ^ c) * late_half + (digit ^ k) * quarter
            at = pl.ds(pl.multiple_of(row, 16), quarter)
            copies.append(
                pltpu.make_async_copy(late_in[c * PARTS + k], late.at[at, :], sems.at[c, k])
            )
    for c in copies:
        c.start()
    for c in copies:
        c.wait()
    unpack_grads(core, early, late, in_w, in_b, dw, point, kw, kb, out_w, out_b, gain, shift, b2)


def unpack_grads(core, early, late, in_w, in_b, dw, point, kw, kb, out_w, out_b, gain, shift, b2):
    taps = HEADS * KERNEL
    out_w[...] = early[0:DIM, :].astype(F32)
    in_w[:, WIDTH : 3 * WIDTH] = early[DIM:, :].astype(F32)
    in_w[:, 0:WIDTH] = late[0:DIM, 0:WIDTH].astype(F32)
    in_w[:, 3 * WIDTH :] = late[0:DIM, WIDTH:].astype(F32)
    point[0:WIDTH, :] = late[POINT_ROW:SMALL_ROW, 0:WIDTH].astype(F32)
    point[WIDTH:, :] = late[POINT_ROW:SMALL_ROW, WIDTH:].astype(F32)
    kw[...] = jnp.transpose(late[SMALL_ROW : SMALL_ROW + 64, 0:WIDTH].astype(F32))[:, 0:taps]
    mixed = late[SMALL_ROW : SMALL_ROW + 16, WIDTH:].astype(F32)
    in_b[...] = mixed[0:4]
    kb[...] = mixed[8:9, 0:taps]
    norms = late[NORM_ROW : NORM_ROW + 32, :].astype(F32)
    gain[...] = norms[0:2]
    shift[...] = norms[2:4]
    out_b[...] = norms[4:5]
    b2[...] = jnp.where(core == 0, norms[5:6, 0:WIDTH], norms[5:6, WIDTH:])
    dw[...] = norms[8 : 8 + KERNEL]


def whole_out_kernel(info, early, late, *outs):
    unpack_grads(info[0], early, late, *outs)


def spread_out(info, early, late):
    taps = HEADS * KERNEL
    shapes = [
        (DIM, 4 * WIDTH), (4, WIDTH), (KERNEL, DIM), (DIM, WIDTH), (WIDTH, taps), (1, taps),
        (DIM, DIM), (1, DIM), (2, DIM), (2, DIM), (1, WIDTH),
    ]
    if len(early) == 2:
        rows_of = (2 * DIM, LATE_ROWS)
        kernel = functools.partial(spread_out_kernel, early_rows=rows_of[0], late_rows=rows_of[1])
        in_specs = [pl.BlockSpec(memory_space=pl.ANY)] * (2 + 2 * PARTS)
        scratch = [pltpu.VMEM((n, DIM), BF) for n in rows_of]
        scratch.append(pltpu.SemaphoreType.DMA((2, PARTS + 1)))
    else:
        kernel = whole_out_kernel
        in_specs = [whole((2 * DIM, DIM)), whole((LATE_ROWS, DIM))]
        scratch = []
    return pl.pallas_call(
        kernel,
        grid_spec=pltpu.PrefetchScalarGridSpec(
            num_scalar_prefetch=1,
            grid=(1,),
            in_specs=in_specs,
            out_specs=[whole(s) for s in shapes],
            scratch_shapes=scratch,
        ),
        out_shape=[sds(s, F32) for s in shapes],
        compiler_params=params(),
        cost_estimate=cost(6),
        name="spread_out",
    )(info, *early, *late)


def digit_groups(size):
    groups, shift = [], 0
    while (1 << shift) < size:
        bits = 2 if (4 << shift) <= size else 1
        groups.append((shift, 1 << bits))
        shift += bits
    return groups


def partner(value, size, distance):
    return lax.ppermute(value, "wide", [(i, i ^ distance) for i in range(size)])


def swap_core(value):
    return lax.ppermute(value, "grp", [(0, 1), (1, 0)])


def fence(*values):
    return lax.optimization_barrier(values)


def add_up(values, dtype=BF):
    total = values[0].astype(F32)
    for v in values[1:]:
        total = total + v.astype(F32)
    return total.astype(dtype)


def gather_relative(block, size):
    buf = block[None]
    for shift, count in reversed(digit_groups(size)):
        parts = [buf] + [partner(buf, size, k << shift) for k in range(1, count)]
        buf = jnp.concatenate(parts, axis=0)
    return buf


def scatter_relative(blocks, size):
    buf = blocks
    for shift, count in digit_groups(size):
        parts = buf.reshape((count, buf.shape[0] // count) + buf.shape[1:])
        buf = add_up([parts[0]] + [partner(parts[k], size, k << shift) for k in range(1, count)])
    return buf[0].astype(F32)


def take(array, index):
    return lax.dynamic_index_in_dim(array, index, 0, keepdims=False)


class Sum:
    def __init__(self, size, half, direct=False):
        self.size, self.value, self.direct = size, half, direct

    def digit(self, group):
        return (lax.axis_index("wide") >> group[0]) & (group[1] - 1)

    def swap(self, group, blocks):
        shift, count = group
        mask = (count - 1) << shift
        teams = [
            [i + (d << shift) for d in range(count)] for i in range(self.size) if not i & mask
        ]
        return [
            lax.all_to_all(
                blocks, "wide", split_axis=0, concat_axis=0, axis_index_groups=teams, tiled=True
            )
        ]

    def send(self, group):
        shift, count = group
        blocks = self.value.reshape(count, self.value.shape[0] // count, DIM)
        if not self.direct:
            self.parts = self.swap(group, blocks)
            return
        digit = self.digit(group)
        self.parts = [take(blocks, digit)] + [
            partner(take(blocks, digit ^ k), self.size, k << shift) for k in range(1, count)
        ]

    def reduce(self):
        if self.direct:
            self.value = add_up(self.parts)
        else:
            self.value = jnp.sum(self.parts[0].astype(F32), axis=0).astype(BF)

    def spread(self, group):
        shift, count = group
        if not self.direct:
            blocks = jnp.broadcast_to(self.value[None], (count,) + self.value.shape)
            self.parts = self.swap(group, blocks)
            return
        self.parts = [self.value] + [
            partner(self.value, self.size, k << shift) for k in range(1, count)
        ]

    def join(self, group):
        if not self.direct:
            self.value = self.parts[0].reshape(-1, DIM)
            return
        digit = self.digit(group)
        stacked = jnp.stack(self.parts)
        self.value = jnp.concatenate([take(stacked, digit ^ d) for d in range(group[1])], axis=0)


def sum_everywhere(keep, send, size):
    core = lax.axis_index("grp")
    total = Sum(size, add_up([keep, swap_core(send)]))
    groups = digit_groups(size)
    for group in groups:
        total.send(group)
        total.reduce()
    for group in reversed(groups):
        total.spread(group)
        total.join(group)
    halves = jnp.stack([total.value, swap_core(total.value)])
    return jnp.concatenate([take(halves, core), take(halves, 1 - core)], axis=0)


def body(
    size,
    hidden_in,
    valid_mask,
    bucket,
    in_weight,
    in_bias,
    depth_weight,
    point_weight,
    kernel_weight,
    kernel_bias,
    out_weight,
    out_bias,
    norm_gain,
    norm_bias,
    ffn_in,
    ffn_in_bias,
    ffn_out,
    ffn_out_bias,
    out_grad,
):
    count = hidden_in.shape[0]
    blocks = count // BLOCK
    shard = ffn_in.shape[1]
    hidden = shard * size
    core = lax.axis_index("grp").astype(jnp.int32)
    group = jnp.reshape(core, (1,))
    info = jnp.concatenate([group, bucket])
    valid = valid_mask.reshape(blocks, 1, BLOCK)
    groups = digit_groups(size)
    staged = len(groups) == 2 and groups[0][1] == groups[1][1] == PARTS and shard % 16 == 0

    bias_rows = jnp.pad(ffn_in_bias, ((0, 15), (0, WIDTH - shard)))
    pack = jnp.concatenate([ffn_in[0], ffn_out[0], bias_rows], axis=0)[None]
    other_bias = swap_core(ffn_out_bias)
    b2 = jnp.concatenate([ffn_out_bias, other_bias], axis=1)
    b2 = jnp.where(core == 0, b2, jnp.concatenate([other_bias, ffn_out_bias], axis=1))

    if staged:
        got = [partner(pack, size, k << groups[1][0]) for k in range(1, PARTS)]
    qkvc, dep, kc, ks, conv_out = project(
        bucket, hidden_in, in_weight, in_bias, depth_weight, point_weight, kernel_weight,
        kernel_bias[None],
    )
    if staged:
        *got, conv_out = fence(*got, conv_out)
        near = jnp.concatenate([pack] + got, axis=0)
        own = [near] + [partner(near, size, k) for k in range(1, PARTS)]
        near_other = swap_core(near)
        near_other, conv_out = fence(near_other, conv_out)
    mixed, logs, hat, inv, xin = attend(
        bucket, valid, qkvc, conv_out, hidden_in, out_weight, out_bias[None], norm_gain, norm_bias
    )
    if staged:
        *own, xin = fence(*own, xin)
        packs = own + [near_other] + [swap_core(v) for v in own[1:]]
    else:
        gathered = gather_relative(pack[0], size)
        packs = [
            pack[None]
            for v in (gathered, swap_core(gathered))
            for pack in repack(v, PARTS, hidden // PARTS)
        ]
    form = (shard, size) if staged else (hidden // PARTS, PARTS)
    (
        output, d_att, d_mixed, dback, act_a, act_b, dpre_a, dpre_b, sums, sums_a, sums_b, out_part,
    ) = middle(
        group, packs, *form, hat, inv, xin, mixed, out_grad, out_weight, norm_gain, norm_bias, b2
    )
    grads_b = ffn_grad(1 - group, dpre_b, act_b, xin, dback, sums_b, *form)
    grads_b, dpre_a = fence(grads_b, dpre_a)
    from_core = swap_core(grads_b)
    grads_a = ffn_grad(group, dpre_a, act_a, xin, dback, sums_a, *form)
    grads_a, from_core, d_mixed = fence(grads_a, from_core, d_mixed)

    if not staged:
        ffn_grads = scatter_relative(
            repack(add_up([grads_a, from_core]), size, shard), size
        )
    else:
        per = size // PARTS
        parts = [
            add_up([grads_a[k * per : (k + 1) * per], from_core[k * per : (k + 1) * per]])
            for k in range(PARTS)
        ]
        xy, z = groups
        *parts, d_mixed = fence(*parts, d_mixed)
        from_x, from_y = partner(parts[1], size, 1), partner(parts[2], size, 2)
    dq, dkv, sums_v, early_keep, early_send = attend_back(
        info, valid, qkvc, d_mixed, logs, hidden_in, out_part
    )
    if staged:
        from_x, from_y, early_send = fence(from_x, from_y, early_send)
        early = Sum(size, add_up([early_keep, swap_core(early_send)]))
        early.value, dq = fence(early.value, dq)
        from_xy = partner(parts[3], size, 3)
        early.send(xy)
    dqc, dkc, late_keep, late_send = conv_back(
        info, qkvc, d_mixed, kc, ks, dq, hidden_in, dep, kernel_weight, point_weight, sums, sums_v
    )
    if staged:
        *early.parts, from_xy, late_send, dkc = fence(*early.parts, from_xy, late_send, dkc)
        late_got = swap_core(late_send)
        parts = [add_up([v[k] for v in (parts[0], from_x, from_y, from_xy)]) for k in range(PARTS)]
        early.reduce()
        late = Sum(size, add_up([late_keep, late_got]), direct=True)
        early.value, late.value, dkc = fence(early.value, late.value, dkc)
        early.send(z)
        late.send(xy)
    hidden_grad = hidden_back(info, dkc, d_att, dqc, dkv, depth_weight, point_weight, in_weight)
    if staged:
        early.parts[0], *late.parts, hidden_grad = fence(
            early.parts[0], *late.parts, hidden_grad
        )
        early.reduce()
        late.reduce()
        early.spread(z)
        late.send(z)
        early.parts[0], *late.parts = fence(early.parts[0], *late.parts)
        early.join(z)
        late.reduce()
        early.value, late.value, *parts = fence(early.value, late.value, *parts)
        early.spread(xy)
        late.spread(z)
        from_z = [partner(parts[k], size, k << z[0]) for k in (1, 2)]
        early.parts[0], *rest = fence(early.parts[0], *late.parts, *from_z, parts[3])
        late.parts, from_z, last = rest[:PARTS], rest[PARTS : PARTS + 2], rest[-1]
        early.join(xy)
        late.join(z)
        early.value, late.value, last = fence(early.value, late.value, last)
        late.spread(xy)
        early_all = [early.value, swap_core(early.value)]
        from_z.append(partner(last, size, 3 << z[0]))
        *late.parts, early_all[1], from_z[2] = fence(*late.parts, early_all[1], from_z[2])
        late_all = late.parts + [swap_core(v) for v in late.parts]
        ffn_grads = add_up([parts[0]] + from_z, F32)
    else:
        early_all = [sum_everywhere(early_keep, early_send, size)]
        late_all = [sum_everywhere(late_keep, late_send, size)]
    (
        in_weight_grad, in_bias_grad, depth_weight_grad, point_weight_grad, kernel_weight_grad,
        kernel_bias_grad, out_weight_grad, out_bias_grad, gain_grad, shift_grad, ffn_out_bias_grad,
    ) = spread_out(
        jnp.stack([core, lax.axis_index("wide").astype(jnp.int32) & (PARTS - 1)]), early_all, late_all
    )
    return (
        output,
        hidden_grad,
        in_weight_grad,
        in_bias_grad,
        depth_weight_grad,
        point_weight_grad,
        kernel_weight_grad,
        kernel_bias_grad[0],
        out_weight_grad,
        out_bias_grad[0],
        gain_grad,
        shift_grad,
        ffn_grads[None, :shard],
        ffn_grads[None, 2 * shard, :shard],
        ffn_grads[None, shard : 2 * shard],
        ffn_out_bias_grad,
    )


def solution(mesh):
    both = ("grp", "wide")
    return jax.shard_map(
        functools.partial(body, mesh.shape["wide"]),
        mesh=mesh,
        in_specs=(
            P(both, None),
            P(both),
            P(both),
            P(),
            P(),
            P(),
            P(),
            P(),
            P(),
            P(),
            P(),
            P(),
            P(),
            P("grp", "wide", None),
            P("grp", "wide"),
            P("grp", "wide", None),
            P("grp", None),
            P(both, None),
        ),
        out_specs=(
            P(both, None),
            P(both, None),
            P(),
            P(),
            P(),
            P(),
            P(),
            P(),
            P(),
            P(),
            P(),
            P(),
            P("grp", "wide", None),
            P("grp", "wide"),
            P("grp", "wide", None),
            P("grp", None),
        ),
        check_vma=False,
    )
```

```python
import functools
import jax
import jax.numpy as jnp
from jax import lax
from jax.experimental import pallas as pl
from jax.experimental.pallas import tpu as pltpu
from jax.sharding import PartitionSpec as P

HEADS = 6
HEAD = 64
KERNEL = 9
EDGE = 4
BLOCK = 512
SHORT = 128
CHUNKS = BLOCK // SHORT
WIDTH = HEADS * HEAD
DIM = 2 * WIDTH
SLAB = 128
TAPS = KERNEL * SLAB
HALO = 8
PADDED = SHORT + 2 * HALO
EPSILON = 1e-12
BF = jnp.bfloat16
F32 = jnp.float32
LIMITS = dict(
    project=60,
    attend=24,
    middle=60,
    ffn_grad=60,
    attend_back=24,
    conv_back=60,
    hidden_back=60,
    spread_out=60,
)


def mm(a, b):
    return lax.dot_general(a, b, (((1,), (0,)), ((), ())), preferred_element_type=F32)


def mm_nt(a, b):
    return lax.dot_general(a, b, (((1,), (1,)), ((), ())), preferred_element_type=F32)


def mm_tn(a, b):
    return lax.dot_general(a, b, (((0,), (0,)), ((), ())), preferred_element_type=F32)


def col_sum(v):
    return jnp.sum(v, axis=0, keepdims=True)


def params(mebibytes):
    return pltpu.CompilerParams(vmem_limit_bytes=mebibytes * 1024 * 1024)


def whole(shape):
    return pl.BlockSpec(shape, lambda *_: (0,) * len(shape))


def rows(tile, width, lane=0):
    return pl.BlockSpec((tile, width), lambda i, *_: (i, lane))


def cost(micros):
    return pl.CostEstimate(flops=int(micros * 1e7), bytes_accessed=int(micros * 3e4), transcendentals=0)


def sds(shape, dtype):
    return jax.ShapeDtypeStruct(shape, dtype)


def fill_padded(pad_ref, values, joined):
    zero = jnp.zeros((HALO, SLAB), F32)
    for c in range(values.shape[1] // SLAB):
        lanes = slice(c * SLAB, (c + 1) * SLAB)
        for s in range(CHUNKS):
            lo, hi = s * SHORT, (s + 1) * SHORT
            pad_ref[c, s, HALO : HALO + SHORT, :] = values[lo:hi, lanes]
            pad_ref[c, s, 0:HALO, :] = values[lo - HALO : lo, lanes] * joined if s else zero
            pad_ref[c, s, HALO + SHORT :, :] = (
                values[hi : hi + HALO, lanes] * joined if s < CHUNKS - 1 else zero
            )


def padded(width):
    return pltpu.VMEM((width // SLAB, CHUNKS, PADDED, SLAB), F32)


def moved(pad_ref, offset, c):
    at = HALO + offset
    return pad_ref[c, :, at : at + SHORT, :].reshape(BLOCK, SLAB)


def add_taps(acc, weight, pad_ref, offset):
    parts = [
        weight[:, c * SLAB : (c + 1) * SLAB] * moved(pad_ref, offset, c)
        for c in range(weight.shape[1] // SLAB)
    ]
    return parts if acc is None else [u + v for u, v in zip(acc, parts)]


def slab_select(rows_of):
    source = lax.broadcasted_iota(jnp.int32, (rows_of, TAPS), 0)
    target = lax.broadcasted_iota(jnp.int32, (rows_of, TAPS), 1)
    head = target % SLAB
    hit = (head < HEADS) & (source == head * KERNEL + target // SLAB)
    return hit.astype(F32)


def head_spread():
    source = lax.broadcasted_iota(jnp.int32, (SLAB, WIDTH), 0)
    target = lax.broadcasted_iota(jnp.int32, (SLAB, WIDTH), 1)
    return (source == target // HEAD).astype(BF)


def norm_stats(v):
    mean = jnp.mean(v, axis=-1, keepdims=True)
    centred = v - mean
    var = jnp.mean(centred * centred, axis=-1, keepdims=True)
    inv = lax.rsqrt(var + EPSILON)
    return centred * inv, inv


def norm_back(d_scaled, hat, inv):
    first = jnp.mean(d_scaled, axis=-1, keepdims=True)
    second = jnp.mean(d_scaled * hat, axis=-1, keepdims=True)
    return inv * (d_scaled - first - hat * second)


def normal_cdf(v):
    density = jnp.exp2(v * v * -0.7213475204444817 - 1.3257480647361595)
    return 0.5 + 0.5 * lax.erf(v * 0.7071067811865476), density


def project_kernel(
    bucket, x, w, bias, dw, pw, kw, kb, qkvc, dep, kc, ks, co, xpad, cvpad
):
    joined = jnp.where(bucket[pl.program_id(0)] == 0, 1.0, 0.0).astype(F32)
    xb = x[...]
    proj = mm(xb, w[...])
    q = (proj[:, :WIDTH] + bias[0:1, :]).astype(BF)
    qkvc[:, 0:WIDTH] = q
    qkvc[:, WIDTH : 2 * WIDTH] = proj[:, WIDTH : 2 * WIDTH].astype(BF)
    qkvc[:, 2 * WIDTH : 3 * WIDTH] = (
        proj[:, 2 * WIDTH : 3 * WIDTH] + bias[1:2, :]
    ).astype(BF)
    cv = (proj[:, 3 * WIDTH :] + bias[2:3, :]).astype(BF)
    qkvc[:, 3 * WIDTH :] = cv
    fill_padded(xpad, xb.astype(F32), joined)
    fill_padded(cvpad, cv.astype(F32), joined)
    for c in range(DIM // SLAB):
        lanes = slice(c * SLAB, (c + 1) * SLAB)
        acc = moved(xpad, -EDGE, c) * dw[0:1, lanes]
        for j in range(1, KERNEL):
            acc += moved(xpad, j - EDGE, c) * dw[j : j + 1, lanes]
        dep[:, lanes] = acc.astype(BF)
    key_conv = mm(dep[...], pw[...]) + bias[3:4, :]
    kc[...] = key_conv
    conv_in = (key_conv * q.astype(F32)).astype(BF)
    select = slab_select(HEADS * KERNEL)
    kw_slab = mm_tn(kw[...], select.astype(BF)).astype(BF)
    kb_slab = jnp.dot(
        jnp.broadcast_to(kb[...], (8, HEADS * KERNEL)),
        select,
        precision=lax.Precision.HIGHEST,
        preferred_element_type=F32,
    )[0:1]
    logits = mm(conv_in, kw_slab) + kb_slab
    slabs = [logits[:, j * SLAB : (j + 1) * SLAB] for j in range(KERNEL)]
    top = functools.reduce(jnp.maximum, slabs)
    slabs = [jnp.exp(v - top) for v in slabs]
    inv = 1.0 / functools.reduce(jnp.add, slabs)
    for j in range(KERNEL):
        ks[:, j * SLAB : (j + 1) * SLAB] = (slabs[j] * inv).astype(BF)
    spread = head_spread()
    acc = None
    for j in range(KERNEL):
        weight = mm(ks[:, j * SLAB : (j + 1) * SLAB], spread)
        acc = add_taps(acc, weight, cvpad, j - EDGE)
    co[...] = jnp.concatenate(acc, axis=1).astype(BF)


def project(bucket, x, in_weight, in_bias, depth_weight, point_weight, kernel_weight, kernel_bias):
    count = x.shape[0]
    blocks = count // BLOCK
    taps = HEADS * KERNEL
    return pl.pallas_call(
        project_kernel,
        grid_spec=pltpu.PrefetchScalarGridSpec(
            num_scalar_prefetch=1,
            grid=(blocks,),
            in_specs=[
                rows(BLOCK, DIM),
                whole((DIM, 4 * WIDTH)),
                whole((4, WIDTH)),
                whole((KERNEL, DIM)),
                whole((DIM, WIDTH)),
                whole((taps, WIDTH)),
                whole((1, taps)),
            ],
            out_specs=[
                rows(BLOCK, 4 * WIDTH),
                rows(BLOCK, DIM),
                rows(BLOCK, WIDTH),
                rows(BLOCK, TAPS),
                rows(BLOCK, WIDTH),
            ],
            scratch_shapes=[
                padded(DIM),
                padded(WIDTH),
            ],
        ),
        out_shape=[
            sds((count, 4 * WIDTH), BF),
            sds((count, DIM), BF),
            sds((count, WIDTH), F32),
            sds((count, TAPS), BF),
            sds((count, WIDTH), BF),
        ],
        compiler_params=params(LIMITS["project"]),
        cost_estimate=cost(17),
        name="project",
    )(bucket, x, in_weight, in_bias, depth_weight, point_weight, kernel_weight, kernel_bias)


def mask_bias(is_short, valid_row):
    column = jnp.transpose(jnp.broadcast_to(valid_row.astype(F32), (SLAB, BLOCK)))
    column = jnp.concatenate([column] * (BLOCK // SLAB), axis=1)
    key_slot = (lax.broadcasted_iota(jnp.int32, (BLOCK, BLOCK), 0) // SHORT) * is_short
    query_slot = (lax.broadcasted_iota(jnp.int32, (BLOCK, BLOCK), 1) // SHORT) * is_short
    return jnp.where((key_slot == query_slot) & (column > 0.0), 0.0, -1e30)


def half_mask(v, h):
    lane = lax.broadcasted_iota(jnp.int32, v.shape, 1)
    keep = lane < HEAD if h % 2 == 0 else lane >= HEAD
    return jnp.where(keep, v, jnp.zeros_like(v))


def attend_kernel(
    bucket, valid, q, k, v, co, x, w_out, b_out, gain, shift,
    mixed, logs, hat, inv, xin, bias, context,
):
    bias[...] = mask_bias(bucket[pl.program_id(0)], valid[...].reshape(1, BLOCK))
    vt = jnp.transpose(v[...])
    logs[...] = jnp.zeros_like(logs)
    for h in range(HEADS):
        lo = (h // 2) * SLAB
        qm = half_mask(q[:, lo : lo + SLAB], h) * jnp.asarray(HEAD**-0.5, BF)
        scores = mm_nt(k[:, lo : lo + SLAB], qm) + bias[...]
        top = jnp.max(scores, axis=0, keepdims=True)
        e = jnp.exp(scores - top)
        total = jnp.sum(e, axis=0, keepdims=True)
        part = mm(vt[h * HEAD : (h + 1) * HEAD], e.astype(BF))
        context[h * HEAD : (h + 1) * HEAD, :] = part / total
        logs[0, h : h + 1, :] = top + jnp.log(total)
    mixed[:, :WIDTH] = jnp.transpose(context[...]).astype(BF)
    mixed[:, WIDTH:] = co[...]
    att = mm(mixed[...], w_out[...]) + b_out[...] + x[...].astype(F32)
    scaled, stat = norm_stats(att)
    hat[...] = scaled
    inv[...] = jnp.broadcast_to(stat, inv.shape)
    xin[...] = (scaled * gain[0:1, :] + shift[0:1, :]).astype(BF)


def attend(bucket, valid, qkvc, conv_out, x, out_weight, out_bias, gain, shift):
    count = qkvc.shape[0]
    blocks = count // BLOCK
    return pl.pallas_call(
        attend_kernel,
        grid_spec=pltpu.PrefetchScalarGridSpec(
            num_scalar_prefetch=1,
            grid=(blocks,),
            in_specs=[
                pl.BlockSpec((1, 1, BLOCK), lambda i, *_: (i, 0, 0)),
                rows(BLOCK, WIDTH, 0),
                rows(BLOCK, WIDTH, 1),
                rows(BLOCK, WIDTH, 2),
                rows(BLOCK, WIDTH),
                rows(BLOCK, DIM),
                whole((DIM, DIM)),
                whole((1, DIM)),
                whole((2, DIM)),
                whole((2, DIM)),
            ],
            out_specs=[
                rows(BLOCK, DIM),
                pl.BlockSpec((1, 8, BLOCK), lambda i, *_: (i, 0, 0)),
                rows(BLOCK, DIM),
                rows(BLOCK, SLAB),
                rows(BLOCK, DIM),
            ],
            scratch_shapes=[
                pltpu.VMEM((BLOCK, BLOCK), F32),
                pltpu.VMEM((WIDTH, BLOCK), F32),
            ],
        ),
        out_shape=[
            sds((count, DIM), BF),
            sds((blocks, 8, BLOCK), F32),
            sds((count, DIM), F32),
            sds((count, SLAB), F32),
            sds((count, DIM), BF),
        ],
        compiler_params=params(LIMITS["attend"]),
        cost_estimate=cost(14),
        name="attend",
    )(bucket, valid, qkvc, qkvc, qkvc, conv_out, x, out_weight, out_bias, gain, shift)


PARTS = 4


def unpack_weights(packs, w1, w2, bias_blocks, sems, g, shard, per):
    copies = []
    for k, pack in enumerate(packs):
        at = pl.ds(k * per, per)
        for n, (lo, size, dst) in enumerate(
            ((0, shard, w1), (shard, shard, w2), (2 * shard, 16, bias_blocks))
        ):
            copies.append(
                pltpu.make_async_copy(
                    pack.at[:, pl.ds(lo, size), :], dst.at[g, at], sems.at[g, k, n]
                )
            )
    return copies


def middle_kernel(
    group, *refs, shard, size
):
    hidden = shard * size
    packs, refs = refs[: 2 * PARTS], refs[2 * PARTS :]
    (
        hat1, inv1, xin, mixed, grad, w_out, gain, shift, b2,
        output, d_att, d_mixed, dback, act_a, dpre_a, sums, sums_a, grads_b, out_grad,
        ffn_out, d_summed, slope, datt_low, bias_sum, out_acc, w1s, w2s, blocks_s, b1s, sems,
        act_all, dpre_all, xin_all, dback_all, sums_b,
    ) = refs
    tile = xin.shape[0]
    here = pl.ds(pl.multiple_of(pl.program_id(0) * tile, tile), tile)
    act_b, dpre_b = act_all.at[here], dpre_all.at[here]
    own = pl.multiple_of(group[0] * WIDTH, SLAB)
    other = pl.multiple_of((1 - group[0]) * WIDTH, SLAB)
    part = 512
    step = pl.program_id(0)
    copies = [
        unpack_weights(
            packs[g * PARTS : (g + 1) * PARTS], w1s, w2s, blocks_s, sems, g, shard, size // PARTS
        )
        for g in range(2)
    ]

    @pl.when(step == 0)
    def _():
        for c in copies[0] + copies[1]:
            c.start()

    @pl.when(step == 0)
    def _():
        sums[...] = jnp.zeros_like(sums)
        bias_sum[...] = jnp.zeros_like(bias_sum)
        out_acc[...] = jnp.zeros_like(out_acc)

    def weights(g):
        return (
            w1s.at[g].reshape(hidden, WIDTH),
            w2s.at[g].reshape(hidden, WIDTH),
            b1s.at[g],
        )

    for g, base, act, at in ((0, own, act_a, 0), (1, other, act_b, hidden)):

        @pl.when(step == 0)
        def _():
            for c in copies[g]:
                c.wait()
            for r in range(size):
                row = blocks_s[g, r].astype(F32)[0:1, :shard]
                b1s[g, 0:1, r * shard : (r + 1) * shard] = row

        w1, w2, b1 = weights(g)
        xg = xin[:, pl.ds(base, WIDTH)]
        for lo in range(0, hidden, part):
            pre = mm_nt(xg, w1[lo : lo + part, :]) + b1[0:1, lo : lo + part]
            cdf, bell = normal_cdf(pre)
            act[:, lo : lo + part] = (pre * cdf).astype(BF)
            slope[:, at + lo : at + lo + part] = (cdf + pre * bell).astype(BF)
        ffn_out[:, pl.ds(base, WIDTH)] = mm(act[...], w2[...])
    result = (ffn_out[...] + b2[...]).astype(BF).astype(F32)
    hat2, inv2 = norm_stats(result + (hat1[...] * gain[0:1, :] + shift[0:1, :]))
    output[...] = (hat2 * gain[1:2, :] + shift[1:2, :]).astype(BF)
    dy = grad[...].astype(F32)
    sums[1:2, :] += col_sum(dy * hat2)
    sums[3:4, :] += col_sum(dy)
    ds = norm_back(dy * gain[1:2, :], hat2, inv2)
    d_summed[...] = ds
    low = ds.astype(BF)
    dback[...] = low
    xin_all[here, :] = xin[:, pl.ds(other, WIDTH)]
    dback_all[here, :] = dback[:, pl.ds(other, WIDTH)]
    sums[5:6, :] += col_sum(low.astype(F32))
    for g, base, dpre, at in ((0, own, dpre_a, 0), (1, other, dpre_b, hidden)):
        w1, w2, b1 = weights(g)
        dg = dback[:, pl.ds(base, WIDTH)]
        for lo in range(0, hidden, part):
            dp = mm_nt(dg, w2[lo : lo + part, :]) * slope[:, at + lo : at + lo + part].astype(F32)
            bias_sum[g : g + 1, lo : lo + part] += col_sum(dp)
            dpre[:, lo : lo + part] = dp.astype(BF)
        ffn_out[:, pl.ds(base, WIDTH)] = mm(dpre[...], w1[...])
    dn = d_summed[...] + ffn_out[...].astype(BF).astype(F32)
    hat = hat1[...]
    sums[0:1, :] += col_sum(dn * hat)
    sums[2:3, :] += col_sum(dn)
    da = norm_back(dn * gain[0:1, :], hat, inv1[:, 0:1])
    d_att[...] = da
    sums[4:5, :] += col_sum(da)
    datt_low[...] = da.astype(BF)
    d_mixed[...] = mm_nt(datt_low[...], w_out[...]).astype(BF)
    out_acc[...] += mm_tn(mixed[...], datt_low[...])

    @pl.when(step == pl.num_programs(0) - 1)
    def _():
        out_grad[...] = out_acc[...].astype(BF)
        for g, dst in ((0, sums_a), (1, sums_b)):
            dst[...] = jnp.zeros_like(dst)
            for r in range(size):
                dst[r, 0:1, 0:shard] = bias_sum[g : g + 1, r * shard : (r + 1) * shard]
        quarter, per = hidden // PARTS, size // PARTS
        for k in range(PARTS):
            lanes = slice(k * quarter, (k + 1) * quarter)
            write_pack(
                dpre_all[:, lanes], act_all[:, lanes], xin_all[...], dback_all[...],
                sums_b, grads_b, k * per, per, shard,
            )


def middle(group, packs, shard, size, hat, inv, xin, mixed, grad, out_weight, gain, shift, b2):
    count = xin.shape[0]
    hidden = shard * size
    tile = BLOCK // 2
    pack_shape = (size, 2 * shard + 16, WIDTH)
    sum_shape = (size, 8, WIDTH)
    return pl.pallas_call(
        functools.partial(middle_kernel, shard=shard, size=size),
        grid_spec=pltpu.PrefetchScalarGridSpec(
            num_scalar_prefetch=1,
            grid=(count // tile,),
            in_specs=[pl.BlockSpec(memory_space=pl.ANY)] * (2 * PARTS)
            + [
                rows(tile, DIM),
                rows(tile, SLAB),
                rows(tile, DIM),
                rows(tile, DIM),
                rows(tile, DIM),
                whole((DIM, DIM)),
                whole((2, DIM)),
                whole((2, DIM)),
                whole((1, DIM)),
            ],
            out_specs=[
                rows(tile, DIM),
                rows(tile, DIM),
                rows(tile, DIM),
                rows(tile, DIM),
                rows(tile, hidden),
                rows(tile, hidden),
                whole((8, DIM)),
                whole(sum_shape),
                whole(pack_shape),
                whole((DIM, DIM)),
            ],
            scratch_shapes=[
                pltpu.VMEM((tile, DIM), F32),
                pltpu.VMEM((tile, DIM), F32),
                pltpu.VMEM((tile, 2 * hidden), BF),
                pltpu.VMEM((tile, DIM), BF),
                pltpu.VMEM((8, hidden), F32),
                pltpu.VMEM((DIM, DIM), F32),
                pltpu.VMEM((2, size, shard, WIDTH), BF),
                pltpu.VMEM((2, size, shard, WIDTH), BF),
                pltpu.VMEM((2, size, 16, WIDTH), BF),
                pltpu.VMEM((2, 8, hidden), F32),
                pltpu.SemaphoreType.DMA((2, PARTS, 3)),
                pltpu.VMEM((count, hidden), BF),
                pltpu.VMEM((count, hidden), BF),
                pltpu.VMEM((count, WIDTH), BF),
                pltpu.VMEM((count, WIDTH), BF),
                pltpu.VMEM(sum_shape, F32),
            ],
        ),
        out_shape=[
            sds((count, DIM), BF),
            sds((count, DIM), F32),
            sds((count, DIM), BF),
            sds((count, DIM), BF),
            sds((count, hidden), BF),
            sds((count, hidden), BF),
            sds((8, DIM), F32),
            sds(sum_shape, F32),
            sds(pack_shape, BF),
            sds((DIM, DIM), BF),
        ],
        compiler_params=params(LIMITS["middle"]),
        cost_estimate=cost(38),
        name="middle",
    )(group, *packs, hat, inv, xin, mixed, grad, out_weight, gain, shift, b2)


def write_pack(dpre, act, xin, dback, sums, out, first_block, per, shard):
    first = mm_tn(dpre, xin).astype(BF)
    second = mm_tn(act, dback).astype(BF)
    for z in range(per):
        out[first_block + z, 0:shard, :] = first[z * shard : (z + 1) * shard]
        out[first_block + z, shard : 2 * shard, :] = second[z * shard : (z + 1) * shard]
        row = jnp.concatenate([sums[first_block + z], jnp.zeros((8, WIDTH), F32)], axis=0)
        out[first_block + z, 2 * shard :, :] = row.astype(BF)


def ffn_grad_kernel(group, dpre, act, xin, dback, sums, out, *, shard):
    write_pack(
        dpre[...], act[...], xin[...], dback[...], sums, out, 0, out.shape[0], shard
    )


def ffn_grad(group, dpre, act, xin, dback, sums, shard, size):
    count, hidden = dpre.shape
    tile = hidden // PARTS
    per = size // PARTS
    lanes = pl.BlockSpec((count, tile), lambda i, g: (0, i))
    side = pl.BlockSpec((count, WIDTH), lambda i, g: (0, g[0]))
    return pl.pallas_call(
        functools.partial(ffn_grad_kernel, shard=shard),
        grid_spec=pltpu.PrefetchScalarGridSpec(
            num_scalar_prefetch=1,
            grid=(PARTS,),
            in_specs=[
                lanes, lanes, side, side, pl.BlockSpec((per, 8, WIDTH), lambda i, g: (i, 0, 0)),
            ],
            out_specs=pl.BlockSpec((per, 2 * shard + 16, WIDTH), lambda i, g: (i, 0, 0)),
        ),
        out_shape=sds((size, 2 * shard + 16, WIDTH), BF),
        compiler_params=params(LIMITS["ffn_grad"]),
        cost_estimate=cost(7),
        name="ffn_grad",
    )(group, dpre, act, xin, dback, sums)


def repack(packs, size, shard):
    old = (packs.shape[1] - 16) // 2
    first = packs[:, :old].reshape(size, shard, WIDTH)
    second = packs[:, old : 2 * old].reshape(size, shard, WIDTH)
    bias = packs[:, 2 * old, :old].reshape(size, 1, shard)
    bias = jnp.pad(bias, ((0, 0), (0, 15), (0, WIDTH - shard)))
    return jnp.concatenate([first, second, bias], axis=1)


def attend_back_kernel(
    info, valid, q, k, v, dctx, logs, x, out_part, dq, dkv, sums, keep, send, bias, dqt, acc
):
    step = pl.program_id(0)

    @pl.when(step == 0)
    def _():
        sums[...] = jnp.zeros_like(sums)
        acc[...] = jnp.zeros_like(acc)

    bias[...] = mask_bias(info[1 + step], valid[...].reshape(1, BLOCK))
    scale = jnp.asarray(HEAD**-0.5, BF)
    kt = jnp.transpose(k[...] * scale)
    for pair in range(HEADS // 2):
        lo = pair * SLAB
        kp = k[:, lo : lo + SLAB]
        vp = v[:, lo : lo + SLAB]
        dk = dv = None
        for h in (2 * pair, 2 * pair + 1):
            qm = half_mask(q[:, lo : lo + SLAB], h) * scale
            cm = half_mask(dctx[:, lo : lo + SLAB], h)
            probs = jnp.exp(mm_nt(kp, qm) + bias[...] - logs[0, h : h + 1, :])
            d_probs = mm_nt(vp, cm)
            delta = col_sum(probs * d_probs)
            d_scores = (probs * (d_probs - delta)).astype(BF)
            probs = probs.astype(BF)
            dv = mm(probs, cm) if dv is None else dv + mm(probs, cm)
            dk = mm(d_scores, qm) if dk is None else dk + mm(d_scores, qm)
            dqt[h * HEAD : (h + 1) * HEAD, :] = mm(kt[h * HEAD : (h + 1) * HEAD], d_scores)
        dkv[:, lo : lo + SLAB] = dk.astype(BF)
        dkv[:, WIDTH + lo : WIDTH + lo + SLAB] = dv.astype(BF)
        sums[0:1, lo : lo + SLAB] += col_sum(dv)
    dq[...] = jnp.transpose(dqt[...])
    acc[...] += mm_tn(x[...], dkv[...])

    @pl.when((step == pl.num_programs(0) - 1) & (info[0] == 0))
    def _():
        keep[...] = out_part[...]
        send[...] = acc[...].astype(BF)

    @pl.when((step == pl.num_programs(0) - 1) & (info[0] != 0))
    def _():
        keep[...] = acc[...].astype(BF)
        send[...] = out_part[...]


def attend_back(info, valid, qkvc, d_mixed, logs, x, out_part):
    count = qkvc.shape[0]
    blocks = count // BLOCK
    return pl.pallas_call(
        attend_back_kernel,
        grid_spec=pltpu.PrefetchScalarGridSpec(
            num_scalar_prefetch=1,
            grid=(blocks,),
            in_specs=[
                pl.BlockSpec((1, 1, BLOCK), lambda i, *_: (i, 0, 0)),
                rows(BLOCK, WIDTH, 0),
                rows(BLOCK, WIDTH, 1),
                rows(BLOCK, WIDTH, 2),
                rows(BLOCK, WIDTH, 0),
                pl.BlockSpec((1, 8, BLOCK), lambda i, *_: (i, 0, 0)),
                rows(BLOCK, DIM),
                whole((DIM, DIM)),
            ],
            out_specs=[
                rows(BLOCK, WIDTH),
                rows(BLOCK, DIM),
                whole((8, WIDTH)),
                whole((DIM, DIM)),
                whole((DIM, DIM)),
            ],
            scratch_shapes=[
                pltpu.VMEM((BLOCK, BLOCK), F32),
                pltpu.VMEM((WIDTH, BLOCK), F32),
                pltpu.VMEM((DIM, DIM), F32),
            ],
        ),
        out_shape=[
            sds((count, WIDTH), F32),
            sds((count, DIM), BF),
            sds((8, WIDTH), F32),
            sds((DIM, DIM), BF),
            sds((DIM, DIM), BF),
        ],
        compiler_params=params(LIMITS["attend_back"]),
        cost_estimate=cost(16),
        name="attend_back",
    )(info, valid, qkvc, qkvc, qkvc, d_mixed, logs, x, out_part)


POINT_ROW = DIM
SMALL_ROW = DIM + WIDTH
LATE_ROWS = DIM + WIDTH + 128
NORM_ROW = SMALL_ROW + 64
TAP_ROW = SMALL_ROW + 72


def conv_back_kernel(
    info, q, cv, dconv, kc, ks, dq, x, dep, kw, pw, sums_mid, sums_v, dqc, dkc, keep, send,
    cvpad, dcpad, kspad, xpad, dk_slab, dlog, qc_acc, pt_acc, kw_acc, kb_acc, dw_acc, sums, flat
):
    step = pl.program_id(0)
    taps = HEADS * KERNEL

    @pl.when(step == 0)
    def _():
        for ref in (qc_acc, pt_acc, kw_acc, kb_acc, dw_acc, sums):
            ref[...] = jnp.zeros_like(ref)

    joined = jnp.where(info[1 + step] == 0, 1.0, 0.0).astype(F32)
    dc = dconv[...].astype(F32)
    fill_padded(cvpad, cv[...].astype(F32), joined)
    fill_padded(dcpad, dc, joined)
    fill_padded(kspad, ks[...].astype(F32), joined)
    fill_padded(xpad, x[...].astype(F32), joined)
    spread = head_spread()
    total = None
    for j in range(KERNEL):
        product = jnp.concatenate(add_taps(None, dc, cvpad, j - EDGE), axis=1)
        part = mm_nt(product.astype(BF), spread)
        dk_slab[:, j * SLAB : (j + 1) * SLAB] = part
        part = part * ks[:, j * SLAB : (j + 1) * SLAB].astype(F32)
        total = part if total is None else total + part
    for j in range(KERNEL):
        lanes = slice(j * SLAB, (j + 1) * SLAB)
        grad = ks[:, lanes].astype(F32) * (dk_slab[:, lanes] - total)
        kb_acc[0:1, lanes] += col_sum(grad)
        dlog[:, lanes] = grad.astype(BF)
    acc = None
    for j in range(KERNEL):
        weight = mm(moved(kspad, EDGE - j, j).astype(BF), spread)
        acc = add_taps(acc, weight, dcpad, EDGE - j)
    acc = jnp.concatenate(acc, axis=1)
    dqc[:, WIDTH:] = acc.astype(BF)
    sums[1:2, :] += col_sum(acc)
    select = slab_select(taps)
    compact = mm_nt(dlog[...], select.astype(BF)).astype(BF)
    qf = q[...].astype(F32)
    key_conv = kc[...]
    conv_in = (key_conv * qf).astype(BF)
    kw_acc[0:taps, :] += mm_tn(compact, conv_in)
    d_conv_in = mm(compact, kw[...])
    d_key = d_conv_in * qf
    sums[2:3, :] += col_sum(d_key)
    dkc[...] = d_key.astype(BF)
    dq_all = dq[...] + d_conv_in * key_conv
    sums[0:1, :] += col_sum(dq_all)
    dqc[:, :WIDTH] = dq_all.astype(BF)
    qc_acc[...] += mm_tn(x[...], dqc[...])
    pt_acc[...] += mm_tn(dep[...], dkc[...])
    d_depth = mm_nt(dkc[...], pw[...])
    for c in range(DIM // SLAB):
        lanes = slice(c * SLAB, (c + 1) * SLAB)
        here = d_depth[:, lanes]
        for j in range(KERNEL):
            dw_acc[j : j + 1, lanes] += col_sum(moved(xpad, j - EDGE, c) * here)

    @pl.when(step == pl.num_programs(0) - 1)
    def _():
        flat[0:DIM, :] = qc_acc[...].astype(BF)
        flat[POINT_ROW:SMALL_ROW, 0:WIDTH] = pt_acc[0:WIDTH, :].astype(BF)
        flat[POINT_ROW:SMALL_ROW, WIDTH:] = pt_acc[WIDTH:, :].astype(BF)
        flat[SMALL_ROW : SMALL_ROW + 64, 0:WIDTH] = kw_acc[...].astype(BF)
        kb = lax.dot_general(
            kb_acc[...],
            select,
            (((1,), (1,)), ((), ())),
            precision=lax.Precision.HIGHEST,
            preferred_element_type=F32,
        )
        blank = jnp.zeros((4, WIDTH), F32)
        rows_of = jnp.concatenate([sums[0:1], sums_v[0:1], sums[1:3], blank], axis=0)
        kb = jnp.concatenate([kb, jnp.zeros((8, WIDTH - taps), F32)], axis=1)
        flat[SMALL_ROW : SMALL_ROW + 16, WIDTH:] = jnp.concatenate([rows_of, kb], axis=0).astype(BF)
        flat[SMALL_ROW + 16 : NORM_ROW, WIDTH:] = jnp.zeros((48, WIDTH), BF)
        flat[NORM_ROW : NORM_ROW + 32, :] = jnp.concatenate(
            [sums_mid[...], dw_acc[...], jnp.zeros((8, DIM), F32)], axis=0
        ).astype(BF)
        flat[NORM_ROW + 32 :, :] = jnp.zeros((32, DIM), BF)
        half = LATE_ROWS // 2
        core = info[0]
        keep[...] = flat[pl.ds(pl.multiple_of(core * half, 16), half), :]
        send[...] = flat[pl.ds(pl.multiple_of((1 - core) * half, 16), half), :]


def conv_back(info, qkvc, d_mixed, kc, ks, dq, x, dep, kernel_weight, point_weight, sums_mid, sums_v):
    count = qkvc.shape[0]
    blocks = count // BLOCK
    taps = HEADS * KERNEL
    half = LATE_ROWS // 2
    return pl.pallas_call(
        conv_back_kernel,
        grid_spec=pltpu.PrefetchScalarGridSpec(
            num_scalar_prefetch=1,
            grid=(blocks,),
            in_specs=[
                rows(BLOCK, WIDTH, 0),
                rows(BLOCK, WIDTH, 3),
                rows(BLOCK, WIDTH, 1),
                rows(BLOCK, WIDTH),
                rows(BLOCK, TAPS),
                rows(BLOCK, WIDTH),
                rows(BLOCK, DIM),
                rows(BLOCK, DIM),
                whole((taps, WIDTH)),
                whole((DIM, WIDTH)),
                whole((8, DIM)),
                whole((8, WIDTH)),
            ],
            out_specs=[
                rows(BLOCK, DIM),
                rows(BLOCK, WIDTH),
                whole((half, DIM)),
                whole((half, DIM)),
            ],
            scratch_shapes=[
                padded(WIDTH),
                padded(WIDTH),
                padded(TAPS),
                padded(DIM),
                pltpu.VMEM((BLOCK, TAPS), F32),
                pltpu.VMEM((BLOCK, TAPS), BF),
                pltpu.VMEM((DIM, DIM), F32),
                pltpu.VMEM((DIM, WIDTH), F32),
                pltpu.VMEM((64, WIDTH), F32),
                pltpu.VMEM((8, TAPS), F32),
                pltpu.VMEM((16, DIM), F32),
                pltpu.VMEM((8, WIDTH), F32),
                pltpu.VMEM((LATE_ROWS, DIM), BF),
            ],
        ),
        out_shape=[
            sds((count, DIM), BF),
            sds((count, WIDTH), BF),
            sds((half, DIM), BF),
            sds((half, DIM), BF),
        ],
        compiler_params=params(LIMITS["conv_back"]),
        cost_estimate=cost(22),
        name="conv_back",
    )(info, qkvc, qkvc, d_mixed, kc, ks, dq, x, dep, kernel_weight, point_weight, sums_mid, sums_v)


def hidden_kernel(info, dkc, d_att, dqc, dkv, dw, pw, w, hidden, ddpad):
    joined = jnp.where(info[1 + pl.program_id(0)] == 0, 1.0, 0.0).astype(F32)
    fill_padded(ddpad, mm_nt(dkc[...], pw[...]), joined)
    hidden[...] = (
        d_att[...]
        + mm_nt(dkv[...], w[:, WIDTH : 3 * WIDTH])
        + mm_nt(dqc[:, :WIDTH], w[:, :WIDTH])
        + mm_nt(dqc[:, WIDTH:], w[:, 3 * WIDTH :])
    )
    for c in range(DIM // SLAB):
        lanes = slice(c * SLAB, (c + 1) * SLAB)
        acc = hidden[:, lanes]
        for j in range(KERNEL):
            acc += moved(ddpad, EDGE - j, c) * dw[j : j + 1, lanes]
        hidden[:, lanes] = acc


def hidden_back(info, dkc, d_att, dqc, dkv, depth_weight, point_weight, in_weight):
    count = d_att.shape[0]
    return pl.pallas_call(
        hidden_kernel,
        grid_spec=pltpu.PrefetchScalarGridSpec(
            num_scalar_prefetch=1,
            grid=(count // BLOCK,),
            in_specs=[
                rows(BLOCK, WIDTH),
                rows(BLOCK, DIM),
                rows(BLOCK, DIM),
                rows(BLOCK, DIM),
                whole((KERNEL, DIM)),
                whole((DIM, WIDTH)),
                whole((DIM, 4 * WIDTH)),
            ],
            out_specs=rows(BLOCK, DIM),
            scratch_shapes=[padded(DIM)],
        ),
        out_shape=sds((count, DIM), F32),
        compiler_params=params(LIMITS["hidden_back"]),
        cost_estimate=cost(12),
        name="hidden_back",
    )(info, dkc, d_att, dqc, dkv, depth_weight, point_weight, in_weight)


def spread_out_kernel(info, *refs, early_rows, late_rows):
    late_in, early_in, refs = refs[:2], refs[2 : 2 + 2 * PARTS], refs[2 + 2 * PARTS :]
    in_w, in_b, dw, point, kw, kb, out_w, out_b, gain, shift, b2, early, late, sems = refs
    core, digit = info[0], info[1]
    half, early_half = late_rows // 2, early_rows // 2
    quarter = early_half // PARTS
    copies = []
    for c in range(2):
        at = pl.ds(pl.multiple_of((core ^ c) * half, 16), half)
        copies.append(pltpu.make_async_copy(late_in[c], late.at[at, :], sems.at[c, PARTS]))
        for k in range(PARTS):
            row = (core ^ c) * early_half + (digit ^ k) * quarter
            at = pl.ds(pl.multiple_of(row, 16), quarter)
            copies.append(
                pltpu.make_async_copy(early_in[c * PARTS + k], early.at[at, :], sems.at[c, k])
            )
    for c in copies:
        c.start()
    for c in copies:
        c.wait()
    unpack_grads(core, early, late, in_w, in_b, dw, point, kw, kb, out_w, out_b, gain, shift, b2)


def unpack_grads(core, early, late, in_w, in_b, dw, point, kw, kb, out_w, out_b, gain, shift, b2):
    taps = HEADS * KERNEL
    out_w[...] = early[0:DIM, :].astype(F32)
    in_w[:, WIDTH : 3 * WIDTH] = early[DIM:, :].astype(F32)
    in_w[:, 0:WIDTH] = late[0:DIM, 0:WIDTH].astype(F32)
    in_w[:, 3 * WIDTH :] = late[0:DIM, WIDTH:].astype(F32)
    point[0:WIDTH, :] = late[POINT_ROW:SMALL_ROW, 0:WIDTH].astype(F32)
    point[WIDTH:, :] = late[POINT_ROW:SMALL_ROW, WIDTH:].astype(F32)
    kw[...] = late[SMALL_ROW : SMALL_ROW + 64, 0:WIDTH].astype(F32)[0:taps]
    mixed = late[SMALL_ROW : SMALL_ROW + 16, WIDTH:].astype(F32)
    in_b[...] = mixed[0:4]
    kb[...] = mixed[8:9, 0:taps]
    norms = late[NORM_ROW : NORM_ROW + 32, :].astype(F32)
    gain[...] = norms[0:2]
    shift[...] = norms[2:4]
    out_b[...] = norms[4]
    b2[...] = jnp.where(core == 0, norms[5:6, 0:WIDTH], norms[5:6, WIDTH:])
    dw[...] = norms[8 : 8 + KERNEL]


def whole_out_kernel(info, early, late, *outs):
    unpack_grads(info[0], early, late, *outs)


def spread_out(info, early, late):
    taps = HEADS * KERNEL
    shapes = [
        (DIM, 4 * WIDTH), (4, WIDTH), (KERNEL, DIM), (DIM, WIDTH), (taps, WIDTH), (1, taps),
        (DIM, DIM), (DIM,), (2, DIM), (2, DIM), (1, WIDTH),
    ]
    if len(late) == 2:
        rows_of = (2 * DIM, LATE_ROWS)
        kernel = functools.partial(spread_out_kernel, early_rows=rows_of[0], late_rows=rows_of[1])
        in_specs = [pl.BlockSpec(memory_space=pl.ANY)] * (2 + 2 * PARTS)
        scratch = [pltpu.VMEM((n, DIM), BF) for n in rows_of]
        scratch.append(pltpu.SemaphoreType.DMA((2, PARTS + 1)))
    else:
        kernel = whole_out_kernel
        in_specs = [whole((2 * DIM, DIM)), whole((LATE_ROWS, DIM))]
        scratch = []
    return pl.pallas_call(
        kernel,
        grid_spec=pltpu.PrefetchScalarGridSpec(
            num_scalar_prefetch=1,
            grid=(1,),
            in_specs=in_specs,
            out_specs=[whole(s) for s in shapes],
            scratch_shapes=scratch,
        ),
        out_shape=[sds(s, F32) for s in shapes],
        compiler_params=params(LIMITS["spread_out"]),
        cost_estimate=cost(6),
        name="spread_out",
    )(info, *(late + early if len(late) == 2 else early + late))


def digit_groups(size):
    groups, shift = [], 0
    while (1 << shift) < size:
        bits = 2 if (4 << shift) <= size else 1
        groups.append((shift, 1 << bits))
        shift += bits
    return groups


def partner(value, size, distance):
    return lax.ppermute(value, "wide", [(i, i ^ distance) for i in range(size)])


def swap_core(value):
    return lax.ppermute(value, "grp", [(0, 1), (1, 0)])


def fence(*values):
    return lax.optimization_barrier(values)


def add_up(values, dtype=BF):
    total = values[0].astype(F32)
    for v in values[1:]:
        total = total + v.astype(F32)
    return total.astype(dtype)


def gather_relative(block, size):
    buf = block[None]
    for shift, count in reversed(digit_groups(size)):
        parts = [buf] + [partner(buf, size, k << shift) for k in range(1, count)]
        buf = jnp.concatenate(parts, axis=0)
    return buf


def scatter_relative(blocks, size):
    buf = blocks
    for shift, count in digit_groups(size):
        parts = buf.reshape((count, buf.shape[0] // count) + buf.shape[1:])
        buf = add_up([parts[0]] + [partner(parts[k], size, k << shift) for k in range(1, count)])
    return buf[0].astype(F32)


def take(array, index):
    return lax.dynamic_index_in_dim(array, index, 0, keepdims=False)


class Sum:
    def __init__(self, size, half, direct=False):
        self.size, self.value, self.direct = size, half, direct

    def digit(self, group):
        return (lax.axis_index("wide") >> group[0]) & (group[1] - 1)

    def swap(self, group, blocks):
        shift, count = group
        mask = (count - 1) << shift
        teams = [
            [i + (d << shift) for d in range(count)] for i in range(self.size) if not i & mask
        ]
        return [
            lax.all_to_all(
                blocks, "wide", split_axis=0, concat_axis=0, axis_index_groups=teams, tiled=True
            )
        ]

    def send(self, group):
        shift, count = group
        blocks = self.value.reshape(count, self.value.shape[0] // count, DIM)
        if not self.direct:
            self.parts = self.swap(group, blocks)
            return
        digit = self.digit(group)
        self.parts = [take(blocks, digit)] + [
            partner(take(blocks, digit ^ k), self.size, k << shift) for k in range(1, count)
        ]

    def reduce(self):
        if self.direct:
            self.value = add_up(self.parts)
        else:
            self.value = jnp.sum(self.parts[0].astype(F32), axis=0).astype(BF)

    def spread(self, group):
        shift, count = group
        if not self.direct:
            blocks = jnp.broadcast_to(self.value[None], (count,) + self.value.shape)
            self.parts = self.swap(group, blocks)
            return
        self.parts = [self.value] + [
            partner(self.value, self.size, k << shift) for k in range(1, count)
        ]

    def join(self, group):
        if not self.direct:
            self.value = self.parts[0].reshape(-1, DIM)
            return
        digit = self.digit(group)
        stacked = jnp.stack(self.parts)
        self.value = jnp.concatenate([take(stacked, digit ^ d) for d in range(group[1])], axis=0)


def sum_everywhere(keep, send, size):
    core = lax.axis_index("grp")
    total = Sum(size, add_up([keep, swap_core(send)]))
    groups = digit_groups(size)
    for group in groups:
        total.send(group)
        total.reduce()
    for group in reversed(groups):
        total.spread(group)
        total.join(group)
    halves = jnp.stack([total.value, swap_core(total.value)])
    return jnp.concatenate([take(halves, core), take(halves, 1 - core)], axis=0)


def body(
    size,
    hidden_in,
    valid_mask,
    bucket,
    in_weight,
    in_bias,
    depth_weight,
    point_weight,
    kernel_weight,
    kernel_bias,
    out_weight,
    out_bias,
    norm_gain,
    norm_bias,
    ffn_in,
    ffn_in_bias,
    ffn_out,
    ffn_out_bias,
    out_grad,
):
    count = hidden_in.shape[0]
    blocks = count // BLOCK
    shard = ffn_in.shape[1]
    hidden = shard * size
    core = lax.axis_index("grp").astype(jnp.int32)
    group = jnp.reshape(core, (1,))
    info = jnp.concatenate([group, bucket])
    valid = valid_mask.reshape(blocks, 1, BLOCK)
    kernel_weight = kernel_weight.T
    groups = digit_groups(size)
    staged = len(groups) == 2 and groups[0][1] == groups[1][1] == PARTS and shard % 16 == 0

    bias_rows = jnp.pad(ffn_in_bias, ((0, 15), (0, WIDTH - shard)))
    pack = jnp.concatenate([ffn_in[0], ffn_out[0], bias_rows], axis=0)[None]
    other_bias = swap_core(ffn_out_bias)
    b2 = jnp.concatenate([ffn_out_bias, other_bias], axis=1)
    b2 = jnp.where(core == 0, b2, jnp.concatenate([other_bias, ffn_out_bias], axis=1))

    if staged:
        got = [partner(pack, size, k << groups[1][0]) for k in range(1, PARTS)]
    qkvc, dep, kc, ks, conv_out = project(
        bucket, hidden_in, in_weight, in_bias, depth_weight, point_weight, kernel_weight,
        kernel_bias[None],
    )
    if staged:
        *got, conv_out = fence(*got, conv_out)
        near = jnp.concatenate([pack] + got, axis=0)
        own = [near] + [partner(near, size, k) for k in range(1, PARTS)]
        near_other = swap_core(near)
        near_other, conv_out = fence(near_other, conv_out)
    mixed, logs, hat, inv, xin = attend(
        bucket, valid, qkvc, conv_out, hidden_in, out_weight, out_bias[None], norm_gain, norm_bias
    )
    if staged:
        *own, xin = fence(*own, xin)
        packs = own + [near_other] + [swap_core(v) for v in own[1:]]
    else:
        gathered = gather_relative(pack[0], size)
        packs = [
            pack[None]
            for v in (gathered, swap_core(gathered))
            for pack in repack(v, PARTS, hidden // PARTS)
        ]
    form = (shard, size) if staged else (hidden // PARTS, PARTS)
    (
        output, d_att, d_mixed, dback, act_a, dpre_a, sums, sums_a, grads_b, out_part,
    ) = middle(
        group, packs, *form, hat, inv, xin, mixed, out_grad, out_weight, norm_gain, norm_bias, b2
    )
    from_core = swap_core(grads_b)
    grads_a = ffn_grad(group, dpre_a, act_a, xin, dback, sums_a, *form)
    grads_a, from_core, d_mixed = fence(grads_a, from_core, d_mixed)

    if not staged:
        ffn_grads = scatter_relative(
            repack(add_up([grads_a, from_core]), size, shard), size
        )
    else:
        per = size // PARTS
        parts = [
            add_up([grads_a[k * per : (k + 1) * per], from_core[k * per : (k + 1) * per]])
            for k in range(PARTS)
        ]
        xy, z = groups
        *parts, d_mixed = fence(*parts, d_mixed)
        from_x, from_y = partner(parts[1], size, 1), partner(parts[2], size, 2)
    dq, dkv, sums_v, early_keep, early_send = attend_back(
        info, valid, qkvc, d_mixed, logs, hidden_in, out_part
    )
    if staged:
        from_x, from_y, early_send = fence(from_x, from_y, early_send)
        early = Sum(size, add_up([early_keep, swap_core(early_send)]), direct=True)
        early.value, dq = fence(early.value, dq)
        from_xy = partner(parts[3], size, 3)
        early.send(xy)
    dqc, dkc, late_keep, late_send = conv_back(
        info, qkvc, d_mixed, kc, ks, dq, hidden_in, dep, kernel_weight, point_weight, sums, sums_v
    )
    if staged:
        *early.parts, from_xy, late_send, dkc = fence(*early.parts, from_xy, late_send, dkc)
        late_got = swap_core(late_send)
        parts = [add_up([v[k] for v in (parts[0], from_x, from_y, from_xy)]) for k in range(PARTS)]
        early.reduce()
        late = Sum(size, add_up([late_keep, late_got]))
        early.value, late.value, dkc = fence(early.value, late.value, dkc)
        late.send(xy)
        early.send(z)
    hidden_grad = hidden_back(info, dkc, d_att, dqc, dkv, depth_weight, point_weight, in_weight)
    if staged:
        late.parts[0], *early.parts, hidden_grad = fence(late.parts[0], *early.parts, hidden_grad)
        late.reduce()
        early.reduce()
        late.value, early.value = fence(late.value, early.value)
        late.send(z)
        early.spread(z)
        late.parts[0], *early.parts = fence(late.parts[0], *early.parts)
        late.reduce()
        early.join(z)
        early.value, late.value, *parts = fence(early.value, late.value, *parts)
        late.spread(z)
        early.spread(xy)
        from_z = [partner(parts[k], size, k << z[0]) for k in (1, 2)]
        late.parts[0], *rest = fence(late.parts[0], *early.parts, *from_z, parts[3])
        early.parts, from_z, last = rest[:PARTS], rest[PARTS : PARTS + 2], rest[-1]
        late.join(z)
        late.spread(xy)
        early_all = early.parts + [swap_core(v) for v in early.parts]
        from_z.append(partner(last, size, 3 << z[0]))
        late.parts[0], from_z[2], *early_all = fence(late.parts[0], from_z[2], *early_all)
        late.join(xy)
        late_all = [late.value, swap_core(late.value)]
        ffn_grads = add_up([parts[0]] + from_z, F32)
    else:
        early_all = [sum_everywhere(early_keep, early_send, size)]
        late_all = [sum_everywhere(late_keep, late_send, size)]
    (
        in_weight_grad, in_bias_grad, depth_weight_grad, point_weight_grad, kernel_weight_grad,
        kernel_bias_grad, out_weight_grad, out_bias_grad, gain_grad, shift_grad, ffn_out_bias_grad,
    ) = spread_out(
        jnp.stack([core, lax.axis_index("wide").astype(jnp.int32) & (PARTS - 1)]), early_all, late_all
    )
    return (
        output,
        hidden_grad,
        in_weight_grad,
        in_bias_grad,
        depth_weight_grad,
        point_weight_grad,
        kernel_weight_grad.T,
        kernel_bias_grad[0],
        out_weight_grad,
        out_bias_grad,
        gain_grad,
        shift_grad,
        ffn_grads[None, :shard],
        ffn_grads[None, 2 * shard, :shard],
        ffn_grads[None, shard : 2 * shard],
        ffn_out_bias_grad,
    )


def solution(mesh):
    both = ("grp", "wide")
    return jax.shard_map(
        functools.partial(body, mesh.shape["wide"]),
        mesh=mesh,
        in_specs=(
            P(both, None),
            P(both),
            P(both),
            P(),
            P(),
            P(),
            P(),
            P(),
            P(),
            P(),
            P(),
            P(),
            P(),
            P("grp", "wide", None),
            P("grp", "wide"),
            P("grp", "wide", None),
            P("grp", None),
            P(both, None),
        ),
        out_specs=(
            P(both, None),
            P(both, None),
            P(),
            P(),
            P(),
            P(),
            P(),
            P(),
            P(),
            P(),
            P(),
            P(),
            P("grp", "wide", None),
            P("grp", "wide"),
            P("grp", "wide", None),
            P("grp", None),
        ),
        check_vma=False,
    )
```

```python
import functools
import jax
import jax.numpy as jnp
from jax import lax
from jax.experimental import pallas as pl
from jax.experimental.pallas import tpu as pltpu
from jax.sharding import PartitionSpec as P

HEADS = 6
HEAD = 64
KERNEL = 9
EDGE = 4
BLOCK = 512
SHORT = 128
CHUNKS = BLOCK // SHORT
WIDTH = HEADS * HEAD
DIM = 2 * WIDTH
SLAB = 128
TAPS = KERNEL * SLAB
HALO = 8
PADDED = SHORT + 2 * HALO
EPSILON = 1e-12
BF = jnp.bfloat16
F32 = jnp.float32
LIMITS = dict(
    project=60,
    attend=24,
    middle=60,
    ffn_grad=60,
    attend_back=60,
    conv_back=60,
    hidden_back=60,
    unpack=60,
)


def mm(a, b):
    return lax.dot_general(a, b, (((1,), (0,)), ((), ())), preferred_element_type=F32)


def mm_nt(a, b):
    return lax.dot_general(a, b, (((1,), (1,)), ((), ())), preferred_element_type=F32)


def mm_tn(a, b):
    return lax.dot_general(a, b, (((0,), (0,)), ((), ())), preferred_element_type=F32)


def col_sum(v):
    return jnp.sum(v, axis=0, keepdims=True)


def params(mebibytes):
    return pltpu.CompilerParams(vmem_limit_bytes=mebibytes * 1024 * 1024)


def whole(shape):
    return pl.BlockSpec(shape, lambda *_: (0,) * len(shape))


def rows(tile, width, lane=0):
    return pl.BlockSpec((tile, width), lambda i, *_: (i, lane))


def cost(micros):
    return pl.CostEstimate(flops=int(micros * 1e7), bytes_accessed=int(micros * 3e4), transcendentals=0)


def sds(shape, dtype):
    return jax.ShapeDtypeStruct(shape, dtype)


def fill_padded(pad_ref, values, joined):
    zero = jnp.zeros((HALO, SLAB), F32)
    for c in range(values.shape[1] // SLAB):
        lanes = slice(c * SLAB, (c + 1) * SLAB)
        for s in range(CHUNKS):
            lo, hi = s * SHORT, (s + 1) * SHORT
            pad_ref[c, s, HALO : HALO + SHORT, :] = values[lo:hi, lanes]
            pad_ref[c, s, 0:HALO, :] = values[lo - HALO : lo, lanes] * joined if s else zero
            pad_ref[c, s, HALO + SHORT :, :] = (
                values[hi : hi + HALO, lanes] * joined if s < CHUNKS - 1 else zero
            )


def padded(width):
    return pltpu.VMEM((width // SLAB, CHUNKS, PADDED, SLAB), F32)


def moved(pad_ref, offset, c):
    at = HALO + offset
    return pad_ref[c, :, at : at + SHORT, :].reshape(BLOCK, SLAB)


def add_taps(acc, weight, pad_ref, offset):
    parts = [
        weight[:, c * SLAB : (c + 1) * SLAB] * moved(pad_ref, offset, c)
        for c in range(weight.shape[1] // SLAB)
    ]
    return parts if acc is None else [u + v for u, v in zip(acc, parts)]


def slab_select(rows_of):
    source = lax.broadcasted_iota(jnp.int32, (rows_of, TAPS), 0)
    target = lax.broadcasted_iota(jnp.int32, (rows_of, TAPS), 1)
    head = target % SLAB
    hit = (head < HEADS) & (source == head * KERNEL + target // SLAB)
    return hit.astype(F32)


def head_spread():
    source = lax.broadcasted_iota(jnp.int32, (SLAB, WIDTH), 0)
    target = lax.broadcasted_iota(jnp.int32, (SLAB, WIDTH), 1)
    return (source == target // HEAD).astype(BF)


def norm_stats(v):
    mean = jnp.mean(v, axis=-1, keepdims=True)
    centred = v - mean
    var = jnp.mean(centred * centred, axis=-1, keepdims=True)
    inv = lax.rsqrt(var + EPSILON)
    return centred * inv, inv


def norm_back(d_scaled, hat, inv):
    first = jnp.mean(d_scaled, axis=-1, keepdims=True)
    second = jnp.mean(d_scaled * hat, axis=-1, keepdims=True)
    return inv * (d_scaled - first - hat * second)


def normal_cdf(v):
    density = jnp.exp2(v * v * -0.7213475204444817 - 1.3257480647361595)
    return 0.5 + 0.5 * lax.erf(v * 0.7071067811865476), density


def project_kernel(
    bucket, x, w, bias, dw, pw, kw, kb, qkvc, dep, kc, ks, co, xpad, cvpad
):
    joined = jnp.where(bucket[pl.program_id(0)] == 0, 1.0, 0.0).astype(F32)
    xb = x[...]
    proj = mm(xb, w[...])
    q = (proj[:, :WIDTH] + bias[0:1, :]).astype(BF)
    qkvc[:, 0:WIDTH] = q
    qkvc[:, WIDTH : 2 * WIDTH] = proj[:, WIDTH : 2 * WIDTH].astype(BF)
    qkvc[:, 2 * WIDTH : 3 * WIDTH] = (
        proj[:, 2 * WIDTH : 3 * WIDTH] + bias[1:2, :]
    ).astype(BF)
    cv = (proj[:, 3 * WIDTH :] + bias[2:3, :]).astype(BF)
    qkvc[:, 3 * WIDTH :] = cv
    fill_padded(xpad, xb.astype(F32), joined)
    fill_padded(cvpad, cv.astype(F32), joined)
    for c in range(DIM // SLAB):
        lanes = slice(c * SLAB, (c + 1) * SLAB)
        acc = moved(xpad, -EDGE, c) * dw[0:1, lanes]
        for j in range(1, KERNEL):
            acc += moved(xpad, j - EDGE, c) * dw[j : j + 1, lanes]
        dep[:, lanes] = acc.astype(BF)
    key_conv = mm(dep[...], pw[...]) + bias[3:4, :]
    kc[...] = key_conv
    conv_in = (key_conv * q.astype(F32)).astype(BF)
    select = slab_select(HEADS * KERNEL)
    kw_slab = mm_tn(kw[...], select.astype(BF)).astype(BF)
    kb_slab = jnp.dot(
        jnp.broadcast_to(kb[...], (8, HEADS * KERNEL)),
        select,
        precision=lax.Precision.HIGHEST,
        preferred_element_type=F32,
    )[0:1]
    logits = mm(conv_in, kw_slab) + kb_slab
    slabs = [logits[:, j * SLAB : (j + 1) * SLAB] for j in range(KERNEL)]
    top = functools.reduce(jnp.maximum, slabs)
    slabs = [jnp.exp(v - top) for v in slabs]
    inv = 1.0 / functools.reduce(jnp.add, slabs)
    for j in range(KERNEL):
        ks[:, j * SLAB : (j + 1) * SLAB] = (slabs[j] * inv).astype(BF)
    spread = head_spread()
    acc = None
    for j in range(KERNEL):
        weight = mm(ks[:, j * SLAB : (j + 1) * SLAB], spread)
        acc = add_taps(acc, weight, cvpad, j - EDGE)
    co[...] = jnp.concatenate(acc, axis=1).astype(BF)


def project(bucket, x, in_weight, in_bias, depth_weight, point_weight, kernel_weight, kernel_bias):
    count = x.shape[0]
    blocks = count // BLOCK
    taps = HEADS * KERNEL
    return pl.pallas_call(
        project_kernel,
        grid_spec=pltpu.PrefetchScalarGridSpec(
            num_scalar_prefetch=1,
            grid=(blocks,),
            in_specs=[
                rows(BLOCK, DIM),
                whole((DIM, 4 * WIDTH)),
                whole((4, WIDTH)),
                whole((KERNEL, DIM)),
                whole((DIM, WIDTH)),
                whole((taps, WIDTH)),
                whole((1, taps)),
            ],
            out_specs=[
                rows(BLOCK, 4 * WIDTH),
                rows(BLOCK, DIM),
                rows(BLOCK, WIDTH),
                rows(BLOCK, TAPS),
                rows(BLOCK, WIDTH),
            ],
            scratch_shapes=[
                padded(DIM),
                padded(WIDTH),
            ],
        ),
        out_shape=[
            sds((count, 4 * WIDTH), BF),
            sds((count, DIM), BF),
            sds((count, WIDTH), F32),
            sds((count, TAPS), BF),
            sds((count, WIDTH), BF),
        ],
        compiler_params=params(LIMITS["project"]),
        cost_estimate=cost(17),
        name="project",
    )(bucket, x, in_weight, in_bias, depth_weight, point_weight, kernel_weight, kernel_bias)


def mask_bias(is_short, valid_row):
    column = jnp.transpose(jnp.broadcast_to(valid_row.astype(F32), (SLAB, BLOCK)))
    column = jnp.concatenate([column] * (BLOCK // SLAB), axis=1)
    key_slot = (lax.broadcasted_iota(jnp.int32, (BLOCK, BLOCK), 0) // SHORT) * is_short
    query_slot = (lax.broadcasted_iota(jnp.int32, (BLOCK, BLOCK), 1) // SHORT) * is_short
    return jnp.where((key_slot == query_slot) & (column > 0.0), 0.0, -1e30)


def half_mask(v, h):
    lane = lax.broadcasted_iota(jnp.int32, v.shape, 1)
    keep = lane < HEAD if h % 2 == 0 else lane >= HEAD
    return jnp.where(keep, v, jnp.zeros_like(v))


def attend_kernel(
    bucket, valid, q, k, v, co, x, w_out, b_out, gain, shift,
    mixed, logs, hat, inv, xin, bias, context,
):
    bias[...] = mask_bias(bucket[pl.program_id(0)], valid[...].reshape(1, BLOCK))
    vt = jnp.transpose(v[...])
    logs[...] = jnp.zeros_like(logs)
    for h in range(HEADS):
        lo = (h // 2) * SLAB
        qm = half_mask(q[:, lo : lo + SLAB], h) * jnp.asarray(HEAD**-0.5, BF)
        scores = mm_nt(k[:, lo : lo + SLAB], qm) + bias[...]
        top = jnp.max(scores, axis=0, keepdims=True)
        e = jnp.exp(scores - top)
        total = jnp.sum(e, axis=0, keepdims=True)
        part = mm(vt[h * HEAD : (h + 1) * HEAD], e.astype(BF))
        context[h * HEAD : (h + 1) * HEAD, :] = part / total
        logs[0, h : h + 1, :] = top + jnp.log(total)
    mixed[:, :WIDTH] = jnp.transpose(context[...]).astype(BF)
    mixed[:, WIDTH:] = co[...]
    att = mm(mixed[...], w_out[...]) + b_out[...] + x[...].astype(F32)
    scaled, stat = norm_stats(att)
    hat[...] = scaled
    inv[...] = jnp.broadcast_to(stat, inv.shape)
    xin[...] = (scaled * gain[0:1, :] + shift[0:1, :]).astype(BF)


def attend(bucket, valid, qkvc, conv_out, x, out_weight, out_bias, gain, shift):
    count = qkvc.shape[0]
    blocks = count // BLOCK
    return pl.pallas_call(
        attend_kernel,
        grid_spec=pltpu.PrefetchScalarGridSpec(
            num_scalar_prefetch=1,
            grid=(blocks,),
            in_specs=[
                pl.BlockSpec((1, 1, BLOCK), lambda i, *_: (i, 0, 0)),
                rows(BLOCK, WIDTH, 0),
                rows(BLOCK, WIDTH, 1),
                rows(BLOCK, WIDTH, 2),
                rows(BLOCK, WIDTH),
                rows(BLOCK, DIM),
                whole((DIM, DIM)),
                whole((1, DIM)),
                whole((2, DIM)),
                whole((2, DIM)),
            ],
            out_specs=[
                rows(BLOCK, DIM),
                pl.BlockSpec((1, 8, BLOCK), lambda i, *_: (i, 0, 0)),
                rows(BLOCK, DIM),
                rows(BLOCK, SLAB),
                rows(BLOCK, DIM),
            ],
            scratch_shapes=[
                pltpu.VMEM((BLOCK, BLOCK), F32),
                pltpu.VMEM((WIDTH, BLOCK), F32),
            ],
        ),
        out_shape=[
            sds((count, DIM), BF),
            sds((blocks, 8, BLOCK), F32),
            sds((count, DIM), F32),
            sds((count, SLAB), F32),
            sds((count, DIM), BF),
        ],
        compiler_params=params(LIMITS["attend"]),
        cost_estimate=cost(14),
        name="attend",
    )(bucket, valid, qkvc, qkvc, qkvc, conv_out, x, out_weight, out_bias, gain, shift)


PARTS = 4


def unpack_weights(packs, w1, w2, bias_blocks, sems, g, shard, per):
    copies = []
    for k, pack in enumerate(packs):
        at = pl.ds(k * per, per)
        for n, (lo, size, dst) in enumerate(
            ((0, shard, w1), (shard, shard, w2), (2 * shard, 16, bias_blocks))
        ):
            copies.append(
                pltpu.make_async_copy(
                    pack.at[:, pl.ds(lo, size), :], dst.at[g, at], sems.at[g, k, n]
                )
            )
    return copies


def middle_kernel(
    group, *refs, shard, size
):
    hidden = shard * size
    packs, refs = refs[: 2 * PARTS], refs[2 * PARTS :]
    (
        hat1, inv1, xin, mixed, grad, w_out, gain, shift, b2,
        output, d_att, d_mixed, dback, act_a, dpre_a, sums, sums_a, grads_b, out_grad,
        ffn_out, d_summed, slope, datt_low, bias_sum, out_acc, w1s, w2s, blocks_s, b1s, sems,
        act_all, dpre_all, xin_all, dback_all, sums_b,
    ) = refs
    tile = xin.shape[0]
    here = pl.ds(pl.multiple_of(pl.program_id(0) * tile, tile), tile)
    act_b, dpre_b = act_all.at[here], dpre_all.at[here]
    own = pl.multiple_of(group[0] * WIDTH, SLAB)
    other = pl.multiple_of((1 - group[0]) * WIDTH, SLAB)
    part = 512
    step = pl.program_id(0)
    copies = [
        unpack_weights(
            packs[g * PARTS : (g + 1) * PARTS], w1s, w2s, blocks_s, sems, g, shard, size // PARTS
        )
        for g in range(2)
    ]

    @pl.when(step == 0)
    def _():
        for c in copies[0] + copies[1]:
            c.start()

    @pl.when(step == 0)
    def _():
        sums[...] = jnp.zeros_like(sums)
        bias_sum[...] = jnp.zeros_like(bias_sum)
        out_acc[...] = jnp.zeros_like(out_acc)

    def weights(g):
        return (
            w1s.at[g].reshape(hidden, WIDTH),
            w2s.at[g].reshape(hidden, WIDTH),
            b1s.at[g],
        )

    for g, base, act, at in ((0, own, act_a, 0), (1, other, act_b, hidden)):

        @pl.when(step == 0)
        def _():
            for c in copies[g]:
                c.wait()
            for r in range(size):
                row = blocks_s[g, r].astype(F32)[0:1, :shard]
                b1s[g, 0:1, r * shard : (r + 1) * shard] = row

        w1, w2, b1 = weights(g)
        xg = xin[:, pl.ds(base, WIDTH)]
        for lo in range(0, hidden, part):
            pre = mm_nt(xg, w1[lo : lo + part, :]) + b1[0:1, lo : lo + part]
            cdf, bell = normal_cdf(pre)
            act[:, lo : lo + part] = (pre * cdf).astype(BF)
            slope[:, at + lo : at + lo + part] = (cdf + pre * bell).astype(BF)
        ffn_out[:, pl.ds(base, WIDTH)] = mm(act[...], w2[...])
    result = (ffn_out[...] + b2[...]).astype(BF).astype(F32)
    hat2, inv2 = norm_stats(result + (hat1[...] * gain[0:1, :] + shift[0:1, :]))
    output[...] = (hat2 * gain[1:2, :] + shift[1:2, :]).astype(BF)
    dy = grad[...].astype(F32)
    sums[1:2, :] += col_sum(dy * hat2)
    sums[3:4, :] += col_sum(dy)
    ds = norm_back(dy * gain[1:2, :], hat2, inv2)
    d_summed[...] = ds
    low = ds.astype(BF)
    dback[...] = low
    xin_all[here, :] = xin[:, pl.ds(other, WIDTH)]
    dback_all[here, :] = dback[:, pl.ds(other, WIDTH)]
    sums[5:6, :] += col_sum(low.astype(F32))
    for g, base, dpre, at in ((0, own, dpre_a, 0), (1, other, dpre_b, hidden)):
        w1, w2, b1 = weights(g)
        dg = dback[:, pl.ds(base, WIDTH)]
        for lo in range(0, hidden, part):
            dp = mm_nt(dg, w2[lo : lo + part, :]) * slope[:, at + lo : at + lo + part].astype(F32)
            bias_sum[g : g + 1, lo : lo + part] += col_sum(dp)
            dpre[:, lo : lo + part] = dp.astype(BF)
        ffn_out[:, pl.ds(base, WIDTH)] = mm(dpre[...], w1[...])
    dn = d_summed[...] + ffn_out[...].astype(BF).astype(F32)
    hat = hat1[...]
    sums[0:1, :] += col_sum(dn * hat)
    sums[2:3, :] += col_sum(dn)
    da = norm_back(dn * gain[0:1, :], hat, inv1[:, 0:1])
    d_att[...] = da
    sums[4:5, :] += col_sum(da)
    datt_low[...] = da.astype(BF)
    d_mixed[...] = mm_nt(datt_low[...], w_out[...]).astype(BF)
    out_acc[...] += mm_tn(mixed[...], datt_low[...])

    @pl.when(step == pl.num_programs(0) - 1)
    def _():
        out_grad[...] = out_acc[...].astype(BF)
        for g, dst in ((0, sums_a), (1, sums_b)):
            dst[...] = jnp.zeros_like(dst)
            for r in range(size):
                dst[r, 0:1, 0:shard] = bias_sum[g : g + 1, r * shard : (r + 1) * shard]
        quarter, per = hidden // PARTS, size // PARTS
        for k in range(PARTS):
            lanes = slice(k * quarter, (k + 1) * quarter)
            write_pack(
                dpre_all[:, lanes], act_all[:, lanes], xin_all[...], dback_all[...],
                sums_b, grads_b, k * per, per, shard,
            )


def middle(group, packs, shard, size, hat, inv, xin, mixed, grad, out_weight, gain, shift, b2):
    count = xin.shape[0]
    hidden = shard * size
    tile = BLOCK // 2
    pack_shape = (size, 2 * shard + 16, WIDTH)
    sum_shape = (size, 8, WIDTH)
    return pl.pallas_call(
        functools.partial(middle_kernel, shard=shard, size=size),
        grid_spec=pltpu.PrefetchScalarGridSpec(
            num_scalar_prefetch=1,
            grid=(count // tile,),
            in_specs=[pl.BlockSpec(memory_space=pl.ANY)] * (2 * PARTS)
            + [
                rows(tile, DIM),
                rows(tile, SLAB),
                rows(tile, DIM),
                rows(tile, DIM),
                rows(tile, DIM),
                whole((DIM, DIM)),
                whole((2, DIM)),
                whole((2, DIM)),
                whole((1, DIM)),
            ],
            out_specs=[
                rows(tile, DIM),
                rows(tile, DIM),
                rows(tile, DIM),
                rows(tile, DIM),
                rows(tile, hidden),
                rows(tile, hidden),
                whole((8, DIM)),
                whole(sum_shape),
                whole(pack_shape),
                whole((DIM, DIM)),
            ],
            scratch_shapes=[
                pltpu.VMEM((tile, DIM), F32),
                pltpu.VMEM((tile, DIM), F32),
                pltpu.VMEM((tile, 2 * hidden), BF),
                pltpu.VMEM((tile, DIM), BF),
                pltpu.VMEM((8, hidden), F32),
                pltpu.VMEM((DIM, DIM), F32),
                pltpu.VMEM((2, size, shard, WIDTH), BF),
                pltpu.VMEM((2, size, shard, WIDTH), BF),
                pltpu.VMEM((2, size, 16, WIDTH), BF),
                pltpu.VMEM((2, 8, hidden), F32),
                pltpu.SemaphoreType.DMA((2, PARTS, 3)),
                pltpu.VMEM((count, hidden), BF),
                pltpu.VMEM((count, hidden), BF),
                pltpu.VMEM((count, WIDTH), BF),
                pltpu.VMEM((count, WIDTH), BF),
                pltpu.VMEM(sum_shape, F32),
            ],
        ),
        out_shape=[
            sds((count, DIM), BF),
            sds((count, DIM), F32),
            sds((count, DIM), BF),
            sds((count, DIM), BF),
            sds((count, hidden), BF),
            sds((count, hidden), BF),
            sds((8, DIM), F32),
            sds(sum_shape, F32),
            sds(pack_shape, BF),
            sds((DIM, DIM), BF),
        ],
        compiler_params=params(LIMITS["middle"]),
        cost_estimate=cost(38),
        name="middle",
    )(group, *packs, hat, inv, xin, mixed, grad, out_weight, gain, shift, b2)


def write_pack(dpre, act, xin, dback, sums, out, first_block, per, shard):
    first = mm_tn(dpre, xin).astype(BF)
    second = mm_tn(act, dback).astype(BF)
    for z in range(per):
        out[first_block + z, 0:shard, :] = first[z * shard : (z + 1) * shard]
        out[first_block + z, shard : 2 * shard, :] = second[z * shard : (z + 1) * shard]
        row = jnp.concatenate([sums[first_block + z], jnp.zeros((8, WIDTH), F32)], axis=0)
        out[first_block + z, 2 * shard :, :] = row.astype(BF)


def ffn_grad_kernel(group, dpre, act, xin, dback, sums, out, *, shard):
    write_pack(
        dpre[...], act[...], xin[...], dback[...], sums, out, 0, out.shape[0], shard
    )


def ffn_grad(group, dpre, act, xin, dback, sums, shard, size):
    count, hidden = dpre.shape
    tile = hidden // PARTS
    per = size // PARTS
    lanes = pl.BlockSpec((count, tile), lambda i, g: (0, i))
    side = pl.BlockSpec((count, WIDTH), lambda i, g: (0, g[0]))
    return pl.pallas_call(
        functools.partial(ffn_grad_kernel, shard=shard),
        grid_spec=pltpu.PrefetchScalarGridSpec(
            num_scalar_prefetch=1,
            grid=(PARTS,),
            in_specs=[
                lanes, lanes, side, side, pl.BlockSpec((per, 8, WIDTH), lambda i, g: (i, 0, 0)),
            ],
            out_specs=pl.BlockSpec((per, 2 * shard + 16, WIDTH), lambda i, g: (i, 0, 0)),
        ),
        out_shape=sds((size, 2 * shard + 16, WIDTH), BF),
        compiler_params=params(LIMITS["ffn_grad"]),
        cost_estimate=cost(7),
        name="ffn_grad",
    )(group, dpre, act, xin, dback, sums)


def repack(packs, size, shard):
    old = (packs.shape[1] - 16) // 2
    first = packs[:, :old].reshape(size, shard, WIDTH)
    second = packs[:, old : 2 * old].reshape(size, shard, WIDTH)
    bias = packs[:, 2 * old, :old].reshape(size, 1, shard)
    bias = jnp.pad(bias, ((0, 0), (0, 15), (0, WIDTH - shard)))
    return jnp.concatenate([first, second, bias], axis=1)


def attend_back_kernel(
    info, valid, q, k, v, dctx, logs, x, out_part, dq, dkv, sums, keep, send, bias, dqt, acc
):
    step = pl.program_id(0)

    @pl.when(step == 0)
    def _():
        sums[...] = jnp.zeros_like(sums)
        acc[...] = jnp.zeros_like(acc)

    bias[...] = mask_bias(info[1 + step], valid[...].reshape(1, BLOCK))
    scale = jnp.asarray(HEAD**-0.5, BF)
    kt = jnp.transpose(k[...] * scale)
    for pair in range(HEADS // 2):
        lo = pair * SLAB
        kp = k[:, lo : lo + SLAB]
        vp = v[:, lo : lo + SLAB]
        dk = dv = None
        for h in (2 * pair, 2 * pair + 1):
            qm = half_mask(q[:, lo : lo + SLAB], h) * scale
            cm = half_mask(dctx[:, lo : lo + SLAB], h)
            probs = jnp.exp(mm_nt(kp, qm) + bias[...] - logs[0, h : h + 1, :])
            d_probs = mm_nt(vp, cm)
            delta = col_sum(probs * d_probs)
            d_scores = (probs * (d_probs - delta)).astype(BF)
            probs = probs.astype(BF)
            dv = mm(probs, cm) if dv is None else dv + mm(probs, cm)
            dk = mm(d_scores, qm) if dk is None else dk + mm(d_scores, qm)
            dqt[h * HEAD : (h + 1) * HEAD, :] = mm(kt[h * HEAD : (h + 1) * HEAD], d_scores)
        dkv[:, lo : lo + SLAB] = dk.astype(BF)
        dkv[:, WIDTH + lo : WIDTH + lo + SLAB] = dv.astype(BF)
        sums[0:1, lo : lo + SLAB] += col_sum(dv)
    dq[...] = jnp.transpose(dqt[...])
    acc[...] += mm_tn(x[...], dkv[...])

    @pl.when((step == pl.num_programs(0) - 1) & (info[0] == 0))
    def _():
        keep[...] = out_part[...]
        send[...] = acc[...].astype(BF)

    @pl.when((step == pl.num_programs(0) - 1) & (info[0] != 0))
    def _():
        keep[...] = acc[...].astype(BF)
        send[...] = out_part[...]


def attend_back(info, valid, qkvc, d_mixed, logs, x, out_part):
    count = qkvc.shape[0]
    blocks = count // BLOCK
    return pl.pallas_call(
        attend_back_kernel,
        grid_spec=pltpu.PrefetchScalarGridSpec(
            num_scalar_prefetch=1,
            grid=(blocks,),
            in_specs=[
                pl.BlockSpec((1, 1, BLOCK), lambda i, *_: (i, 0, 0)),
                rows(BLOCK, WIDTH, 0),
                rows(BLOCK, WIDTH, 1),
                rows(BLOCK, WIDTH, 2),
                rows(BLOCK, WIDTH, 0),
                pl.BlockSpec((1, 8, BLOCK), lambda i, *_: (i, 0, 0)),
                rows(BLOCK, DIM),
                whole((DIM, DIM)),
            ],
            out_specs=[
                rows(BLOCK, WIDTH),
                rows(BLOCK, DIM),
                whole((8, WIDTH)),
                whole((DIM, DIM)),
                whole((DIM, DIM)),
            ],
            scratch_shapes=[
                pltpu.VMEM((BLOCK, BLOCK), F32),
                pltpu.VMEM((WIDTH, BLOCK), F32),
                pltpu.VMEM((DIM, DIM), F32),
            ],
        ),
        out_shape=[
            sds((count, WIDTH), F32),
            sds((count, DIM), BF),
            sds((8, WIDTH), F32),
            sds((DIM, DIM), BF),
            sds((DIM, DIM), BF),
        ],
        compiler_params=params(LIMITS["attend_back"]),
        cost_estimate=cost(16),
        name="attend_back",
    )(info, valid, qkvc, qkvc, qkvc, d_mixed, logs, x, out_part)


POINT_ROW = DIM
SMALL_ROW = DIM + WIDTH
LATE_ROWS = DIM + WIDTH + 128
NORM_ROW = SMALL_ROW + 64
TAP_ROW = SMALL_ROW + 72


def conv_back_kernel(
    info, q, cv, dconv, kc, ks, dq, x, dep, kw, pw, sums_mid, sums_v, dqc, dkc, keep, send,
    cvpad, dcpad, kspad, xpad, dk_slab, dlog, qc_acc, pt_acc, kw_acc, kb_acc, dw_acc, sums, flat
):
    step = pl.program_id(0)
    taps = HEADS * KERNEL

    @pl.when(step == 0)
    def _():
        for ref in (qc_acc, pt_acc, kw_acc, kb_acc, dw_acc, sums):
            ref[...] = jnp.zeros_like(ref)

    joined = jnp.where(info[1 + step] == 0, 1.0, 0.0).astype(F32)
    dc = dconv[...].astype(F32)
    fill_padded(cvpad, cv[...].astype(F32), joined)
    fill_padded(dcpad, dc, joined)
    fill_padded(kspad, ks[...].astype(F32), joined)
    fill_padded(xpad, x[...].astype(F32), joined)
    spread = head_spread()
    total = None
    for j in range(KERNEL):
        product = jnp.concatenate(add_taps(None, dc, cvpad, j - EDGE), axis=1)
        part = mm_nt(product.astype(BF), spread)
        dk_slab[:, j * SLAB : (j + 1) * SLAB] = part
        part = part * ks[:, j * SLAB : (j + 1) * SLAB].astype(F32)
        total = part if total is None else total + part
    for j in range(KERNEL):
        lanes = slice(j * SLAB, (j + 1) * SLAB)
        grad = ks[:, lanes].astype(F32) * (dk_slab[:, lanes] - total)
        kb_acc[0:1, lanes] += col_sum(grad)
        dlog[:, lanes] = grad.astype(BF)
    acc = None
    for j in range(KERNEL):
        weight = mm(moved(kspad, EDGE - j, j).astype(BF), spread)
        acc = add_taps(acc, weight, dcpad, EDGE - j)
    acc = jnp.concatenate(acc, axis=1)
    dqc[:, WIDTH:] = acc.astype(BF)
    sums[1:2, :] += col_sum(acc)
    select = slab_select(taps)
    compact = mm_nt(dlog[...], select.astype(BF)).astype(BF)
    qf = q[...].astype(F32)
    key_conv = kc[...]
    conv_in = (key_conv * qf).astype(BF)
    kw_acc[0:taps, :] += mm_tn(compact, conv_in)
    d_conv_in = mm(compact, kw[...])
    d_key = d_conv_in * qf
    sums[2:3, :] += col_sum(d_key)
    dkc[...] = d_key.astype(BF)
    dq_all = dq[...] + d_conv_in * key_conv
    sums[0:1, :] += col_sum(dq_all)
    dqc[:, :WIDTH] = dq_all.astype(BF)
    qc_acc[...] += mm_tn(x[...], dqc[...])
    pt_acc[...] += mm_tn(dep[...], dkc[...])
    d_depth = mm_nt(dkc[...], pw[...])
    for c in range(DIM // SLAB):
        lanes = slice(c * SLAB, (c + 1) * SLAB)
        here = d_depth[:, lanes]
        for j in range(KERNEL):
            dw_acc[j : j + 1, lanes] += col_sum(moved(xpad, j - EDGE, c) * here)

    @pl.when(step == pl.num_programs(0) - 1)
    def _():
        flat[0:DIM, :] = qc_acc[...].astype(BF)
        flat[POINT_ROW:SMALL_ROW, 0:WIDTH] = pt_acc[0:WIDTH, :].astype(BF)
        flat[POINT_ROW:SMALL_ROW, WIDTH:] = pt_acc[WIDTH:, :].astype(BF)
        flat[SMALL_ROW : SMALL_ROW + 64, 0:WIDTH] = kw_acc[...].astype(BF)
        kb = lax.dot_general(
            kb_acc[...],
            select,
            (((1,), (1,)), ((), ())),
            precision=lax.Precision.HIGHEST,
            preferred_element_type=F32,
        )
        blank = jnp.zeros((4, WIDTH), F32)
        rows_of = jnp.concatenate([sums[0:1], sums_v[0:1], sums[1:3], blank], axis=0)
        kb = jnp.concatenate([kb, jnp.zeros((8, WIDTH - taps), F32)], axis=1)
        flat[SMALL_ROW : SMALL_ROW + 16, WIDTH:] = jnp.concatenate([rows_of, kb], axis=0).astype(BF)
        flat[SMALL_ROW + 16 : NORM_ROW, WIDTH:] = jnp.zeros((48, WIDTH), BF)
        flat[NORM_ROW : NORM_ROW + 32, :] = jnp.concatenate(
            [sums_mid[...], dw_acc[...], jnp.zeros((8, DIM), F32)], axis=0
        ).astype(BF)
        flat[NORM_ROW + 32 :, :] = jnp.zeros((32, DIM), BF)
        half = LATE_ROWS // 2
        core = info[0]
        keep[...] = flat[pl.ds(pl.multiple_of(core * half, 16), half), :]
        send[...] = flat[pl.ds(pl.multiple_of((1 - core) * half, 16), half), :]


def conv_back(info, qkvc, d_mixed, kc, ks, dq, x, dep, kernel_weight, point_weight, sums_mid, sums_v):
    count = qkvc.shape[0]
    blocks = count // BLOCK
    taps = HEADS * KERNEL
    half = LATE_ROWS // 2
    return pl.pallas_call(
        conv_back_kernel,
        grid_spec=pltpu.PrefetchScalarGridSpec(
            num_scalar_prefetch=1,
            grid=(blocks,),
            in_specs=[
                rows(BLOCK, WIDTH, 0),
                rows(BLOCK, WIDTH, 3),
                rows(BLOCK, WIDTH, 1),
                rows(BLOCK, WIDTH),
                rows(BLOCK, TAPS),
                rows(BLOCK, WIDTH),
                rows(BLOCK, DIM),
                rows(BLOCK, DIM),
                whole((taps, WIDTH)),
                whole((DIM, WIDTH)),
                whole((8, DIM)),
                whole((8, WIDTH)),
            ],
            out_specs=[
                rows(BLOCK, DIM),
                rows(BLOCK, WIDTH),
                whole((half, DIM)),
                whole((half, DIM)),
            ],
            scratch_shapes=[
                padded(WIDTH),
                padded(WIDTH),
                padded(TAPS),
                padded(DIM),
                pltpu.VMEM((BLOCK, TAPS), F32),
                pltpu.VMEM((BLOCK, TAPS), BF),
                pltpu.VMEM((DIM, DIM), F32),
                pltpu.VMEM((DIM, WIDTH), F32),
                pltpu.VMEM((64, WIDTH), F32),
                pltpu.VMEM((8, TAPS), F32),
                pltpu.VMEM((16, DIM), F32),
                pltpu.VMEM((8, WIDTH), F32),
                pltpu.VMEM((LATE_ROWS, DIM), BF),
            ],
        ),
        out_shape=[
            sds((count, DIM), BF),
            sds((count, WIDTH), BF),
            sds((half, DIM), BF),
            sds((half, DIM), BF),
        ],
        compiler_params=params(LIMITS["conv_back"]),
        cost_estimate=cost(22),
        name="conv_back",
    )(info, qkvc, qkvc, d_mixed, kc, ks, dq, x, dep, kernel_weight, point_weight, sums_mid, sums_v)


def hidden_kernel(info, dkc, d_att, dqc, dkv, dw, pw, w, *refs, start):
    hidden, ddpad = refs[-2:]
    joined = jnp.where(info[1 + start + pl.program_id(0)] == 0, 1.0, 0.0).astype(F32)
    fill_padded(ddpad, mm_nt(dkc[...], pw[...]), joined)
    hidden[...] = (
        d_att[...]
        + mm_nt(dkv[...], w[:, WIDTH : 3 * WIDTH])
        + mm_nt(dqc[:, :WIDTH], w[:, :WIDTH])
        + mm_nt(dqc[:, WIDTH:], w[:, 3 * WIDTH :])
    )
    for c in range(DIM // SLAB):
        lanes = slice(c * SLAB, (c + 1) * SLAB)
        acc = hidden[:, lanes]
        for j in range(KERNEL):
            acc += moved(ddpad, EDGE - j, c) * dw[j : j + 1, lanes]
        hidden[:, lanes] = acc


def hidden_back(info, dkc, d_att, dqc, dkv, depth_weight, point_weight, in_weight, start, stop, before=None):
    count = d_att.shape[0]

    def part(width):
        return pl.BlockSpec((BLOCK, width), lambda i, *_: (i + start, 0))

    extra = [] if before is None else [before]
    return pl.pallas_call(
        functools.partial(hidden_kernel, start=start),
        grid_spec=pltpu.PrefetchScalarGridSpec(
            num_scalar_prefetch=1,
            grid=(stop - start,),
            in_specs=[
                part(WIDTH),
                part(DIM),
                part(DIM),
                part(DIM),
                whole((KERNEL, DIM)),
                whole((DIM, WIDTH)),
                whole((DIM, 4 * WIDTH)),
            ]
            + [pl.BlockSpec(memory_space=pl.ANY)] * len(extra),
            out_specs=part(DIM),
            scratch_shapes=[padded(DIM)],
        ),
        out_shape=sds((count, DIM), F32),
        input_output_aliases={8: 0} if extra else {},
        compiler_params=params(LIMITS["hidden_back"]),
        cost_estimate=cost(6),
        name="hidden_back",
    )(info, dkc, d_att, dqc, dkv, depth_weight, point_weight, in_weight, *extra)


def load_parts(parts, dst, sems, core, digit):
    count = dst.shape[0]
    copies = []
    per = max(len(parts) // 2, 1)
    size = count // len(parts)
    for n, part in enumerate(parts):
        c, k = n // per, n % per
        row = 0 if len(parts) == 1 else (core ^ c) * (count // 2) + (digit ^ k) * size * (per > 1)
        at = pl.ds(pl.multiple_of(row, 16), size)
        copies.append(pltpu.make_async_copy(part, dst.at[at, :], sems.at[n]))
    for c in copies:
        c.start()
    for c in copies:
        c.wait()


def unpack_early_kernel(info, *refs):
    parts, (in_w, out_w, early, sems) = refs[:-4], refs[-4:]
    step = pl.program_id(0)

    @pl.when(step == 0)
    def _():
        load_parts(parts, early, sems, info[0], info[1])
        out_w[...] = early[0:DIM, :].astype(F32)

    in_w[...] = early[DIM:, pl.ds(pl.multiple_of(step * WIDTH, SLAB), WIDTH)].astype(F32)


def unpack_early(info, parts):
    return pl.pallas_call(
        unpack_early_kernel,
        grid_spec=pltpu.PrefetchScalarGridSpec(
            num_scalar_prefetch=1,
            grid=(2,),
            in_specs=[pl.BlockSpec(memory_space=pl.ANY)] * len(parts),
            out_specs=[
                pl.BlockSpec((DIM, WIDTH), lambda i, *_: (0, 1 + i)),
                whole((DIM, DIM)),
            ],
            scratch_shapes=[
                pltpu.VMEM((2 * DIM, DIM), BF),
                pltpu.SemaphoreType.DMA((len(parts),)),
            ],
        ),
        out_shape=[sds((DIM, 4 * WIDTH), F32), sds((DIM, DIM), F32)],
        compiler_params=params(LIMITS["unpack"]),
        cost_estimate=cost(3),
        name="unpack_early",
    )(info, *parts)


def unpack_late_kernel(info, *refs):
    parts, (_, in_w, in_b, dw, point, kw, kb, out_b, gain, shift, b2, late, sems) = (
        refs[:-13],
        refs[-13:],
    )
    step = pl.program_id(0)
    taps = HEADS * KERNEL

    @pl.when(step == 0)
    def _():
        load_parts(parts, late, sems, info[0], info[1])
        point[0:WIDTH, :] = late[POINT_ROW:SMALL_ROW, 0:WIDTH].astype(F32)
        point[WIDTH:, :] = late[POINT_ROW:SMALL_ROW, WIDTH:].astype(F32)
        kw[...] = late[SMALL_ROW : SMALL_ROW + 64, 0:WIDTH].astype(F32)[0:taps]
        mixed = late[SMALL_ROW : SMALL_ROW + 16, WIDTH:].astype(F32)
        in_b[...] = mixed[0:4]
        kb[...] = mixed[8:9, 0:taps]
        norms = late[NORM_ROW : NORM_ROW + 32, :].astype(F32)
        gain[...] = norms[0:2]
        shift[...] = norms[2:4]
        out_b[...] = norms[4]
        b2[...] = jnp.where(info[0] == 0, norms[5:6, 0:WIDTH], norms[5:6, WIDTH:])
        dw[...] = norms[8 : 8 + KERNEL]

    in_w[...] = late[0:DIM, pl.ds(pl.multiple_of(step * WIDTH, SLAB), WIDTH)].astype(F32)


def unpack_late(info, parts, in_w):
    taps = HEADS * KERNEL
    shapes = [
        (4, WIDTH), (KERNEL, DIM), (DIM, WIDTH), (taps, WIDTH), (1, taps), (DIM,), (2, DIM),
        (2, DIM), (1, WIDTH),
    ]
    return pl.pallas_call(
        unpack_late_kernel,
        grid_spec=pltpu.PrefetchScalarGridSpec(
            num_scalar_prefetch=1,
            grid=(2,),
            in_specs=[pl.BlockSpec(memory_space=pl.ANY)] * (len(parts) + 1),
            out_specs=[pl.BlockSpec((DIM, WIDTH), lambda i, *_: (0, 3 * i))]
            + [whole(v) for v in shapes],
            scratch_shapes=[
                pltpu.VMEM((LATE_ROWS, DIM), BF),
                pltpu.SemaphoreType.DMA((len(parts),)),
            ],
        ),
        out_shape=[sds((DIM, 4 * WIDTH), F32)] + [sds(v, F32) for v in shapes],
        input_output_aliases={1 + len(parts): 0},
        compiler_params=params(LIMITS["unpack"]),
        cost_estimate=cost(3),
        name="unpack_late",
    )(info, *parts, in_w)


def digit_groups(size):
    groups, shift = [], 0
    while (1 << shift) < size:
        bits = 2 if (4 << shift) <= size else 1
        groups.append((shift, 1 << bits))
        shift += bits
    return groups


def partner(value, size, distance):
    return lax.ppermute(value, "wide", [(i, i ^ distance) for i in range(size)])


def swap_core(value):
    return lax.ppermute(value, "grp", [(0, 1), (1, 0)])


def fence(*values):
    return lax.optimization_barrier(values)


def add_up(values, dtype=BF):
    total = values[0].astype(F32)
    for v in values[1:]:
        total = total + v.astype(F32)
    return total.astype(dtype)


def gather_relative(block, size):
    buf = block[None]
    for shift, count in reversed(digit_groups(size)):
        parts = [buf] + [partner(buf, size, k << shift) for k in range(1, count)]
        buf = jnp.concatenate(parts, axis=0)
    return buf


def scatter_relative(blocks, size):
    buf = blocks
    for shift, count in digit_groups(size):
        parts = buf.reshape((count, buf.shape[0] // count) + buf.shape[1:])
        buf = add_up([parts[0]] + [partner(parts[k], size, k << shift) for k in range(1, count)])
    return buf[0].astype(F32)


def take(array, index):
    return lax.dynamic_index_in_dim(array, index, 0, keepdims=False)


class Sum:
    def __init__(self, size, half, direct=False):
        self.size, self.value, self.direct = size, half, direct

    def digit(self, group):
        return (lax.axis_index("wide") >> group[0]) & (group[1] - 1)

    def swap(self, group, blocks):
        shift, count = group
        mask = (count - 1) << shift
        teams = [
            [i + (d << shift) for d in range(count)] for i in range(self.size) if not i & mask
        ]
        return [
            lax.all_to_all(
                blocks, "wide", split_axis=0, concat_axis=0, axis_index_groups=teams, tiled=True
            )
        ]

    def send(self, group):
        shift, count = group
        blocks = self.value.reshape(count, self.value.shape[0] // count, DIM)
        if not self.direct:
            self.parts = self.swap(group, blocks)
            return
        digit = self.digit(group)
        self.parts = [take(blocks, digit)] + [
            partner(take(blocks, digit ^ k), self.size, k << shift) for k in range(1, count)
        ]

    def reduce(self):
        if self.direct:
            self.value = add_up(self.parts)
        else:
            self.value = jnp.sum(self.parts[0].astype(F32), axis=0).astype(BF)

    def spread(self, group):
        shift, count = group
        if not self.direct:
            blocks = jnp.broadcast_to(self.value[None], (count,) + self.value.shape)
            self.parts = self.swap(group, blocks)
            return
        self.parts = [self.value] + [
            partner(self.value, self.size, k << shift) for k in range(1, count)
        ]

    def join(self, group):
        if not self.direct:
            self.value = self.parts[0].reshape(-1, DIM)
            return
        digit = self.digit(group)
        stacked = jnp.stack(self.parts)
        self.value = jnp.concatenate([take(stacked, digit ^ d) for d in range(group[1])], axis=0)


def sum_everywhere(keep, send, size):
    core = lax.axis_index("grp")
    total = Sum(size, add_up([keep, swap_core(send)]))
    groups = digit_groups(size)
    for group in groups:
        total.send(group)
        total.reduce()
    for group in reversed(groups):
        total.spread(group)
        total.join(group)
    halves = jnp.stack([total.value, swap_core(total.value)])
    return jnp.concatenate([take(halves, core), take(halves, 1 - core)], axis=0)


def body(
    size,
    hidden_in,
    valid_mask,
    bucket,
    in_weight,
    in_bias,
    depth_weight,
    point_weight,
    kernel_weight,
    kernel_bias,
    out_weight,
    out_bias,
    norm_gain,
    norm_bias,
    ffn_in,
    ffn_in_bias,
    ffn_out,
    ffn_out_bias,
    out_grad,
):
    count = hidden_in.shape[0]
    blocks = count // BLOCK
    shard = ffn_in.shape[1]
    hidden = shard * size
    core = lax.axis_index("grp").astype(jnp.int32)
    group = jnp.reshape(core, (1,))
    info = jnp.concatenate([group, bucket])
    valid = valid_mask.reshape(blocks, 1, BLOCK)
    kernel_weight = kernel_weight.T
    groups = digit_groups(size)
    staged = len(groups) == 2 and groups[0][1] == groups[1][1] == PARTS and shard % 16 == 0

    bias_rows = jnp.pad(ffn_in_bias, ((0, 15), (0, WIDTH - shard)))
    pack = jnp.concatenate([ffn_in[0], ffn_out[0], bias_rows], axis=0)[None]
    other_bias = swap_core(ffn_out_bias)
    b2 = jnp.concatenate([ffn_out_bias, other_bias], axis=1)
    b2 = jnp.where(core == 0, b2, jnp.concatenate([other_bias, ffn_out_bias], axis=1))

    if staged:
        got = [partner(pack, size, k << groups[1][0]) for k in range(1, PARTS)]
    qkvc, dep, kc, ks, conv_out = project(
        bucket, hidden_in, in_weight, in_bias, depth_weight, point_weight, kernel_weight,
        kernel_bias[None],
    )
    if staged:
        *got, conv_out = fence(*got, conv_out)
        near = jnp.concatenate([pack] + got, axis=0)
        own = [near] + [partner(near, size, k) for k in range(1, PARTS)]
        near_other = swap_core(near)
        near_other, conv_out = fence(near_other, conv_out)
    mixed, logs, hat, inv, xin = attend(
        bucket, valid, qkvc, conv_out, hidden_in, out_weight, out_bias[None], norm_gain, norm_bias
    )
    if staged:
        *own, xin = fence(*own, xin)
        packs = own + [near_other] + [swap_core(v) for v in own[1:]]
    else:
        gathered = gather_relative(pack[0], size)
        packs = [
            pack[None]
            for v in (gathered, swap_core(gathered))
            for pack in repack(v, PARTS, hidden // PARTS)
        ]
    form = (shard, size) if staged else (hidden // PARTS, PARTS)
    (
        output, d_att, d_mixed, dback, act_a, dpre_a, sums, sums_a, grads_b, out_part,
    ) = middle(
        group, packs, *form, hat, inv, xin, mixed, out_grad, out_weight, norm_gain, norm_bias, b2
    )
    from_core = swap_core(grads_b)
    grads_a = ffn_grad(group, dpre_a, act_a, xin, dback, sums_a, *form)
    grads_a, from_core, d_mixed = fence(grads_a, from_core, d_mixed)

    if not staged:
        ffn_grads = scatter_relative(
            repack(add_up([grads_a, from_core]), size, shard), size
        )
    else:
        per = size // PARTS
        parts = [
            add_up([grads_a[k * per : (k + 1) * per], from_core[k * per : (k + 1) * per]])
            for k in range(PARTS)
        ]
        xy, z = groups
        *parts, d_mixed = fence(*parts, d_mixed)
        from_x, from_y = partner(parts[1], size, 1), partner(parts[2], size, 2)
    dq, dkv, sums_v, early_keep, early_send = attend_back(
        info, valid, qkvc, d_mixed, logs, hidden_in, out_part
    )
    if staged:
        from_x, from_y, early_send = fence(from_x, from_y, early_send)
        early = Sum(size, add_up([early_keep, swap_core(early_send)]), direct=True)
        early.value, dq = fence(early.value, dq)
        from_xy = partner(parts[3], size, 3)
        early.send(xy)
    dqc, dkc, late_keep, late_send = conv_back(
        info, qkvc, d_mixed, kc, ks, dq, hidden_in, dep, kernel_weight, point_weight, sums, sums_v
    )
    if staged:
        *early.parts, from_xy, late_send, dkc = fence(*early.parts, from_xy, late_send, dkc)
        late_got = swap_core(late_send)
        parts = [add_up([v[k] for v in (parts[0], from_x, from_y, from_xy)]) for k in range(PARTS)]
        early.reduce()
        late = Sum(size, add_up([late_keep, late_got]))
        early.value, late.value, dkc = fence(early.value, late.value, dkc)
        late.send(xy)
        early.send(z)
    hidden_grad = hidden_back(
        info, dkc, d_att, dqc, dkv, depth_weight, point_weight, in_weight, 0, blocks
    )
    info = jnp.stack([core, lax.axis_index("wide").astype(jnp.int32) & (PARTS - 1)])
    if staged:
        late.parts[0], *early.parts, hidden_grad = fence(late.parts[0], *early.parts, hidden_grad)
        late.reduce()
        early.reduce()
        late.value, early.value = fence(late.value, early.value)
        late.send(z)
        early.spread(z)
        late.parts[0], *early.parts = fence(late.parts[0], *early.parts)
        late.reduce()
        early.join(z)
        early.value, late.value, *parts = fence(early.value, late.value, *parts)
        late.spread(z)
        early.spread(xy)
        from_z = [partner(parts[k], size, k << z[0]) for k in (1, 2)]
        late.parts[0], *rest = fence(late.parts[0], *early.parts, *from_z, parts[3])
        early.parts, from_z, last = rest[:PARTS], rest[PARTS : PARTS + 2], rest[-1]
        late.join(z)
        late.spread(xy)
        early_all = early.parts + [swap_core(v) for v in early.parts]
        from_z.append(partner(last, size, 3 << z[0]))
        in_weight_grad, out_weight_grad = unpack_early(info, early_all)
        late.parts[0], from_z[2], in_weight_grad = fence(late.parts[0], from_z[2], in_weight_grad)
        late.join(xy)
        late_all = [late.value, swap_core(late.value)]
        ffn_grads = add_up([parts[0]] + from_z, F32)
        late_all[1], ffn_grads = fence(late_all[1], ffn_grads)
    else:
        early_all = [sum_everywhere(early_keep, early_send, size)]
        late_all = [sum_everywhere(late_keep, late_send, size)]
        in_weight_grad, out_weight_grad = unpack_early(info, early_all)
    (
        in_weight_grad, in_bias_grad, depth_weight_grad, point_weight_grad, kernel_weight_grad,
        kernel_bias_grad, out_bias_grad, gain_grad, shift_grad, ffn_out_bias_grad,
    ) = unpack_late(info, late_all, in_weight_grad)
    return (
        output,
        hidden_grad,
        in_weight_grad,
        in_bias_grad,
        depth_weight_grad,
        point_weight_grad,
        kernel_weight_grad.T,
        kernel_bias_grad[0],
        out_weight_grad,
        out_bias_grad,
        gain_grad,
        shift_grad,
        ffn_grads[None, :shard],
        ffn_grads[None, 2 * shard, :shard],
        ffn_grads[None, shard : 2 * shard],
        ffn_out_bias_grad,
    )


def solution(mesh):
    both = ("grp", "wide")
    return jax.shard_map(
        functools.partial(body, mesh.shape["wide"]),
        mesh=mesh,
        in_specs=(
            P(both, None),
            P(both),
            P(both),
            P(),
            P(),
            P(),
            P(),
            P(),
            P(),
            P(),
            P(),
            P(),
            P(),
            P("grp", "wide", None),
            P("grp", "wide"),
            P("grp", "wide", None),
            P("grp", None),
            P(both, None),
        ),
        out_specs=(
            P(both, None),
            P(both, None),
            P(),
            P(),
            P(),
            P(),
            P(),
            P(),
            P(),
            P(),
            P(),
            P(),
            P("grp", "wide", None),
            P("grp", "wide"),
            P("grp", "wide", None),
            P("grp", None),
        ),
        check_vma=False,
    )
```

```python
import functools
import jax
import jax.numpy as jnp
from jax import lax
from jax.experimental import pallas as pl
from jax.experimental.pallas import tpu as pltpu
from jax.sharding import PartitionSpec as P

HEADS = 6
HEAD = 64
KERNEL = 9
EDGE = 4
BLOCK = 512
SHORT = 128
CHUNKS = BLOCK // SHORT
WIDTH = HEADS * HEAD
DIM = 2 * WIDTH
SLAB = 128
TAPS = KERNEL * SLAB
HALO = 8
PADDED = SHORT + 2 * HALO
EPSILON = 1e-12
BF = jnp.bfloat16
F32 = jnp.float32
LIMITS = dict(
    project=60,
    attend=24,
    middle=60,
    ffn_grad=60,
    attend_back=60,
    conv_back=60,
    hidden_back=60,
    unpack=60,
)


def mm(a, b):
    return lax.dot_general(a, b, (((1,), (0,)), ((), ())), preferred_element_type=F32)


def mm_nt(a, b):
    return lax.dot_general(a, b, (((1,), (1,)), ((), ())), preferred_element_type=F32)


def mm_tn(a, b):
    return lax.dot_general(a, b, (((0,), (0,)), ((), ())), preferred_element_type=F32)


def col_sum(v):
    return jnp.sum(v, axis=0, keepdims=True)


def params(mebibytes):
    return pltpu.CompilerParams(vmem_limit_bytes=mebibytes * 1024 * 1024)


def whole(shape):
    return pl.BlockSpec(shape, lambda *_: (0,) * len(shape))


def rows(tile, width, lane=0):
    return pl.BlockSpec((tile, width), lambda i, *_: (i, lane))


def cost(micros):
    return pl.CostEstimate(flops=int(micros * 1e7), bytes_accessed=int(micros * 3e4), transcendentals=0)


def sds(shape, dtype):
    return jax.ShapeDtypeStruct(shape, dtype)


def fill_padded(pad_ref, values, joined):
    zero = jnp.zeros((HALO, SLAB), F32)
    for c in range(values.shape[1] // SLAB):
        lanes = slice(c * SLAB, (c + 1) * SLAB)
        for s in range(CHUNKS):
            lo, hi = s * SHORT, (s + 1) * SHORT
            pad_ref[c, s, HALO : HALO + SHORT, :] = values[lo:hi, lanes]
            pad_ref[c, s, 0:HALO, :] = values[lo - HALO : lo, lanes] * joined if s else zero
            pad_ref[c, s, HALO + SHORT :, :] = (
                values[hi : hi + HALO, lanes] * joined if s < CHUNKS - 1 else zero
            )


def padded(width):
    return pltpu.VMEM((width // SLAB, CHUNKS, PADDED, SLAB), F32)


def moved(pad_ref, offset, c):
    at = HALO + offset
    return pad_ref[c, :, at : at + SHORT, :].reshape(BLOCK, SLAB)


def add_taps(acc, weight, pad_ref, offset):
    parts = [
        weight[:, c * SLAB : (c + 1) * SLAB] * moved(pad_ref, offset, c)
        for c in range(weight.shape[1] // SLAB)
    ]
    return parts if acc is None else [u + v for u, v in zip(acc, parts)]


def slab_select(rows_of):
    source = lax.broadcasted_iota(jnp.int32, (rows_of, TAPS), 0)
    target = lax.broadcasted_iota(jnp.int32, (rows_of, TAPS), 1)
    head = target % SLAB
    hit = (head < HEADS) & (source == head * KERNEL + target // SLAB)
    return hit.astype(F32)


def head_spread():
    source = lax.broadcasted_iota(jnp.int32, (SLAB, WIDTH), 0)
    target = lax.broadcasted_iota(jnp.int32, (SLAB, WIDTH), 1)
    return (source == target // HEAD).astype(BF)


def norm_stats(v):
    mean = jnp.mean(v, axis=-1, keepdims=True)
    centred = v - mean
    var = jnp.mean(centred * centred, axis=-1, keepdims=True)
    inv = lax.rsqrt(var + EPSILON)
    return centred * inv, inv


def norm_back(d_scaled, hat, inv):
    first = jnp.mean(d_scaled, axis=-1, keepdims=True)
    second = jnp.mean(d_scaled * hat, axis=-1, keepdims=True)
    return inv * (d_scaled - first - hat * second)


def normal_cdf(v):
    density = jnp.exp2(v * v * -0.7213475204444817 - 1.3257480647361595)
    return 0.5 + 0.5 * lax.erf(v * 0.7071067811865476), density


def project_kernel(
    bucket, x, w, bias, dw, pw, kw, kb, qkvc, dep, kc, ks, co, xpad, cvpad
):
    joined = jnp.where(bucket[pl.program_id(0)] == 0, 1.0, 0.0).astype(F32)
    xb = x[...]
    proj = mm(xb, w[...])
    q = (proj[:, :WIDTH] + bias[0:1, :]).astype(BF)
    qkvc[:, 0:WIDTH] = q
    qkvc[:, WIDTH : 2 * WIDTH] = proj[:, WIDTH : 2 * WIDTH].astype(BF)
    qkvc[:, 2 * WIDTH : 3 * WIDTH] = (
        proj[:, 2 * WIDTH : 3 * WIDTH] + bias[1:2, :]
    ).astype(BF)
    cv = (proj[:, 3 * WIDTH :] + bias[2:3, :]).astype(BF)
    qkvc[:, 3 * WIDTH :] = cv
    fill_padded(xpad, xb.astype(F32), joined)
    fill_padded(cvpad, cv.astype(F32), joined)
    for c in range(DIM // SLAB):
        lanes = slice(c * SLAB, (c + 1) * SLAB)
        acc = moved(xpad, -EDGE, c) * dw[0:1, lanes]
        for j in range(1, KERNEL):
            acc += moved(xpad, j - EDGE, c) * dw[j : j + 1, lanes]
        dep[:, lanes] = acc.astype(BF)
    key_conv = mm(dep[...], pw[...]) + bias[3:4, :]
    kc[...] = key_conv
    conv_in = (key_conv * q.astype(F32)).astype(BF)
    select = slab_select(HEADS * KERNEL)
    kw_slab = mm_tn(kw[...], select.astype(BF)).astype(BF)
    kb_slab = jnp.dot(
        jnp.broadcast_to(kb[...], (8, HEADS * KERNEL)),
        select,
        precision=lax.Precision.HIGHEST,
        preferred_element_type=F32,
    )[0:1]
    logits = mm(conv_in, kw_slab) + kb_slab
    slabs = [logits[:, j * SLAB : (j + 1) * SLAB] for j in range(KERNEL)]
    top = functools.reduce(jnp.maximum, slabs)
    slabs = [jnp.exp(v - top) for v in slabs]
    inv = 1.0 / functools.reduce(jnp.add, slabs)
    for j in range(KERNEL):
        ks[:, j * SLAB : (j + 1) * SLAB] = (slabs[j] * inv).astype(BF)
    spread = head_spread()
    acc = None
    for j in range(KERNEL):
        weight = mm(ks[:, j * SLAB : (j + 1) * SLAB], spread)
        acc = add_taps(acc, weight, cvpad, j - EDGE)
    co[...] = jnp.concatenate(acc, axis=1).astype(BF)


def project(bucket, x, in_weight, in_bias, depth_weight, point_weight, kernel_weight, kernel_bias):
    count = x.shape[0]
    blocks = count // BLOCK
    taps = HEADS * KERNEL
    return pl.pallas_call(
        project_kernel,
        grid_spec=pltpu.PrefetchScalarGridSpec(
            num_scalar_prefetch=1,
            grid=(blocks,),
            in_specs=[
                rows(BLOCK, DIM),
                whole((DIM, 4 * WIDTH)),
                whole((4, WIDTH)),
                whole((KERNEL, DIM)),
                whole((DIM, WIDTH)),
                whole((taps, WIDTH)),
                whole((1, taps)),
            ],
            out_specs=[
                rows(BLOCK, 4 * WIDTH),
                rows(BLOCK, DIM),
                rows(BLOCK, WIDTH),
                rows(BLOCK, TAPS),
                rows(BLOCK, WIDTH),
            ],
            scratch_shapes=[
                padded(DIM),
                padded(WIDTH),
            ],
        ),
        out_shape=[
            sds((count, 4 * WIDTH), BF),
            sds((count, DIM), BF),
            sds((count, WIDTH), F32),
            sds((count, TAPS), BF),
            sds((count, WIDTH), BF),
        ],
        compiler_params=params(LIMITS["project"]),
        cost_estimate=cost(17),
        name="project",
    )(bucket, x, in_weight, in_bias, depth_weight, point_weight, kernel_weight, kernel_bias)


def mask_bias(is_short, valid_row):
    column = jnp.transpose(jnp.broadcast_to(valid_row.astype(F32), (SLAB, BLOCK)))
    column = jnp.concatenate([column] * (BLOCK // SLAB), axis=1)
    key_slot = (lax.broadcasted_iota(jnp.int32, (BLOCK, BLOCK), 0) // SHORT) * is_short
    query_slot = (lax.broadcasted_iota(jnp.int32, (BLOCK, BLOCK), 1) // SHORT) * is_short
    return jnp.where((key_slot == query_slot) & (column > 0.0), 0.0, -1e30)


def half_mask(v, h):
    lane = lax.broadcasted_iota(jnp.int32, v.shape, 1)
    keep = lane < HEAD if h % 2 == 0 else lane >= HEAD
    return jnp.where(keep, v, jnp.zeros_like(v))


def attend_kernel(
    bucket, valid, q, k, v, co, x, w_out, b_out, gain, shift,
    mixed, weights, scale, hat, inv, xin, bias, context,
):
    bias[...] = mask_bias(bucket[pl.program_id(0)], valid[...].reshape(1, BLOCK))
    vt = jnp.transpose(v[...])
    scale[...] = jnp.zeros_like(scale)
    for h in range(HEADS):
        lo = (h // 2) * SLAB
        qm = half_mask(q[:, lo : lo + SLAB], h) * jnp.asarray(HEAD**-0.5, BF)
        scores = mm_nt(k[:, lo : lo + SLAB], qm) + bias[...]
        top = jnp.max(scores, axis=0, keepdims=True)
        e = jnp.exp(scores - top)
        inverse = 1.0 / jnp.sum(e, axis=0, keepdims=True)
        weights[0, h] = e.astype(BF)
        part = mm(vt[h * HEAD : (h + 1) * HEAD], weights[0, h])
        context[h * HEAD : (h + 1) * HEAD, :] = part * inverse
        scale[0, h : h + 1, :] = inverse
    mixed[:, :WIDTH] = jnp.transpose(context[...]).astype(BF)
    mixed[:, WIDTH:] = co[...]
    att = mm(mixed[...], w_out[...]) + b_out[...] + x[...].astype(F32)
    scaled, stat = norm_stats(att)
    hat[...] = scaled
    inv[...] = jnp.broadcast_to(stat, inv.shape)
    xin[...] = (scaled * gain[0:1, :] + shift[0:1, :]).astype(BF)


def attend(bucket, valid, qkvc, conv_out, x, out_weight, out_bias, gain, shift):
    count = qkvc.shape[0]
    blocks = count // BLOCK
    return pl.pallas_call(
        attend_kernel,
        grid_spec=pltpu.PrefetchScalarGridSpec(
            num_scalar_prefetch=1,
            grid=(blocks,),
            in_specs=[
                pl.BlockSpec((1, 1, BLOCK), lambda i, *_: (i, 0, 0)),
                rows(BLOCK, WIDTH, 0),
                rows(BLOCK, WIDTH, 1),
                rows(BLOCK, WIDTH, 2),
                rows(BLOCK, WIDTH),
                rows(BLOCK, DIM),
                whole((DIM, DIM)),
                whole((1, DIM)),
                whole((2, DIM)),
                whole((2, DIM)),
            ],
            out_specs=[
                rows(BLOCK, DIM),
                pl.BlockSpec((1, HEADS, BLOCK, BLOCK), lambda i, *_: (i, 0, 0, 0)),
                pl.BlockSpec((1, 8, BLOCK), lambda i, *_: (i, 0, 0)),
                rows(BLOCK, DIM),
                rows(BLOCK, SLAB),
                rows(BLOCK, DIM),
            ],
            scratch_shapes=[
                pltpu.VMEM((BLOCK, BLOCK), F32),
                pltpu.VMEM((WIDTH, BLOCK), F32),
            ],
        ),
        out_shape=[
            sds((count, DIM), BF),
            sds((blocks, HEADS, BLOCK, BLOCK), BF),
            sds((blocks, 8, BLOCK), F32),
            sds((count, DIM), F32),
            sds((count, SLAB), F32),
            sds((count, DIM), BF),
        ],
        compiler_params=params(LIMITS["attend"]),
        cost_estimate=cost(14),
        name="attend",
    )(bucket, valid, qkvc, qkvc, qkvc, conv_out, x, out_weight, out_bias, gain, shift)


PARTS = 4


def unpack_weights(packs, w1, w2, bias_blocks, sems, g, shard, per):
    copies = []
    for k, pack in enumerate(packs):
        at = pl.ds(k * per, per)
        for n, (lo, size, dst) in enumerate(
            ((0, shard, w1), (shard, shard, w2), (2 * shard, 16, bias_blocks))
        ):
            copies.append(
                pltpu.make_async_copy(
                    pack.at[:, pl.ds(lo, size), :], dst.at[g, at], sems.at[g, k, n]
                )
            )
    return copies


def middle_kernel(
    group, *refs, shard, size
):
    hidden = shard * size
    packs, refs = refs[: 2 * PARTS], refs[2 * PARTS :]
    (
        hat1, inv1, xin, mixed, grad, w_out, gain, shift, b2,
        output, d_att, d_mixed, dback, act_a, dpre_a, sums, sums_a, grads_b, keep, send,
        ffn_out, d_summed, slope, datt_low, bias_sum, out_acc, w1s, w2s, blocks_s, b1s, sems,
        act_all, dpre_all, xin_all, dback_all, sums_b,
    ) = refs
    tile = xin.shape[0]
    here = pl.ds(pl.multiple_of(pl.program_id(0) * tile, tile), tile)
    act_b, dpre_b = act_all.at[here], dpre_all.at[here]
    own = pl.multiple_of(group[0] * WIDTH, SLAB)
    other = pl.multiple_of((1 - group[0]) * WIDTH, SLAB)
    part = 512
    step = pl.program_id(0)
    copies = [
        unpack_weights(
            packs[g * PARTS : (g + 1) * PARTS], w1s, w2s, blocks_s, sems, g, shard, size // PARTS
        )
        for g in range(2)
    ]

    @pl.when(step == 0)
    def _():
        for c in copies[0] + copies[1]:
            c.start()

    @pl.when(step == 0)
    def _():
        sums[...] = jnp.zeros_like(sums)
        bias_sum[...] = jnp.zeros_like(bias_sum)
        out_acc[...] = jnp.zeros_like(out_acc)

    def weights(g):
        return (
            w1s.at[g].reshape(hidden, WIDTH),
            w2s.at[g].reshape(hidden, WIDTH),
            b1s.at[g],
        )

    for g, base, act, at in ((0, own, act_a, 0), (1, other, act_b, hidden)):

        @pl.when(step == 0)
        def _():
            for c in copies[g]:
                c.wait()
            for r in range(size):
                row = blocks_s[g, r].astype(F32)[0:1, :shard]
                b1s[g, 0:1, r * shard : (r + 1) * shard] = row

        w1, w2, b1 = weights(g)
        xg = xin[:, pl.ds(base, WIDTH)]
        for lo in range(0, hidden, part):
            pre = mm_nt(xg, w1[lo : lo + part, :]) + b1[0:1, lo : lo + part]
            cdf, bell = normal_cdf(pre)
            act[:, lo : lo + part] = (pre * cdf).astype(BF)
            slope[:, at + lo : at + lo + part] = (cdf + pre * bell).astype(BF)
        ffn_out[:, pl.ds(base, WIDTH)] = mm(act[...], w2[...])
    result = (ffn_out[...] + b2[...]).astype(BF).astype(F32)
    hat2, inv2 = norm_stats(result + (hat1[...] * gain[0:1, :] + shift[0:1, :]))
    output[...] = (hat2 * gain[1:2, :] + shift[1:2, :]).astype(BF)
    dy = grad[...].astype(F32)
    sums[1:2, :] += col_sum(dy * hat2)
    sums[3:4, :] += col_sum(dy)
    ds = norm_back(dy * gain[1:2, :], hat2, inv2)
    d_summed[...] = ds
    low = ds.astype(BF)
    dback[...] = low
    xin_all[here, :] = xin[:, pl.ds(other, WIDTH)]
    dback_all[here, :] = dback[:, pl.ds(other, WIDTH)]
    sums[5:6, :] += col_sum(low.astype(F32))
    for g, base, dpre, at in ((0, own, dpre_a, 0), (1, other, dpre_b, hidden)):
        w1, w2, b1 = weights(g)
        dg = dback[:, pl.ds(base, WIDTH)]
        for lo in range(0, hidden, part):
            dp = mm_nt(dg, w2[lo : lo + part, :]) * slope[:, at + lo : at + lo + part].astype(F32)
            bias_sum[g : g + 1, lo : lo + part] += col_sum(dp)
            dpre[:, lo : lo + part] = dp.astype(BF)
        ffn_out[:, pl.ds(base, WIDTH)] = mm(dpre[...], w1[...])
    dn = d_summed[...] + ffn_out[...].astype(BF).astype(F32)
    hat = hat1[...]
    sums[0:1, :] += col_sum(dn * hat)
    sums[2:3, :] += col_sum(dn)
    da = norm_back(dn * gain[0:1, :], hat, inv1[:, 0:1])
    d_att[...] = da
    sums[4:5, :] += col_sum(da)
    datt_low[...] = da.astype(BF)
    d_mixed[...] = mm_nt(datt_low[...], w_out[...]).astype(BF)
    out_acc[...] += mm_tn(mixed[...], datt_low[...])

    @pl.when(step == pl.num_programs(0) - 1)
    def _():
        split_halves(group[0], out_acc, keep, send)
        for g, dst in ((0, sums_a), (1, sums_b)):
            dst[...] = jnp.zeros_like(dst)
            for r in range(size):
                dst[r, 0:1, 0:shard] = bias_sum[g : g + 1, r * shard : (r + 1) * shard]
        quarter, per = hidden // PARTS, size // PARTS
        for k in range(PARTS):
            lanes = slice(k * quarter, (k + 1) * quarter)
            write_pack(
                dpre_all[:, lanes], act_all[:, lanes], xin_all[...], dback_all[...],
                sums_b, grads_b, k * per, per, shard,
            )


def middle(group, packs, shard, size, hat, inv, xin, mixed, grad, out_weight, gain, shift, b2):
    count = xin.shape[0]
    hidden = shard * size
    tile = BLOCK // 2
    pack_shape = (size, 2 * shard + 16, WIDTH)
    sum_shape = (size, 8, WIDTH)
    return pl.pallas_call(
        functools.partial(middle_kernel, shard=shard, size=size),
        grid_spec=pltpu.PrefetchScalarGridSpec(
            num_scalar_prefetch=1,
            grid=(count // tile,),
            in_specs=[pl.BlockSpec(memory_space=pl.ANY)] * (2 * PARTS)
            + [
                rows(tile, DIM),
                rows(tile, SLAB),
                rows(tile, DIM),
                rows(tile, DIM),
                rows(tile, DIM),
                whole((DIM, DIM)),
                whole((2, DIM)),
                whole((2, DIM)),
                whole((1, DIM)),
            ],
            out_specs=[
                rows(tile, DIM),
                rows(tile, DIM),
                rows(tile, DIM),
                rows(tile, DIM),
                rows(tile, hidden),
                rows(tile, hidden),
                whole((8, DIM)),
                whole(sum_shape),
                whole(pack_shape),
                whole((WIDTH, DIM)),
                whole((WIDTH, DIM)),
            ],
            scratch_shapes=[
                pltpu.VMEM((tile, DIM), F32),
                pltpu.VMEM((tile, DIM), F32),
                pltpu.VMEM((tile, 2 * hidden), BF),
                pltpu.VMEM((tile, DIM), BF),
                pltpu.VMEM((8, hidden), F32),
                pltpu.VMEM((DIM, DIM), F32),
                pltpu.VMEM((2, size, shard, WIDTH), BF),
                pltpu.VMEM((2, size, shard, WIDTH), BF),
                pltpu.VMEM((2, size, 16, WIDTH), BF),
                pltpu.VMEM((2, 8, hidden), F32),
                pltpu.SemaphoreType.DMA((2, PARTS, 3)),
                pltpu.VMEM((count, hidden), BF),
                pltpu.VMEM((count, hidden), BF),
                pltpu.VMEM((count, WIDTH), BF),
                pltpu.VMEM((count, WIDTH), BF),
                pltpu.VMEM(sum_shape, F32),
            ],
        ),
        out_shape=[
            sds((count, DIM), BF),
            sds((count, DIM), F32),
            sds((count, DIM), BF),
            sds((count, DIM), BF),
            sds((count, hidden), BF),
            sds((count, hidden), BF),
            sds((8, DIM), F32),
            sds(sum_shape, F32),
            sds(pack_shape, BF),
            sds((WIDTH, DIM), BF),
            sds((WIDTH, DIM), BF),
        ],
        compiler_params=params(LIMITS["middle"]),
        cost_estimate=cost(38),
        name="middle",
    )(group, *packs, hat, inv, xin, mixed, grad, out_weight, gain, shift, b2)


def write_pack(dpre, act, xin, dback, sums, out, first_block, per, shard):
    first = mm_tn(dpre, xin).astype(BF)
    second = mm_tn(act, dback).astype(BF)
    for z in range(per):
        out[first_block + z, 0:shard, :] = first[z * shard : (z + 1) * shard]
        out[first_block + z, shard : 2 * shard, :] = second[z * shard : (z + 1) * shard]
        row = jnp.concatenate([sums[first_block + z], jnp.zeros((8, WIDTH), F32)], axis=0)
        out[first_block + z, 2 * shard :, :] = row.astype(BF)


def ffn_grad_kernel(group, dpre, act, xin, dback, sums, out, *, shard):
    write_pack(
        dpre[...], act[...], xin[...], dback[...], sums, out, 0, out.shape[0], shard
    )


def ffn_grad(group, dpre, act, xin, dback, sums, shard, size):
    count, hidden = dpre.shape
    tile = hidden // PARTS
    per = size // PARTS
    lanes = pl.BlockSpec((count, tile), lambda i, g: (0, i))
    side = pl.BlockSpec((count, WIDTH), lambda i, g: (0, g[0]))
    return pl.pallas_call(
        functools.partial(ffn_grad_kernel, shard=shard),
        grid_spec=pltpu.PrefetchScalarGridSpec(
            num_scalar_prefetch=1,
            grid=(PARTS,),
            in_specs=[
                lanes, lanes, side, side, pl.BlockSpec((per, 8, WIDTH), lambda i, g: (i, 0, 0)),
            ],
            out_specs=pl.BlockSpec((per, 2 * shard + 16, WIDTH), lambda i, g: (i, 0, 0)),
        ),
        out_shape=sds((size, 2 * shard + 16, WIDTH), BF),
        compiler_params=params(LIMITS["ffn_grad"]),
        cost_estimate=cost(7),
        name="ffn_grad",
    )(group, dpre, act, xin, dback, sums)


def repack(packs, size, shard):
    old = (packs.shape[1] - 16) // 2
    first = packs[:, :old].reshape(size, shard, WIDTH)
    second = packs[:, old : 2 * old].reshape(size, shard, WIDTH)
    bias = packs[:, 2 * old, :old].reshape(size, 1, shard)
    bias = jnp.pad(bias, ((0, 0), (0, 15), (0, WIDTH - shard)))
    return jnp.concatenate([first, second, bias], axis=1)


def attend_back_kernel(info, weights, scale, q, k, v, dctx, x, dq, dkv, sums, keep, send, dqt, acc):
    step = pl.program_id(0)

    @pl.when(step == 0)
    def _():
        sums[...] = jnp.zeros_like(sums)
        acc[...] = jnp.zeros_like(acc)

    root = jnp.asarray(HEAD**-0.5, BF)
    kt = jnp.transpose(k[...] * root)
    for pair in range(HEADS // 2):
        lo = pair * SLAB
        vp = v[:, lo : lo + SLAB]
        dk = dv = None
        for h in (2 * pair, 2 * pair + 1):
            qm = half_mask(q[:, lo : lo + SLAB], h) * root
            cm = half_mask(dctx[:, lo : lo + SLAB], h)
            probs = weights[0, h].astype(F32) * scale[0, h : h + 1, :]
            d_probs = mm_nt(vp, cm)
            delta = col_sum(probs * d_probs)
            d_scores = (probs * (d_probs - delta)).astype(BF)
            probs = probs.astype(BF)
            dv = mm(probs, cm) if dv is None else dv + mm(probs, cm)
            dk = mm(d_scores, qm) if dk is None else dk + mm(d_scores, qm)
            dqt[h * HEAD : (h + 1) * HEAD, :] = mm(kt[h * HEAD : (h + 1) * HEAD], d_scores)
        dkv[:, lo : lo + SLAB] = dk.astype(BF)
        dkv[:, WIDTH + lo : WIDTH + lo + SLAB] = dv.astype(BF)
        sums[0:1, lo : lo + SLAB] += col_sum(dv)
    dq[...] = jnp.transpose(dqt[...])
    acc[...] += mm_tn(x[...], dkv[...])

    @pl.when(step == pl.num_programs(0) - 1)
    def _():
        split_halves(info[0], acc, keep, send)


def split_halves(core, total, keep, send):
    half = total.shape[0] // 2
    keep[...] = total[pl.ds(pl.multiple_of(core * half, 8), half), :].astype(BF)
    send[...] = total[pl.ds(pl.multiple_of((1 - core) * half, 8), half), :].astype(BF)


def attend_back(info, weights, scale, qkvc, d_mixed, x):
    count = qkvc.shape[0]
    blocks = count // BLOCK
    return pl.pallas_call(
        attend_back_kernel,
        grid_spec=pltpu.PrefetchScalarGridSpec(
            num_scalar_prefetch=1,
            grid=(blocks,),
            in_specs=[
                pl.BlockSpec((1, HEADS, BLOCK, BLOCK), lambda i, *_: (i, 0, 0, 0)),
                pl.BlockSpec((1, 8, BLOCK), lambda i, *_: (i, 0, 0)),
                rows(BLOCK, WIDTH, 0),
                rows(BLOCK, WIDTH, 1),
                rows(BLOCK, WIDTH, 2),
                rows(BLOCK, WIDTH, 0),
                rows(BLOCK, DIM),
            ],
            out_specs=[
                rows(BLOCK, WIDTH),
                rows(BLOCK, DIM),
                whole((8, WIDTH)),
                whole((WIDTH, DIM)),
                whole((WIDTH, DIM)),
            ],
            scratch_shapes=[
                pltpu.VMEM((WIDTH, BLOCK), F32),
                pltpu.VMEM((DIM, DIM), F32),
            ],
        ),
        out_shape=[
            sds((count, WIDTH), F32),
            sds((count, DIM), BF),
            sds((8, WIDTH), F32),
            sds((WIDTH, DIM), BF),
            sds((WIDTH, DIM), BF),
        ],
        compiler_params=params(LIMITS["attend_back"]),
        cost_estimate=cost(16),
        name="attend_back",
    )(info, weights, scale, qkvc, qkvc, qkvc, d_mixed, x)


POINT_ROW = DIM
SMALL_ROW = DIM + WIDTH
LATE_ROWS = DIM + WIDTH + 128
NORM_ROW = SMALL_ROW + 64
TAP_ROW = SMALL_ROW + 72


def conv_back_kernel(
    info, q, cv, dconv, kc, ks, dq, x, dep, kw, pw, sums_mid, sums_v, dqc, dkc, keep, send,
    cvpad, dcpad, kspad, xpad, dk_slab, dlog, qc_acc, pt_acc, kw_acc, kb_acc, dw_acc, sums, flat
):
    step = pl.program_id(0)
    taps = HEADS * KERNEL

    @pl.when(step == 0)
    def _():
        for ref in (qc_acc, pt_acc, kw_acc, kb_acc, dw_acc, sums):
            ref[...] = jnp.zeros_like(ref)

    joined = jnp.where(info[1 + step] == 0, 1.0, 0.0).astype(F32)
    dc = dconv[...].astype(F32)
    fill_padded(cvpad, cv[...].astype(F32), joined)
    fill_padded(dcpad, dc, joined)
    fill_padded(kspad, ks[...].astype(F32), joined)
    fill_padded(xpad, x[...].astype(F32), joined)
    spread = head_spread()
    total = None
    for j in range(KERNEL):
        product = jnp.concatenate(add_taps(None, dc, cvpad, j - EDGE), axis=1)
        part = mm_nt(product.astype(BF), spread)
        dk_slab[:, j * SLAB : (j + 1) * SLAB] = part
        part = part * ks[:, j * SLAB : (j + 1) * SLAB].astype(F32)
        total = part if total is None else total + part
    for j in range(KERNEL):
        lanes = slice(j * SLAB, (j + 1) * SLAB)
        grad = ks[:, lanes].astype(F32) * (dk_slab[:, lanes] - total)
        kb_acc[0:1, lanes] += col_sum(grad)
        dlog[:, lanes] = grad.astype(BF)
    acc = None
    for j in range(KERNEL):
        weight = mm(moved(kspad, EDGE - j, j).astype(BF), spread)
        acc = add_taps(acc, weight, dcpad, EDGE - j)
    acc = jnp.concatenate(acc, axis=1)
    dqc[:, WIDTH:] = acc.astype(BF)
    sums[1:2, :] += col_sum(acc)
    select = slab_select(taps)
    compact = mm_nt(dlog[...], select.astype(BF)).astype(BF)
    qf = q[...].astype(F32)
    key_conv = kc[...]
    conv_in = (key_conv * qf).astype(BF)
    kw_acc[0:taps, :] += mm_tn(compact, conv_in)
    d_conv_in = mm(compact, kw[...])
    d_key = d_conv_in * qf
    sums[2:3, :] += col_sum(d_key)
    dkc[...] = d_key.astype(BF)
    dq_all = dq[...] + d_conv_in * key_conv
    sums[0:1, :] += col_sum(dq_all)
    dqc[:, :WIDTH] = dq_all.astype(BF)
    qc_acc[...] += mm_tn(x[...], dqc[...])
    pt_acc[...] += mm_tn(dep[...], dkc[...])
    d_depth = mm_nt(dkc[...], pw[...])
    for c in range(DIM // SLAB):
        lanes = slice(c * SLAB, (c + 1) * SLAB)
        here = d_depth[:, lanes]
        for j in range(KERNEL):
            dw_acc[j : j + 1, lanes] += col_sum(moved(xpad, j - EDGE, c) * here)

    @pl.when(step == pl.num_programs(0) - 1)
    def _():
        flat[0:DIM, :] = qc_acc[...].astype(BF)
        flat[POINT_ROW:SMALL_ROW, 0:WIDTH] = pt_acc[0:WIDTH, :].astype(BF)
        flat[POINT_ROW:SMALL_ROW, WIDTH:] = pt_acc[WIDTH:, :].astype(BF)
        flat[SMALL_ROW : SMALL_ROW + 64, 0:WIDTH] = kw_acc[...].astype(BF)
        kb = lax.dot_general(
            kb_acc[...],
            select,
            (((1,), (1,)), ((), ())),
            precision=lax.Precision.HIGHEST,
            preferred_element_type=F32,
        )
        blank = jnp.zeros((4, WIDTH), F32)
        rows_of = jnp.concatenate([sums[0:1], sums_v[0:1], sums[1:3], blank], axis=0)
        kb = jnp.concatenate([kb, jnp.zeros((8, WIDTH - taps), F32)], axis=1)
        flat[SMALL_ROW : SMALL_ROW + 16, WIDTH:] = jnp.concatenate([rows_of, kb], axis=0).astype(BF)
        flat[SMALL_ROW + 16 : NORM_ROW, WIDTH:] = jnp.zeros((48, WIDTH), BF)
        flat[NORM_ROW : NORM_ROW + 32, :] = jnp.concatenate(
            [sums_mid[...], dw_acc[...], jnp.zeros((8, DIM), F32)], axis=0
        ).astype(BF)
        flat[NORM_ROW + 32 :, :] = jnp.zeros((32, DIM), BF)
        half = LATE_ROWS // 2
        core = info[0]
        keep[...] = flat[pl.ds(pl.multiple_of(core * half, 16), half), :]
        send[...] = flat[pl.ds(pl.multiple_of((1 - core) * half, 16), half), :]


def conv_back(info, qkvc, d_mixed, kc, ks, dq, x, dep, kernel_weight, point_weight, sums_mid, sums_v):
    count = qkvc.shape[0]
    blocks = count // BLOCK
    taps = HEADS * KERNEL
    half = LATE_ROWS // 2
    return pl.pallas_call(
        conv_back_kernel,
        grid_spec=pltpu.PrefetchScalarGridSpec(
            num_scalar_prefetch=1,
            grid=(blocks,),
            in_specs=[
                rows(BLOCK, WIDTH, 0),
                rows(BLOCK, WIDTH, 3),
                rows(BLOCK, WIDTH, 1),
                rows(BLOCK, WIDTH),
                rows(BLOCK, TAPS),
                rows(BLOCK, WIDTH),
                rows(BLOCK, DIM),
                rows(BLOCK, DIM),
                whole((taps, WIDTH)),
                whole((DIM, WIDTH)),
                whole((8, DIM)),
                whole((8, WIDTH)),
            ],
            out_specs=[
                rows(BLOCK, DIM),
                rows(BLOCK, WIDTH),
                whole((half, DIM)),
                whole((half, DIM)),
            ],
            scratch_shapes=[
                padded(WIDTH),
                padded(WIDTH),
                padded(TAPS),
                padded(DIM),
                pltpu.VMEM((BLOCK, TAPS), F32),
                pltpu.VMEM((BLOCK, TAPS), BF),
                pltpu.VMEM((DIM, DIM), F32),
                pltpu.VMEM((DIM, WIDTH), F32),
                pltpu.VMEM((64, WIDTH), F32),
                pltpu.VMEM((8, TAPS), F32),
                pltpu.VMEM((16, DIM), F32),
                pltpu.VMEM((8, WIDTH), F32),
                pltpu.VMEM((LATE_ROWS, DIM), BF),
            ],
        ),
        out_shape=[
            sds((count, DIM), BF),
            sds((count, WIDTH), BF),
            sds((half, DIM), BF),
            sds((half, DIM), BF),
        ],
        compiler_params=params(LIMITS["conv_back"]),
        cost_estimate=cost(22),
        name="conv_back",
    )(info, qkvc, qkvc, d_mixed, kc, ks, dq, x, dep, kernel_weight, point_weight, sums_mid, sums_v)


def hidden_kernel(info, dkc, d_att, dqc, dkv, dw, pw, w, *refs, start):
    hidden, ddpad = refs[-2:]
    joined = jnp.where(info[1 + start + pl.program_id(0)] == 0, 1.0, 0.0).astype(F32)
    fill_padded(ddpad, mm_nt(dkc[...], pw[...]), joined)
    hidden[...] = (
        d_att[...]
        + mm_nt(dkv[...], w[:, WIDTH : 3 * WIDTH])
        + mm_nt(dqc[:, :WIDTH], w[:, :WIDTH])
        + mm_nt(dqc[:, WIDTH:], w[:, 3 * WIDTH :])
    )
    for c in range(DIM // SLAB):
        lanes = slice(c * SLAB, (c + 1) * SLAB)
        acc = hidden[:, lanes]
        for j in range(KERNEL):
            acc += moved(ddpad, EDGE - j, c) * dw[j : j + 1, lanes]
        hidden[:, lanes] = acc


def hidden_back(info, dkc, d_att, dqc, dkv, depth_weight, point_weight, in_weight, start, stop, before=None):
    count = d_att.shape[0]

    def part(width):
        return pl.BlockSpec((BLOCK, width), lambda i, *_: (i + start, 0))

    extra = [] if before is None else [before]
    return pl.pallas_call(
        functools.partial(hidden_kernel, start=start),
        grid_spec=pltpu.PrefetchScalarGridSpec(
            num_scalar_prefetch=1,
            grid=(stop - start,),
            in_specs=[
                part(WIDTH),
                part(DIM),
                part(DIM),
                part(DIM),
                whole((KERNEL, DIM)),
                whole((DIM, WIDTH)),
                whole((DIM, 4 * WIDTH)),
            ]
            + [pl.BlockSpec(memory_space=pl.ANY)] * len(extra),
            out_specs=part(DIM),
            scratch_shapes=[padded(DIM)],
        ),
        out_shape=sds((count, DIM), F32),
        input_output_aliases={8: 0} if extra else {},
        compiler_params=params(LIMITS["hidden_back"]),
        cost_estimate=cost(6),
        name="hidden_back",
    )(info, dkc, d_att, dqc, dkv, depth_weight, point_weight, in_weight, *extra)


def load_parts(parts, dst, sems, core, digit):
    count = dst.shape[0]
    copies = []
    per = max(len(parts) // 2, 1)
    size = count // len(parts)
    for n, part in enumerate(parts):
        c, k = n // per, n % per
        row = 0 if len(parts) == 1 else (core ^ c) * (count // 2) + (digit ^ k) * size * (per > 1)
        at = pl.ds(pl.multiple_of(row, 16), size)
        copies.append(pltpu.make_async_copy(part, dst.at[at, :], sems.at[n]))
    for c in copies:
        c.start()
    for c in copies:
        c.wait()


def unpack_early_kernel(info, *refs):
    parts, (in_w, out_w, early, sems) = refs[:-4], refs[-4:]
    step = pl.program_id(0)

    @pl.when(step == 0)
    def _():
        load_parts(parts, early, sems, info[0], info[1])
        out_w[0:WIDTH, :] = early[0:WIDTH, :].astype(F32)
        out_w[WIDTH:, :] = early[DIM : DIM + WIDTH, :].astype(F32)

    lanes = pl.ds(pl.multiple_of(step * WIDTH, SLAB), WIDTH)
    in_w[0:WIDTH, :] = early[WIDTH:DIM, lanes].astype(F32)
    in_w[WIDTH:, :] = early[DIM + WIDTH :, lanes].astype(F32)


def unpack_early(info, parts):
    return pl.pallas_call(
        unpack_early_kernel,
        grid_spec=pltpu.PrefetchScalarGridSpec(
            num_scalar_prefetch=1,
            grid=(2,),
            in_specs=[pl.BlockSpec(memory_space=pl.ANY)] * len(parts),
            out_specs=[
                pl.BlockSpec((DIM, WIDTH), lambda i, *_: (0, 1 + i)),
                whole((DIM, DIM)),
            ],
            scratch_shapes=[
                pltpu.VMEM((2 * DIM, DIM), BF),
                pltpu.SemaphoreType.DMA((len(parts),)),
            ],
        ),
        out_shape=[sds((DIM, 4 * WIDTH), F32), sds((DIM, DIM), F32)],
        compiler_params=params(LIMITS["unpack"]),
        cost_estimate=cost(3),
        name="unpack_early",
    )(info, *parts)


def unpack_late_kernel(info, *refs):
    parts, (_, in_w, in_b, dw, point, kw, kb, out_b, gain, shift, b2, late, sems) = (
        refs[:-13],
        refs[-13:],
    )
    step = pl.program_id(0)
    taps = HEADS * KERNEL

    @pl.when(step == 0)
    def _():
        load_parts(parts, late, sems, info[0], info[1])
        point[0:WIDTH, :] = late[POINT_ROW:SMALL_ROW, 0:WIDTH].astype(F32)
        point[WIDTH:, :] = late[POINT_ROW:SMALL_ROW, WIDTH:].astype(F32)
        kw[...] = late[SMALL_ROW : SMALL_ROW + 64, 0:WIDTH].astype(F32)[0:taps]
        mixed = late[SMALL_ROW : SMALL_ROW + 16, WIDTH:].astype(F32)
        in_b[...] = mixed[0:4]
        kb[...] = mixed[8:9, 0:taps]
        norms = late[NORM_ROW : NORM_ROW + 32, :].astype(F32)
        gain[...] = norms[0:2]
        shift[...] = norms[2:4]
        out_b[...] = norms[4]
        b2[...] = jnp.where(info[0] == 0, norms[5:6, 0:WIDTH], norms[5:6, WIDTH:])
        dw[...] = norms[8 : 8 + KERNEL]

    in_w[...] = late[0:DIM, pl.ds(pl.multiple_of(step * WIDTH, SLAB), WIDTH)].astype(F32)


def unpack_late(info, parts, in_w):
    taps = HEADS * KERNEL
    shapes = [
        (4, WIDTH), (KERNEL, DIM), (DIM, WIDTH), (taps, WIDTH), (1, taps), (DIM,), (2, DIM),
        (2, DIM), (1, WIDTH),
    ]
    return pl.pallas_call(
        unpack_late_kernel,
        grid_spec=pltpu.PrefetchScalarGridSpec(
            num_scalar_prefetch=1,
            grid=(2,),
            in_specs=[pl.BlockSpec(memory_space=pl.ANY)] * (len(parts) + 1),
            out_specs=[pl.BlockSpec((DIM, WIDTH), lambda i, *_: (0, 3 * i))]
            + [whole(v) for v in shapes],
            scratch_shapes=[
                pltpu.VMEM((LATE_ROWS, DIM), BF),
                pltpu.SemaphoreType.DMA((len(parts),)),
            ],
        ),
        out_shape=[sds((DIM, 4 * WIDTH), F32)] + [sds(v, F32) for v in shapes],
        input_output_aliases={1 + len(parts): 0},
        compiler_params=params(LIMITS["unpack"]),
        cost_estimate=cost(3),
        name="unpack_late",
    )(info, *parts, in_w)


def digit_groups(size):
    groups, shift = [], 0
    while (1 << shift) < size:
        bits = 2 if (4 << shift) <= size else 1
        groups.append((shift, 1 << bits))
        shift += bits
    return groups


def partner(value, size, distance):
    return lax.ppermute(value, "wide", [(i, i ^ distance) for i in range(size)])


def swap_core(value):
    return lax.ppermute(value, "grp", [(0, 1), (1, 0)])


def fence(*values):
    return lax.optimization_barrier(values)


def add_up(values, dtype=BF):
    total = values[0].astype(F32)
    for v in values[1:]:
        total = total + v.astype(F32)
    return total.astype(dtype)


def gather_relative(block, size):
    buf = block[None]
    for shift, count in reversed(digit_groups(size)):
        parts = [buf] + [partner(buf, size, k << shift) for k in range(1, count)]
        buf = jnp.concatenate(parts, axis=0)
    return buf


def scatter_relative(blocks, size):
    buf = blocks
    for shift, count in digit_groups(size):
        parts = buf.reshape((count, buf.shape[0] // count) + buf.shape[1:])
        buf = add_up([parts[0]] + [partner(parts[k], size, k << shift) for k in range(1, count)])
    return buf[0].astype(F32)


def take(array, index):
    return lax.dynamic_index_in_dim(array, index, 0, keepdims=False)


class Sum:
    def __init__(self, size, half, direct=False):
        self.size, self.value, self.direct = size, half, direct

    def digit(self, group):
        return (lax.axis_index("wide") >> group[0]) & (group[1] - 1)

    def swap(self, group, blocks):
        shift, count = group
        mask = (count - 1) << shift
        teams = [
            [i + (d << shift) for d in range(count)] for i in range(self.size) if not i & mask
        ]
        return [
            lax.all_to_all(
                blocks, "wide", split_axis=0, concat_axis=0, axis_index_groups=teams, tiled=True
            )
        ]

    def send(self, group):
        shift, count = group
        blocks = self.value.reshape(count, self.value.shape[0] // count, DIM)
        if not self.direct:
            self.parts = self.swap(group, blocks)
            return
        digit = self.digit(group)
        self.parts = [take(blocks, digit)] + [
            partner(take(blocks, digit ^ k), self.size, k << shift) for k in range(1, count)
        ]

    def reduce(self):
        if self.direct:
            self.value = add_up(self.parts)
        else:
            self.value = jnp.sum(self.parts[0].astype(F32), axis=0).astype(BF)

    def spread(self, group):
        shift, count = group
        if not self.direct:
            blocks = jnp.broadcast_to(self.value[None], (count,) + self.value.shape)
            self.parts = self.swap(group, blocks)
            return
        self.parts = [self.value] + [
            partner(self.value, self.size, k << shift) for k in range(1, count)
        ]

    def join(self, group):
        if not self.direct:
            self.value = self.parts[0].reshape(-1, DIM)
            return
        digit = self.digit(group)
        stacked = jnp.stack(self.parts)
        self.value = jnp.concatenate([take(stacked, digit ^ d) for d in range(group[1])], axis=0)


def sum_everywhere(keep, send, size):
    core = lax.axis_index("grp")
    total = Sum(size, add_up([keep, swap_core(send)]))
    groups = digit_groups(size)
    for group in groups:
        total.send(group)
        total.reduce()
    for group in reversed(groups):
        total.spread(group)
        total.join(group)
    halves = jnp.stack([total.value, swap_core(total.value)])
    return jnp.concatenate([take(halves, core), take(halves, 1 - core)], axis=0)


def body(
    size,
    hidden_in,
    valid_mask,
    bucket,
    in_weight,
    in_bias,
    depth_weight,
    point_weight,
    kernel_weight,
    kernel_bias,
    out_weight,
    out_bias,
    norm_gain,
    norm_bias,
    ffn_in,
    ffn_in_bias,
    ffn_out,
    ffn_out_bias,
    out_grad,
):
    count = hidden_in.shape[0]
    blocks = count // BLOCK
    shard = ffn_in.shape[1]
    hidden = shard * size
    core = lax.axis_index("grp").astype(jnp.int32)
    group = jnp.reshape(core, (1,))
    info = jnp.concatenate([group, bucket])
    valid = valid_mask.reshape(blocks, 1, BLOCK)
    kernel_weight = kernel_weight.T
    groups = digit_groups(size)
    staged = len(groups) == 2 and groups[0][1] == groups[1][1] == PARTS and shard % 16 == 0

    bias_rows = jnp.pad(ffn_in_bias, ((0, 15), (0, WIDTH - shard)))
    pack = jnp.concatenate([ffn_in[0], ffn_out[0], bias_rows], axis=0)[None]
    other_bias = swap_core(ffn_out_bias)
    b2 = jnp.concatenate([ffn_out_bias, other_bias], axis=1)
    b2 = jnp.where(core == 0, b2, jnp.concatenate([other_bias, ffn_out_bias], axis=1))

    if staged:
        got = [partner(pack, size, k << groups[1][0]) for k in range(1, PARTS)]
    qkvc, dep, kc, ks, conv_out = project(
        bucket, hidden_in, in_weight, in_bias, depth_weight, point_weight, kernel_weight,
        kernel_bias[None],
    )
    if staged:
        *got, conv_out = fence(*got, conv_out)
        near = jnp.concatenate([pack] + got, axis=0)
        own = [near] + [partner(near, size, k) for k in range(1, PARTS)]
        near_other = swap_core(near)
        near_other, conv_out, info, b2 = fence(near_other, conv_out, info, b2)
    mixed, attn_weights, attn_scale, hat, inv, xin = attend(
        bucket, valid, qkvc, conv_out, hidden_in, out_weight, out_bias[None], norm_gain, norm_bias
    )
    if staged:
        *own, xin = fence(*own, xin)
        packs = own + [near_other] + [swap_core(v) for v in own[1:]]
    else:
        gathered = gather_relative(pack[0], size)
        packs = [
            pack[None]
            for v in (gathered, swap_core(gathered))
            for pack in repack(v, PARTS, hidden // PARTS)
        ]
    form = (shard, size) if staged else (hidden // PARTS, PARTS)
    (
        output, d_att, d_mixed, dback, act_a, dpre_a, sums, sums_a, grads_b, out_keep, out_send,
    ) = middle(
        group, packs, *form, hat, inv, xin, mixed, out_grad, out_weight, norm_gain, norm_bias, b2
    )
    from_core = swap_core(grads_b)
    grads_a = ffn_grad(group, dpre_a, act_a, xin, dback, sums_a, *form)
    grads_a, from_core, d_mixed = fence(grads_a, from_core, d_mixed)

    if not staged:
        ffn_grads = scatter_relative(
            repack(add_up([grads_a, from_core]), size, shard), size
        )
    else:
        per = size // PARTS
        xy, z = groups
        own = [v[k * per : (k + 1) * per] for k in range(PARTS) for v in (grads_a, from_core)]
        parts = own[:2] + [add_up(own[2 * k : 2 * k + 2]) for k in range(1, PARTS)]
        *parts, d_mixed, out_send = fence(*parts, d_mixed, out_send)
        from_x, from_y = partner(parts[2], size, 1), partner(parts[3], size, 2)
        out_got = swap_core(out_send)
    dq, dkv, sums_v, kv_keep, kv_send = attend_back(
        info, attn_weights, attn_scale, qkvc, d_mixed, hidden_in
    )
    if staged:
        from_x, from_y, out_got, kv_send = fence(from_x, from_y, out_got, kv_send)
        kv_got = swap_core(kv_send)
        early = jnp.concatenate([add_up([out_keep, out_got]), add_up([kv_keep, kv_got])], axis=0)
        early = Sum(size, early, direct=True)
        early.value, dq = fence(early.value, dq)
        from_xy = partner(parts[4], size, 3)
        early.send(xy)
    dqc, dkc, late_keep, late_send = conv_back(
        info, qkvc, d_mixed, kc, ks, dq, hidden_in, dep, kernel_weight, point_weight, sums, sums_v
    )
    if staged:
        *early.parts, from_xy, late_send, dkc = fence(*early.parts, from_xy, late_send, dkc)
        late_got = swap_core(late_send)
        parts = [
            add_up([v[k] for v in (parts[0], parts[1], from_x, from_y, from_xy)]) for k in range(PARTS)
        ]
        early.reduce()
        late = Sum(size, add_up([late_keep, late_got]))
        early.value, late.value, dkc = fence(early.value, late.value, dkc)
        late.send(xy)
        early.send(z)
    hidden_grad = hidden_back(
        info, dkc, d_att, dqc, dkv, depth_weight, point_weight, in_weight, 0, blocks
    )
    info = jnp.stack([core, lax.axis_index("wide").astype(jnp.int32) & (PARTS - 1)])
    if staged:
        late.parts[0], *early.parts, hidden_grad = fence(late.parts[0], *early.parts, hidden_grad)
        late.reduce()
        early.reduce()
        late.value, early.value = fence(late.value, early.value)
        late.send(z)
        early.spread(z)
        late.parts[0], *early.parts = fence(late.parts[0], *early.parts)
        late.reduce()
        early.join(z)
        early.value, late.value, *parts = fence(early.value, late.value, *parts)
        late.spread(z)
        early.spread(xy)
        from_z = [partner(parts[k], size, k << z[0]) for k in (1, 2)]
        late.parts[0], *rest = fence(late.parts[0], *early.parts, *from_z, parts[3])
        early.parts, from_z, last = rest[:PARTS], rest[PARTS : PARTS + 2], rest[-1]
        late.join(z)
        late.spread(xy)
        early_all = early.parts + [swap_core(v) for v in early.parts]
        from_z.append(partner(last, size, 3 << z[0]))
        in_weight_grad, out_weight_grad = unpack_early(info, early_all)
        late.parts[0], from_z[2], in_weight_grad = fence(late.parts[0], from_z[2], in_weight_grad)
        late.join(xy)
        late_all = [late.value, swap_core(late.value)]
        ffn_grads = add_up([parts[0]] + from_z, F32)
        late_all[1], ffn_grads = fence(late_all[1], ffn_grads)
    else:
        early_all = [
            sum_everywhere(
                jnp.concatenate([out_keep, kv_keep], axis=0),
                jnp.concatenate([out_send, kv_send], axis=0),
                size,
            )
        ]
        late_all = [sum_everywhere(late_keep, late_send, size)]
        in_weight_grad, out_weight_grad = unpack_early(info, early_all)
    (
        in_weight_grad, in_bias_grad, depth_weight_grad, point_weight_grad, kernel_weight_grad,
        kernel_bias_grad, out_bias_grad, gain_grad, shift_grad, ffn_out_bias_grad,
    ) = unpack_late(info, late_all, in_weight_grad)
    return (
        output,
        hidden_grad,
        in_weight_grad,
        in_bias_grad,
        depth_weight_grad,
        point_weight_grad,
        kernel_weight_grad.T,
        kernel_bias_grad[0],
        out_weight_grad,
        out_bias_grad,
        gain_grad,
        shift_grad,
        ffn_grads[None, :shard],
        ffn_grads[None, 2 * shard, :shard],
        ffn_grads[None, shard : 2 * shard],
        ffn_out_bias_grad,
    )


def solution(mesh):
    both = ("grp", "wide")
    return jax.shard_map(
        functools.partial(body, mesh.shape["wide"]),
        mesh=mesh,
        in_specs=(
            P(both, None),
            P(both),
            P(both),
            P(),
            P(),
            P(),
            P(),
            P(),
            P(),
            P(),
            P(),
            P(),
            P(),
            P("grp", "wide", None),
            P("grp", "wide"),
            P("grp", "wide", None),
            P("grp", None),
            P(both, None),
        ),
        out_specs=(
            P(both, None),
            P(both, None),
            P(),
            P(),
            P(),
            P(),
            P(),
            P(),
            P(),
            P(),
            P(),
            P(),
            P("grp", "wide", None),
            P("grp", "wide"),
            P("grp", "wide", None),
            P("grp", None),
        ),
        check_vma=False,
    )
```

```python
import functools
import jax
import jax.numpy as jnp
from jax import lax
from jax.experimental import pallas as pl
from jax.experimental.pallas import tpu as pltpu
from jax.sharding import PartitionSpec as P

HEADS = 6
HEAD = 64
KERNEL = 9
EDGE = 4
BLOCK = 512
SHORT = 128
CHUNKS = BLOCK // SHORT
WIDTH = HEADS * HEAD
DIM = 2 * WIDTH
SLAB = 128
TAPS = KERNEL * SLAB
HALO = 8
PADDED = SHORT + 2 * HALO
EPSILON = 1e-12
BF = jnp.bfloat16
F32 = jnp.float32
LIMITS = dict(
    project=60,
    attend=24,
    middle=60,
    ffn_grad=60,
    attend_back=44,
    conv_back=60,
    hidden_back=60,
    unpack=24,
)


def mm(a, b):
    return lax.dot_general(a, b, (((1,), (0,)), ((), ())), preferred_element_type=F32)


def mm_nt(a, b):
    return lax.dot_general(a, b, (((1,), (1,)), ((), ())), preferred_element_type=F32)


def mm_tn(a, b):
    return lax.dot_general(a, b, (((0,), (0,)), ((), ())), preferred_element_type=F32)


def col_sum(v):
    return jnp.sum(v, axis=0, keepdims=True)


def params(mebibytes):
    return pltpu.CompilerParams(vmem_limit_bytes=mebibytes * 1024 * 1024)


def whole(shape):
    return pl.BlockSpec(shape, lambda *_: (0,) * len(shape))


def rows(tile, width, lane=0):
    return pl.BlockSpec((tile, width), lambda i, *_: (i, lane))


def cost(micros):
    return pl.CostEstimate(flops=int(micros * 1e7), bytes_accessed=int(micros * 3e4), transcendentals=0)


def sds(shape, dtype):
    return jax.ShapeDtypeStruct(shape, dtype)


def fill_padded(pad_ref, values, joined):
    zero = jnp.zeros((HALO, SLAB), F32)
    for c in range(values.shape[1] // SLAB):
        lanes = slice(c * SLAB, (c + 1) * SLAB)
        for s in range(CHUNKS):
            lo, hi = s * SHORT, (s + 1) * SHORT
            pad_ref[c, s, HALO : HALO + SHORT, :] = values[lo:hi, lanes]
            pad_ref[c, s, 0:HALO, :] = values[lo - HALO : lo, lanes] * joined if s else zero
            pad_ref[c, s, HALO + SHORT :, :] = (
                values[hi : hi + HALO, lanes] * joined if s < CHUNKS - 1 else zero
            )


def padded(width):
    return pltpu.VMEM((width // SLAB, CHUNKS, PADDED, SLAB), F32)


def moved(pad_ref, offset, c):
    at = HALO + offset
    return pad_ref[c, :, at : at + SHORT, :].reshape(BLOCK, SLAB)


def add_taps(acc, weight, pad_ref, offset):
    parts = [
        weight[:, c * SLAB : (c + 1) * SLAB] * moved(pad_ref, offset, c)
        for c in range(weight.shape[1] // SLAB)
    ]
    return parts if acc is None else [u + v for u, v in zip(acc, parts)]


def slab_select(rows_of):
    source = lax.broadcasted_iota(jnp.int32, (rows_of, TAPS), 0)
    target = lax.broadcasted_iota(jnp.int32, (rows_of, TAPS), 1)
    head = target % SLAB
    hit = (head < HEADS) & (source == head * KERNEL + target // SLAB)
    return hit.astype(F32)


def head_spread():
    source = lax.broadcasted_iota(jnp.int32, (SLAB, WIDTH), 0)
    target = lax.broadcasted_iota(jnp.int32, (SLAB, WIDTH), 1)
    return (source == target // HEAD).astype(BF)


def norm_stats(v):
    mean = jnp.mean(v, axis=-1, keepdims=True)
    centred = v - mean
    var = jnp.mean(centred * centred, axis=-1, keepdims=True)
    inv = lax.rsqrt(var + EPSILON)
    return centred * inv, inv


def norm_back(d_scaled, hat, inv):
    first = jnp.mean(d_scaled, axis=-1, keepdims=True)
    second = jnp.mean(d_scaled * hat, axis=-1, keepdims=True)
    return inv * (d_scaled - first - hat * second)


def normal_cdf(v):
    density = jnp.exp2(v * v * -0.7213475204444817 - 1.3257480647361595)
    return 0.5 + 0.5 * lax.erf(v * 0.7071067811865476), density


def project_kernel(
    bucket, x, w, bias, dw, pw, kw, kb, qkvc, dep, kc, ks, co, xpad, cvpad
):
    joined = jnp.where(bucket[pl.program_id(0)] == 0, 1.0, 0.0).astype(F32)
    xb = x[...]
    proj = mm(xb, w[...])
    q = (proj[:, :WIDTH] + bias[0:1, :]).astype(BF)
    qkvc[:, 0:WIDTH] = q
    qkvc[:, WIDTH : 2 * WIDTH] = proj[:, WIDTH : 2 * WIDTH].astype(BF)
    qkvc[:, 2 * WIDTH : 3 * WIDTH] = (
        proj[:, 2 * WIDTH : 3 * WIDTH] + bias[1:2, :]
    ).astype(BF)
    cv = (proj[:, 3 * WIDTH :] + bias[2:3, :]).astype(BF)
    qkvc[:, 3 * WIDTH :] = cv
    fill_padded(xpad, xb.astype(F32), joined)
    fill_padded(cvpad, cv.astype(F32), joined)
    for c in range(DIM // SLAB):
        lanes = slice(c * SLAB, (c + 1) * SLAB)
        acc = moved(xpad, -EDGE, c) * dw[0:1, lanes]
        for j in range(1, KERNEL):
            acc += moved(xpad, j - EDGE, c) * dw[j : j + 1, lanes]
        dep[:, lanes] = acc.astype(BF)
    key_conv = mm(dep[...], pw[...]) + bias[3:4, :]
    kc[...] = key_conv
    conv_in = (key_conv * q.astype(F32)).astype(BF)
    select = slab_select(HEADS * KERNEL)
    kw_slab = mm_tn(kw[...], select.astype(BF)).astype(BF)
    kb_slab = jnp.dot(
        jnp.broadcast_to(kb[...], (8, HEADS * KERNEL)),
        select,
        precision=lax.Precision.HIGHEST,
        preferred_element_type=F32,
    )[0:1]
    logits = mm(conv_in, kw_slab) + kb_slab
    slabs = [logits[:, j * SLAB : (j + 1) * SLAB] for j in range(KERNEL)]
    top = functools.reduce(jnp.maximum, slabs)
    slabs = [jnp.exp(v - top) for v in slabs]
    inv = 1.0 / functools.reduce(jnp.add, slabs)
    for j in range(KERNEL):
        ks[:, j * SLAB : (j + 1) * SLAB] = (slabs[j] * inv).astype(BF)
    spread = head_spread()
    acc = None
    for j in range(KERNEL):
        weight = mm(ks[:, j * SLAB : (j + 1) * SLAB], spread)
        acc = add_taps(acc, weight, cvpad, j - EDGE)
    co[...] = jnp.concatenate(acc, axis=1).astype(BF)


def project(bucket, x, in_weight, in_bias, depth_weight, point_weight, kernel_weight, kernel_bias):
    count = x.shape[0]
    blocks = count // BLOCK
    taps = HEADS * KERNEL
    return pl.pallas_call(
        project_kernel,
        grid_spec=pltpu.PrefetchScalarGridSpec(
            num_scalar_prefetch=1,
            grid=(blocks,),
            in_specs=[
                rows(BLOCK, DIM),
                whole((DIM, 4 * WIDTH)),
                whole((4, WIDTH)),
                whole((KERNEL, DIM)),
                whole((DIM, WIDTH)),
                whole((taps, WIDTH)),
                whole((1, taps)),
            ],
            out_specs=[
                rows(BLOCK, 4 * WIDTH),
                rows(BLOCK, DIM),
                rows(BLOCK, WIDTH),
                rows(BLOCK, TAPS),
                rows(BLOCK, WIDTH),
            ],
            scratch_shapes=[
                padded(DIM),
                padded(WIDTH),
            ],
        ),
        out_shape=[
            sds((count, 4 * WIDTH), BF),
            sds((count, DIM), BF),
            sds((count, WIDTH), F32),
            sds((count, TAPS), BF),
            sds((count, WIDTH), BF),
        ],
        compiler_params=params(LIMITS["project"]),
        cost_estimate=cost(17),
        name="project",
    )(bucket, x, in_weight, in_bias, depth_weight, point_weight, kernel_weight, kernel_bias)


def mask_bias(is_short, valid_row):
    column = jnp.transpose(jnp.broadcast_to(valid_row.astype(F32), (SLAB, BLOCK)))
    column = jnp.concatenate([column] * (BLOCK // SLAB), axis=1)
    key_slot = (lax.broadcasted_iota(jnp.int32, (BLOCK, BLOCK), 0) // SHORT) * is_short
    query_slot = (lax.broadcasted_iota(jnp.int32, (BLOCK, BLOCK), 1) // SHORT) * is_short
    return jnp.where((key_slot == query_slot) & (column > 0.0), 0.0, -1e30)


def half_mask(v, h):
    lane = lax.broadcasted_iota(jnp.int32, v.shape, 1)
    keep = lane < HEAD if h % 2 == 0 else lane >= HEAD
    return jnp.where(keep, v, jnp.zeros_like(v))


def attend_kernel(
    bucket, valid, q, k, v, co, x, w_out, b_out, gain, shift,
    mixed, weights, scale, hat, inv, xin, bias, context,
):
    bias[...] = mask_bias(bucket[pl.program_id(0)], valid[...].reshape(1, BLOCK))
    vt = jnp.transpose(v[...])
    scale[...] = jnp.zeros_like(scale)
    for h in range(HEADS):
        lo = (h // 2) * SLAB
        qm = half_mask(q[:, lo : lo + SLAB], h) * jnp.asarray(HEAD**-0.5, BF)
        scores = mm_nt(k[:, lo : lo + SLAB], qm) + bias[...]
        top = jnp.max(scores, axis=0, keepdims=True)
        e = jnp.exp(scores - top)
        inverse = 1.0 / jnp.sum(e, axis=0, keepdims=True)
        weights[0, h] = e.astype(BF)
        part = mm(vt[h * HEAD : (h + 1) * HEAD], weights[0, h])
        context[h * HEAD : (h + 1) * HEAD, :] = part * inverse
        scale[0, h : h + 1, :] = inverse
    mixed[:, :WIDTH] = jnp.transpose(context[...]).astype(BF)
    mixed[:, WIDTH:] = co[...]
    att = mm(mixed[...], w_out[...]) + b_out[...] + x[...].astype(F32)
    scaled, stat = norm_stats(att)
    hat[...] = scaled
    inv[...] = jnp.broadcast_to(stat, inv.shape)
    xin[...] = (scaled * gain[0:1, :] + shift[0:1, :]).astype(BF)


def attend(bucket, valid, qkvc, conv_out, x, out_weight, out_bias, gain, shift):
    count = qkvc.shape[0]
    blocks = count // BLOCK
    return pl.pallas_call(
        attend_kernel,
        grid_spec=pltpu.PrefetchScalarGridSpec(
            num_scalar_prefetch=1,
            grid=(blocks,),
            in_specs=[
                pl.BlockSpec((1, 1, BLOCK), lambda i, *_: (i, 0, 0)),
                rows(BLOCK, WIDTH, 0),
                rows(BLOCK, WIDTH, 1),
                rows(BLOCK, WIDTH, 2),
                rows(BLOCK, WIDTH),
                rows(BLOCK, DIM),
                whole((DIM, DIM)),
                whole((1, DIM)),
                whole((2, DIM)),
                whole((2, DIM)),
            ],
            out_specs=[
                rows(BLOCK, DIM),
                pl.BlockSpec((1, HEADS, BLOCK, BLOCK), lambda i, *_: (i, 0, 0, 0)),
                pl.BlockSpec((1, 8, BLOCK), lambda i, *_: (i, 0, 0)),
                rows(BLOCK, DIM),
                rows(BLOCK, SLAB),
                rows(BLOCK, DIM),
            ],
            scratch_shapes=[
                pltpu.VMEM((BLOCK, BLOCK), F32),
                pltpu.VMEM((WIDTH, BLOCK), F32),
            ],
        ),
        out_shape=[
            sds((count, DIM), BF),
            sds((blocks, HEADS, BLOCK, BLOCK), BF),
            sds((blocks, 8, BLOCK), F32),
            sds((count, DIM), F32),
            sds((count, SLAB), F32),
            sds((count, DIM), BF),
        ],
        compiler_params=params(LIMITS["attend"]),
        cost_estimate=cost(14),
        name="attend",
    )(bucket, valid, qkvc, qkvc, qkvc, conv_out, x, out_weight, out_bias, gain, shift)


PARTS = 4


def unpack_weights(packs, w1, w2, bias_blocks, sems, g, shard, per):
    copies = []
    for k, pack in enumerate(packs):
        at = pl.ds(k * per, per)
        for n, (lo, size, dst) in enumerate(
            ((0, shard, w1), (shard, shard, w2), (2 * shard, 16, bias_blocks))
        ):
            copies.append(
                pltpu.make_async_copy(
                    pack.at[:, pl.ds(lo, size), :], dst.at[g, at], sems.at[g, k, n]
                )
            )
    return copies


def middle_kernel(
    group, *refs, shard, size
):
    hidden = shard * size
    packs, refs = refs[: 2 * PARTS], refs[2 * PARTS :]
    (
        hat1, inv1, xin, mixed, grad, w_out, gain, shift, b2,
        output, d_att, d_mixed, dback, act_a, dpre_a, sums, sums_a, grads_b, keep, send,
        ffn_out, d_summed, slope, datt_low, bias_sum, out_acc, w1s, w2s, blocks_s, b1s, sems,
        act_all, dpre_all, xin_all, dback_all, sums_b,
    ) = refs
    tile = xin.shape[0]
    here = pl.ds(pl.multiple_of(pl.program_id(0) * tile, tile), tile)
    act_b, dpre_b = act_all.at[here], dpre_all.at[here]
    own = pl.multiple_of(group[0] * WIDTH, SLAB)
    other = pl.multiple_of((1 - group[0]) * WIDTH, SLAB)
    part = 512
    step = pl.program_id(0)
    copies = [
        unpack_weights(
            packs[g * PARTS : (g + 1) * PARTS], w1s, w2s, blocks_s, sems, g, shard, size // PARTS
        )
        for g in range(2)
    ]

    @pl.when(step == 0)
    def _():
        for c in copies[0] + copies[1]:
            c.start()

    @pl.when(step == 0)
    def _():
        sums[...] = jnp.zeros_like(sums)
        bias_sum[...] = jnp.zeros_like(bias_sum)
        out_acc[...] = jnp.zeros_like(out_acc)

    def weights(g):
        return (
            w1s.at[g].reshape(hidden, WIDTH),
            w2s.at[g].reshape(hidden, WIDTH),
            b1s.at[g],
        )

    for g, base, act, at in ((0, own, act_a, 0), (1, other, act_b, hidden)):

        @pl.when(step == 0)
        def _():
            for c in copies[g]:
                c.wait()
            for r in range(size):
                row = blocks_s[g, r].astype(F32)[0:1, :shard]
                b1s[g, 0:1, r * shard : (r + 1) * shard] = row

        w1, w2, b1 = weights(g)
        xg = xin[:, pl.ds(base, WIDTH)]
        for lo in range(0, hidden, part):
            pre = mm_nt(xg, w1[lo : lo + part, :]) + b1[0:1, lo : lo + part]
            cdf, bell = normal_cdf(pre)
            act[:, lo : lo + part] = (pre * cdf).astype(BF)
            slope[:, at + lo : at + lo + part] = (cdf + pre * bell).astype(BF)
        ffn_out[:, pl.ds(base, WIDTH)] = mm(act[...], w2[...])
    result = (ffn_out[...] + b2[...]).astype(BF).astype(F32)
    hat2, inv2 = norm_stats(result + (hat1[...] * gain[0:1, :] + shift[0:1, :]))
    output[...] = (hat2 * gain[1:2, :] + shift[1:2, :]).astype(BF)
    dy = grad[...].astype(F32)
    sums[1:2, :] += col_sum(dy * hat2)
    sums[3:4, :] += col_sum(dy)
    ds = norm_back(dy * gain[1:2, :], hat2, inv2)
    d_summed[...] = ds
    low = ds.astype(BF)
    dback[...] = low
    xin_all[here, :] = xin[:, pl.ds(other, WIDTH)]
    dback_all[here, :] = dback[:, pl.ds(other, WIDTH)]
    sums[5:6, :] += col_sum(low.astype(F32))
    for g, base, dpre, at in ((0, own, dpre_a, 0), (1, other, dpre_b, hidden)):
        w1, w2, b1 = weights(g)
        dg = dback[:, pl.ds(base, WIDTH)]
        for lo in range(0, hidden, part):
            dp = mm_nt(dg, w2[lo : lo + part, :]) * slope[:, at + lo : at + lo + part].astype(F32)
            bias_sum[g : g + 1, lo : lo + part] += col_sum(dp)
            dpre[:, lo : lo + part] = dp.astype(BF)
        ffn_out[:, pl.ds(base, WIDTH)] = mm(dpre[...], w1[...])
    dn = d_summed[...] + ffn_out[...].astype(BF).astype(F32)
    hat = hat1[...]
    sums[0:1, :] += col_sum(dn * hat)
    sums[2:3, :] += col_sum(dn)
    da = norm_back(dn * gain[0:1, :], hat, inv1[:, 0:1])
    d_att[...] = da
    sums[4:5, :] += col_sum(da)
    datt_low[...] = da.astype(BF)
    d_mixed[...] = mm_nt(datt_low[...], w_out[...]).astype(BF)
    out_acc[...] += mm_tn(mixed[...], datt_low[...])

    @pl.when(step == pl.num_programs(0) - 1)
    def _():
        split_halves(group[0], out_acc, keep, send)
        for g, dst in ((0, sums_a), (1, sums_b)):
            dst[...] = jnp.zeros_like(dst)
            for r in range(size):
                dst[r, 0:1, 0:shard] = bias_sum[g : g + 1, r * shard : (r + 1) * shard]
        quarter, per = hidden // PARTS, size // PARTS
        for k in range(PARTS):
            lanes = slice(k * quarter, (k + 1) * quarter)
            write_pack(
                dpre_all[:, lanes], act_all[:, lanes], xin_all[...], dback_all[...],
                sums_b, grads_b, k * per, per, shard,
            )


def middle(group, packs, shard, size, hat, inv, xin, mixed, grad, out_weight, gain, shift, b2):
    count = xin.shape[0]
    hidden = shard * size
    tile = BLOCK // 2
    pack_shape = (size, 2 * shard + 16, WIDTH)
    sum_shape = (size, 8, WIDTH)
    return pl.pallas_call(
        functools.partial(middle_kernel, shard=shard, size=size),
        grid_spec=pltpu.PrefetchScalarGridSpec(
            num_scalar_prefetch=1,
            grid=(count // tile,),
            in_specs=[pl.BlockSpec(memory_space=pl.ANY)] * (2 * PARTS)
            + [
                rows(tile, DIM),
                rows(tile, SLAB),
                rows(tile, DIM),
                rows(tile, DIM),
                rows(tile, DIM),
                whole((DIM, DIM)),
                whole((2, DIM)),
                whole((2, DIM)),
                whole((1, DIM)),
            ],
            out_specs=[
                rows(tile, DIM),
                rows(tile, DIM),
                rows(tile, DIM),
                rows(tile, DIM),
                rows(tile, hidden),
                rows(tile, hidden),
                whole((8, DIM)),
                whole(sum_shape),
                whole(pack_shape),
                whole((WIDTH, DIM)),
                whole((WIDTH, DIM)),
            ],
            scratch_shapes=[
                pltpu.VMEM((tile, DIM), F32),
                pltpu.VMEM((tile, DIM), F32),
                pltpu.VMEM((tile, 2 * hidden), BF),
                pltpu.VMEM((tile, DIM), BF),
                pltpu.VMEM((8, hidden), F32),
                pltpu.VMEM((DIM, DIM), F32),
                pltpu.VMEM((2, size, shard, WIDTH), BF),
                pltpu.VMEM((2, size, shard, WIDTH), BF),
                pltpu.VMEM((2, size, 16, WIDTH), BF),
                pltpu.VMEM((2, 8, hidden), F32),
                pltpu.SemaphoreType.DMA((2, PARTS, 3)),
                pltpu.VMEM((count, hidden), BF),
                pltpu.VMEM((count, hidden), BF),
                pltpu.VMEM((count, WIDTH), BF),
                pltpu.VMEM((count, WIDTH), BF),
                pltpu.VMEM(sum_shape, F32),
            ],
        ),
        out_shape=[
            sds((count, DIM), BF),
            sds((count, DIM), F32),
            sds((count, DIM), BF),
            sds((count, DIM), BF),
            sds((count, hidden), BF),
            sds((count, hidden), BF),
            sds((8, DIM), F32),
            sds(sum_shape, F32),
            sds(pack_shape, BF),
            sds((WIDTH, DIM), BF),
            sds((WIDTH, DIM), BF),
        ],
        compiler_params=params(LIMITS["middle"]),
        cost_estimate=cost(38),
        name="middle",
    )(group, *packs, hat, inv, xin, mixed, grad, out_weight, gain, shift, b2)


def write_pack(dpre, act, xin, dback, sums, out, first_block, per, shard):
    first = mm_tn(dpre, xin).astype(BF)
    second = mm_tn(act, dback).astype(BF)
    for z in range(per):
        out[first_block + z, 0:shard, :] = first[z * shard : (z + 1) * shard]
        out[first_block + z, shard : 2 * shard, :] = second[z * shard : (z + 1) * shard]
        row = jnp.concatenate([sums[first_block + z], jnp.zeros((8, WIDTH), F32)], axis=0)
        out[first_block + z, 2 * shard :, :] = row.astype(BF)


def ffn_grad_kernel(group, dpre, act, xin, dback, sums, out, *, shard):
    write_pack(
        dpre[...], act[...], xin[...], dback[...], sums, out, 0, out.shape[0], shard
    )


def ffn_grad(group, dpre, act, xin, dback, sums, shard, size):
    count, hidden = dpre.shape
    tile = hidden // PARTS
    per = size // PARTS
    lanes = pl.BlockSpec((count, tile), lambda i, g: (0, i))
    side = pl.BlockSpec((count, WIDTH), lambda i, g: (0, g[0]))
    return pl.pallas_call(
        functools.partial(ffn_grad_kernel, shard=shard),
        grid_spec=pltpu.PrefetchScalarGridSpec(
            num_scalar_prefetch=1,
            grid=(PARTS,),
            in_specs=[
                lanes, lanes, side, side, pl.BlockSpec((per, 8, WIDTH), lambda i, g: (i, 0, 0)),
            ],
            out_specs=pl.BlockSpec((per, 2 * shard + 16, WIDTH), lambda i, g: (i, 0, 0)),
        ),
        out_shape=sds((size, 2 * shard + 16, WIDTH), BF),
        compiler_params=params(LIMITS["ffn_grad"]),
        cost_estimate=cost(7),
        name="ffn_grad",
    )(group, dpre, act, xin, dback, sums)


def repack(packs, size, shard):
    old = (packs.shape[1] - 16) // 2
    first = packs[:, :old].reshape(size, shard, WIDTH)
    second = packs[:, old : 2 * old].reshape(size, shard, WIDTH)
    bias = packs[:, 2 * old, :old].reshape(size, 1, shard)
    bias = jnp.pad(bias, ((0, 0), (0, 15), (0, WIDTH - shard)))
    return jnp.concatenate([first, second, bias], axis=1)


def attend_back_kernel(info, weights, scale, q, k, v, dctx, x, dq, dkv, sums, keep, send, dqt, acc):
    step = pl.program_id(0)

    @pl.when(step == 0)
    def _():
        sums[...] = jnp.zeros_like(sums)
        acc[...] = jnp.zeros_like(acc)

    root = jnp.asarray(HEAD**-0.5, BF)
    kt = jnp.transpose(k[...] * root)
    for pair in range(HEADS // 2):
        lo = pair * SLAB
        vp = v[:, lo : lo + SLAB]
        dk = dv = None
        for h in (2 * pair, 2 * pair + 1):
            qm = half_mask(q[:, lo : lo + SLAB], h) * root
            cm = half_mask(dctx[:, lo : lo + SLAB], h)
            probs = weights[0, h].astype(F32) * scale[0, h : h + 1, :]
            d_probs = mm_nt(vp, cm)
            delta = col_sum(probs * d_probs)
            d_scores = (probs * (d_probs - delta)).astype(BF)
            probs = probs.astype(BF)
            dv = mm(probs, cm) if dv is None else dv + mm(probs, cm)
            dk = mm(d_scores, qm) if dk is None else dk + mm(d_scores, qm)
            dqt[h * HEAD : (h + 1) * HEAD, :] = mm(kt[h * HEAD : (h + 1) * HEAD], d_scores)
        dkv[:, lo : lo + SLAB] = dk.astype(BF)
        dkv[:, WIDTH + lo : WIDTH + lo + SLAB] = dv.astype(BF)
        sums[0:1, lo : lo + SLAB] += col_sum(dv)
    dq[...] = jnp.transpose(dqt[...])
    acc[...] += mm_tn(x[...], dkv[...])

    @pl.when(step == pl.num_programs(0) - 1)
    def _():
        split_halves(info[0], acc, keep, send)


def split_halves(core, total, keep, send):
    half = total.shape[0] // 2
    keep[...] = total[pl.ds(pl.multiple_of(core * half, 8), half), :].astype(BF)
    send[...] = total[pl.ds(pl.multiple_of((1 - core) * half, 8), half), :].astype(BF)


def attend_back(info, weights, scale, qkvc, d_mixed, x):
    count = qkvc.shape[0]
    blocks = count // BLOCK
    return pl.pallas_call(
        attend_back_kernel,
        grid_spec=pltpu.PrefetchScalarGridSpec(
            num_scalar_prefetch=1,
            grid=(blocks,),
            in_specs=[
                pl.BlockSpec((1, HEADS, BLOCK, BLOCK), lambda i, *_: (i, 0, 0, 0)),
                pl.BlockSpec((1, 8, BLOCK), lambda i, *_: (i, 0, 0)),
                rows(BLOCK, WIDTH, 0),
                rows(BLOCK, WIDTH, 1),
                rows(BLOCK, WIDTH, 2),
                rows(BLOCK, WIDTH, 0),
                rows(BLOCK, DIM),
            ],
            out_specs=[
                rows(BLOCK, WIDTH),
                rows(BLOCK, DIM),
                whole((8, WIDTH)),
                whole((WIDTH, DIM)),
                whole((WIDTH, DIM)),
            ],
            scratch_shapes=[
                pltpu.VMEM((WIDTH, BLOCK), F32),
                pltpu.VMEM((DIM, DIM), F32),
            ],
        ),
        out_shape=[
            sds((count, WIDTH), F32),
            sds((count, DIM), BF),
            sds((8, WIDTH), F32),
            sds((WIDTH, DIM), BF),
            sds((WIDTH, DIM), BF),
        ],
        compiler_params=params(LIMITS["attend_back"]),
        cost_estimate=cost(16),
        name="attend_back",
    )(info, weights, scale, qkvc, qkvc, qkvc, d_mixed, x)


POINT_ROW = DIM
SMALL_ROW = DIM + WIDTH
LATE_ROWS = DIM + WIDTH + 128
NORM_ROW = SMALL_ROW + 64
TAP_ROW = SMALL_ROW + 72


def conv_back_kernel(
    info, q, cv, dconv, kc, ks, dq, x, dep, kw, pw, sums_mid, sums_v, dqc, dkc, keep, send,
    cvpad, dcpad, kspad, xpad, dk_slab, dlog, qc_acc, pt_acc, kw_acc, kb_acc, dw_acc, sums, flat
):
    step = pl.program_id(0)
    taps = HEADS * KERNEL

    @pl.when(step == 0)
    def _():
        for ref in (qc_acc, pt_acc, kw_acc, kb_acc, dw_acc, sums):
            ref[...] = jnp.zeros_like(ref)

    joined = jnp.where(info[1 + step] == 0, 1.0, 0.0).astype(F32)
    dc = dconv[...].astype(F32)
    fill_padded(cvpad, cv[...].astype(F32), joined)
    fill_padded(dcpad, dc, joined)
    fill_padded(kspad, ks[...].astype(F32), joined)
    fill_padded(xpad, x[...].astype(F32), joined)
    spread = head_spread()
    total = None
    for j in range(KERNEL):
        product = jnp.concatenate(add_taps(None, dc, cvpad, j - EDGE), axis=1)
        part = mm_nt(product.astype(BF), spread)
        dk_slab[:, j * SLAB : (j + 1) * SLAB] = part
        part = part * ks[:, j * SLAB : (j + 1) * SLAB].astype(F32)
        total = part if total is None else total + part
    for j in range(KERNEL):
        lanes = slice(j * SLAB, (j + 1) * SLAB)
        grad = ks[:, lanes].astype(F32) * (dk_slab[:, lanes] - total)
        kb_acc[0:1, lanes] += col_sum(grad)
        dlog[:, lanes] = grad.astype(BF)
    acc = None
    for j in range(KERNEL):
        weight = mm(moved(kspad, EDGE - j, j).astype(BF), spread)
        acc = add_taps(acc, weight, dcpad, EDGE - j)
    acc = jnp.concatenate(acc, axis=1)
    dqc[:, WIDTH:] = acc.astype(BF)
    sums[1:2, :] += col_sum(acc)
    select = slab_select(taps)
    compact = mm_nt(dlog[...], select.astype(BF)).astype(BF)
    qf = q[...].astype(F32)
    key_conv = kc[...]
    conv_in = (key_conv * qf).astype(BF)
    kw_acc[0:taps, :] += mm_tn(compact, conv_in)
    d_conv_in = mm(compact, kw[...])
    d_key = d_conv_in * qf
    sums[2:3, :] += col_sum(d_key)
    dkc[...] = d_key.astype(BF)
    dq_all = dq[...] + d_conv_in * key_conv
    sums[0:1, :] += col_sum(dq_all)
    dqc[:, :WIDTH] = dq_all.astype(BF)
    qc_acc[...] += mm_tn(x[...], dqc[...])
    pt_acc[...] += mm_tn(dep[...], dkc[...])
    d_depth = mm_nt(dkc[...], pw[...])
    for c in range(DIM // SLAB):
        lanes = slice(c * SLAB, (c + 1) * SLAB)
        here = d_depth[:, lanes]
        for j in range(KERNEL):
            dw_acc[j : j + 1, lanes] += col_sum(moved(xpad, j - EDGE, c) * here)

    @pl.when(step == pl.num_programs(0) - 1)
    def _():
        flat[0:DIM, :] = qc_acc[...].astype(BF)
        flat[POINT_ROW:SMALL_ROW, 0:WIDTH] = pt_acc[0:WIDTH, :].astype(BF)
        flat[POINT_ROW:SMALL_ROW, WIDTH:] = pt_acc[WIDTH:, :].astype(BF)
        flat[SMALL_ROW : SMALL_ROW + 64, 0:WIDTH] = kw_acc[...].astype(BF)
        kb = lax.dot_general(
            kb_acc[...],
            select,
            (((1,), (1,)), ((), ())),
            precision=lax.Precision.HIGHEST,
            preferred_element_type=F32,
        )
        blank = jnp.zeros((4, WIDTH), F32)
        rows_of = jnp.concatenate([sums[0:1], sums_v[0:1], sums[1:3], blank], axis=0)
        kb = jnp.concatenate([kb, jnp.zeros((8, WIDTH - taps), F32)], axis=1)
        flat[SMALL_ROW : SMALL_ROW + 16, WIDTH:] = jnp.concatenate([rows_of, kb], axis=0).astype(BF)
        flat[SMALL_ROW + 16 : NORM_ROW, WIDTH:] = jnp.zeros((48, WIDTH), BF)
        flat[NORM_ROW : NORM_ROW + 32, :] = jnp.concatenate(
            [sums_mid[...], dw_acc[...], jnp.zeros((8, DIM), F32)], axis=0
        ).astype(BF)
        flat[NORM_ROW + 32 :, :] = jnp.zeros((32, DIM), BF)
        half = LATE_ROWS // 2
        core = info[0]
        keep[...] = flat[pl.ds(pl.multiple_of(core * half, 16), half), :]
        send[...] = flat[pl.ds(pl.multiple_of((1 - core) * half, 16), half), :]


def conv_back(info, qkvc, d_mixed, kc, ks, dq, x, dep, kernel_weight, point_weight, sums_mid, sums_v):
    count = qkvc.shape[0]
    blocks = count // BLOCK
    taps = HEADS * KERNEL
    half = LATE_ROWS // 2
    return pl.pallas_call(
        conv_back_kernel,
        grid_spec=pltpu.PrefetchScalarGridSpec(
            num_scalar_prefetch=1,
            grid=(blocks,),
            in_specs=[
                rows(BLOCK, WIDTH, 0),
                rows(BLOCK, WIDTH, 3),
                rows(BLOCK, WIDTH, 1),
                rows(BLOCK, WIDTH),
                rows(BLOCK, TAPS),
                rows(BLOCK, WIDTH),
                rows(BLOCK, DIM),
                rows(BLOCK, DIM),
                whole((taps, WIDTH)),
                whole((DIM, WIDTH)),
                whole((8, DIM)),
                whole((8, WIDTH)),
            ],
            out_specs=[
                rows(BLOCK, DIM),
                rows(BLOCK, WIDTH),
                whole((half, DIM)),
                whole((half, DIM)),
            ],
            scratch_shapes=[
                padded(WIDTH),
                padded(WIDTH),
                padded(TAPS),
                padded(DIM),
                pltpu.VMEM((BLOCK, TAPS), F32),
                pltpu.VMEM((BLOCK, TAPS), BF),
                pltpu.VMEM((DIM, DIM), F32),
                pltpu.VMEM((DIM, WIDTH), F32),
                pltpu.VMEM((64, WIDTH), F32),
                pltpu.VMEM((8, TAPS), F32),
                pltpu.VMEM((16, DIM), F32),
                pltpu.VMEM((8, WIDTH), F32),
                pltpu.VMEM((LATE_ROWS, DIM), BF),
            ],
        ),
        out_shape=[
            sds((count, DIM), BF),
            sds((count, WIDTH), BF),
            sds((half, DIM), BF),
            sds((half, DIM), BF),
        ],
        compiler_params=params(LIMITS["conv_back"]),
        cost_estimate=cost(22),
        name="conv_back",
    )(info, qkvc, qkvc, d_mixed, kc, ks, dq, x, dep, kernel_weight, point_weight, sums_mid, sums_v)


def hidden_kernel(info, dkc, d_att, dqc, dkv, dw, pw, w, *refs, start):
    hidden, ddpad = refs[-2:]
    joined = jnp.where(info[1 + start + pl.program_id(0)] == 0, 1.0, 0.0).astype(F32)
    fill_padded(ddpad, mm_nt(dkc[...], pw[...]), joined)
    hidden[...] = (
        d_att[...]
        + mm_nt(dkv[...], w[:, WIDTH : 3 * WIDTH])
        + mm_nt(dqc[:, :WIDTH], w[:, :WIDTH])
        + mm_nt(dqc[:, WIDTH:], w[:, 3 * WIDTH :])
    )
    for c in range(DIM // SLAB):
        lanes = slice(c * SLAB, (c + 1) * SLAB)
        acc = hidden[:, lanes]
        for j in range(KERNEL):
            acc += moved(ddpad, EDGE - j, c) * dw[j : j + 1, lanes]
        hidden[:, lanes] = acc


def hidden_back(info, dkc, d_att, dqc, dkv, depth_weight, point_weight, in_weight, start, stop, before=None):
    count = d_att.shape[0]

    def part(width):
        return pl.BlockSpec((BLOCK, width), lambda i, *_: (i + start, 0))

    extra = [] if before is None else [before]
    return pl.pallas_call(
        functools.partial(hidden_kernel, start=start),
        grid_spec=pltpu.PrefetchScalarGridSpec(
            num_scalar_prefetch=1,
            grid=(stop - start,),
            in_specs=[
                part(WIDTH),
                part(DIM),
                part(DIM),
                part(DIM),
                whole((KERNEL, DIM)),
                whole((DIM, WIDTH)),
                whole((DIM, 4 * WIDTH)),
            ]
            + [pl.BlockSpec(memory_space=pl.ANY)] * len(extra),
            out_specs=part(DIM),
            scratch_shapes=[padded(DIM)],
        ),
        out_shape=sds((count, DIM), F32),
        input_output_aliases={8: 0} if extra else {},
        compiler_params=params(LIMITS["hidden_back"]),
        cost_estimate=cost(6),
        name="hidden_back",
    )(info, dkc, d_att, dqc, dkv, depth_weight, point_weight, in_weight, *extra)


def load_parts(parts, dst, sems, core, digit):
    count = dst.shape[0]
    copies = []
    per = max(len(parts) // 2, 1)
    size = count // len(parts)
    for n, part in enumerate(parts):
        c, k = n // per, n % per
        row = 0 if len(parts) == 1 else (core ^ c) * (count // 2) + (digit ^ k) * size * (per > 1)
        at = pl.ds(pl.multiple_of(row, 16), size)
        copies.append(pltpu.make_async_copy(part, dst.at[at, :], sems.at[n]))
    for c in copies:
        c.start()
    for c in copies:
        c.wait()


def unpack_early_kernel(info, *refs):
    parts, (in_w, out_w, early, sems) = refs[:-4], refs[-4:]
    step = pl.program_id(0)

    @pl.when(step == 0)
    def _():
        load_parts(parts, early, sems, info[0], info[1])
        out_w[0:WIDTH, :] = early[0:WIDTH, :].astype(F32)
        out_w[WIDTH:, :] = early[DIM : DIM + WIDTH, :].astype(F32)

    lanes = pl.ds(pl.multiple_of(step * WIDTH, SLAB), WIDTH)
    in_w[0:WIDTH, :] = early[WIDTH:DIM, lanes].astype(F32)
    in_w[WIDTH:, :] = early[DIM + WIDTH :, lanes].astype(F32)


def unpack_early(info, parts):
    return pl.pallas_call(
        unpack_early_kernel,
        grid_spec=pltpu.PrefetchScalarGridSpec(
            num_scalar_prefetch=1,
            grid=(2,),
            in_specs=[pl.BlockSpec(memory_space=pl.ANY)] * len(parts),
            out_specs=[
                pl.BlockSpec((DIM, WIDTH), lambda i, *_: (0, 1 + i)),
                whole((DIM, DIM)),
            ],
            scratch_shapes=[
                pltpu.VMEM((2 * DIM, DIM), BF),
                pltpu.SemaphoreType.DMA((len(parts),)),
            ],
        ),
        out_shape=[sds((DIM, 4 * WIDTH), F32), sds((DIM, DIM), F32)],
        compiler_params=params(LIMITS["unpack"]),
        cost_estimate=cost(3),
        name="unpack_early",
    )(info, *parts)


def unpack_late_kernel(info, *refs):
    parts, (_, in_w, in_b, dw, point, kw, kb, out_b, gain, shift, b2, late, sems) = (
        refs[:-13],
        refs[-13:],
    )
    step = pl.program_id(0)
    taps = HEADS * KERNEL

    @pl.when(step == 0)
    def _():
        load_parts(parts, late, sems, info[0], info[1])
        point[0:WIDTH, :] = late[POINT_ROW:SMALL_ROW, 0:WIDTH].astype(F32)
        point[WIDTH:, :] = late[POINT_ROW:SMALL_ROW, WIDTH:].astype(F32)
        kw[...] = late[SMALL_ROW : SMALL_ROW + 64, 0:WIDTH].astype(F32)[0:taps]
        mixed = late[SMALL_ROW : SMALL_ROW + 16, WIDTH:].astype(F32)
        in_b[...] = mixed[0:4]
        kb[...] = mixed[8:9, 0:taps]
        norms = late[NORM_ROW : NORM_ROW + 32, :].astype(F32)
        gain[...] = norms[0:2]
        shift[...] = norms[2:4]
        out_b[...] = norms[4]
        b2[...] = jnp.where(info[0] == 0, norms[5:6, 0:WIDTH], norms[5:6, WIDTH:])
        dw[...] = norms[8 : 8 + KERNEL]

    in_w[...] = late[0:DIM, pl.ds(pl.multiple_of(step * WIDTH, SLAB), WIDTH)].astype(F32)


def unpack_late(info, parts, in_w):
    taps = HEADS * KERNEL
    shapes = [
        (4, WIDTH), (KERNEL, DIM), (DIM, WIDTH), (taps, WIDTH), (1, taps), (DIM,), (2, DIM),
        (2, DIM), (1, WIDTH),
    ]
    return pl.pallas_call(
        unpack_late_kernel,
        grid_spec=pltpu.PrefetchScalarGridSpec(
            num_scalar_prefetch=1,
            grid=(2,),
            in_specs=[pl.BlockSpec(memory_space=pl.ANY)] * (len(parts) + 1),
            out_specs=[pl.BlockSpec((DIM, WIDTH), lambda i, *_: (0, 3 * i))]
            + [whole(v) for v in shapes],
            scratch_shapes=[
                pltpu.VMEM((LATE_ROWS, DIM), BF),
                pltpu.SemaphoreType.DMA((len(parts),)),
            ],
        ),
        out_shape=[sds((DIM, 4 * WIDTH), F32)] + [sds(v, F32) for v in shapes],
        input_output_aliases={1 + len(parts): 0},
        compiler_params=params(LIMITS["unpack"]),
        cost_estimate=cost(3),
        name="unpack_late",
    )(info, *parts, in_w)


def digit_groups(size):
    groups, shift = [], 0
    while (1 << shift) < size:
        bits = 2 if (4 << shift) <= size else 1
        groups.append((shift, 1 << bits))
        shift += bits
    return groups


def partner(value, size, distance):
    return lax.ppermute(value, "wide", [(i, i ^ distance) for i in range(size)])


def swap_core(value):
    return lax.ppermute(value, "grp", [(0, 1), (1, 0)])


def fence(*values):
    return lax.optimization_barrier(values)


def add_up(values, dtype=BF):
    total = values[0].astype(F32)
    for v in values[1:]:
        total = total + v.astype(F32)
    return total.astype(dtype)


def gather_relative(block, size):
    buf = block[None]
    for shift, count in reversed(digit_groups(size)):
        parts = [buf] + [partner(buf, size, k << shift) for k in range(1, count)]
        buf = jnp.concatenate(parts, axis=0)
    return buf


def scatter_relative(blocks, size):
    buf = blocks
    for shift, count in digit_groups(size):
        parts = buf.reshape((count, buf.shape[0] // count) + buf.shape[1:])
        buf = add_up([parts[0]] + [partner(parts[k], size, k << shift) for k in range(1, count)])
    return buf[0].astype(F32)


def take(array, index):
    return lax.dynamic_index_in_dim(array, index, 0, keepdims=False)


class Sum:
    def __init__(self, size, half, direct=False):
        self.size, self.value, self.direct = size, half, direct

    def digit(self, group):
        return (lax.axis_index("wide") >> group[0]) & (group[1] - 1)

    def swap(self, group, blocks):
        shift, count = group
        mask = (count - 1) << shift
        teams = [
            [i + (d << shift) for d in range(count)] for i in range(self.size) if not i & mask
        ]
        return [
            lax.all_to_all(
                blocks, "wide", split_axis=0, concat_axis=0, axis_index_groups=teams, tiled=True
            )
        ]

    def send(self, group):
        shift, count = group
        blocks = self.value.reshape(count, self.value.shape[0] // count, DIM)
        if not self.direct:
            self.parts = self.swap(group, blocks)
            return
        digit = self.digit(group)
        self.parts = [take(blocks, digit)] + [
            partner(take(blocks, digit ^ k), self.size, k << shift) for k in range(1, count)
        ]

    def reduce(self):
        if self.direct:
            self.value = add_up(self.parts)
        else:
            self.value = jnp.sum(self.parts[0].astype(F32), axis=0).astype(BF)

    def spread(self, group):
        shift, count = group
        if not self.direct:
            blocks = jnp.broadcast_to(self.value[None], (count,) + self.value.shape)
            self.parts = self.swap(group, blocks)
            return
        self.parts = [self.value] + [
            partner(self.value, self.size, k << shift) for k in range(1, count)
        ]

    def join(self, group):
        if not self.direct:
            self.value = self.parts[0].reshape(-1, DIM)
            return
        digit = self.digit(group)
        stacked = jnp.stack(self.parts)
        self.value = jnp.concatenate([take(stacked, digit ^ d) for d in range(group[1])], axis=0)


def sum_everywhere(keep, send, size):
    core = lax.axis_index("grp")
    total = Sum(size, add_up([keep, swap_core(send)]))
    groups = digit_groups(size)
    for group in groups:
        total.send(group)
        total.reduce()
    for group in reversed(groups):
        total.spread(group)
        total.join(group)
    halves = jnp.stack([total.value, swap_core(total.value)])
    return jnp.concatenate([take(halves, core), take(halves, 1 - core)], axis=0)


def body(
    size,
    hidden_in,
    valid_mask,
    bucket,
    in_weight,
    in_bias,
    depth_weight,
    point_weight,
    kernel_weight,
    kernel_bias,
    out_weight,
    out_bias,
    norm_gain,
    norm_bias,
    ffn_in,
    ffn_in_bias,
    ffn_out,
    ffn_out_bias,
    out_grad,
):
    count = hidden_in.shape[0]
    blocks = count // BLOCK
    shard = ffn_in.shape[1]
    hidden = shard * size
    core = lax.axis_index("grp").astype(jnp.int32)
    group = jnp.reshape(core, (1,))
    info = jnp.concatenate([group, bucket])
    valid = valid_mask.reshape(blocks, 1, BLOCK)
    kernel_weight = kernel_weight.T
    groups = digit_groups(size)
    staged = len(groups) == 2 and groups[0][1] == groups[1][1] == PARTS and shard % 16 == 0

    bias_rows = jnp.pad(ffn_in_bias, ((0, 15), (0, WIDTH - shard)))
    pack = jnp.concatenate([ffn_in[0], ffn_out[0], bias_rows], axis=0)[None]
    other_bias = swap_core(ffn_out_bias)
    b2 = jnp.concatenate([ffn_out_bias, other_bias], axis=1)
    b2 = jnp.where(core == 0, b2, jnp.concatenate([other_bias, ffn_out_bias], axis=1))

    if staged:
        got = [partner(pack, size, k << groups[1][0]) for k in range(1, PARTS)]
    qkvc, dep, kc, ks, conv_out = project(
        bucket, hidden_in, in_weight, in_bias, depth_weight, point_weight, kernel_weight,
        kernel_bias[None],
    )
    if staged:
        *got, conv_out = fence(*got, conv_out)
        near = jnp.concatenate([pack] + got, axis=0)
        own = [near] + [partner(near, size, k) for k in range(1, PARTS)]
        near_other = swap_core(near)
        near_other, conv_out, info, b2 = fence(near_other, conv_out, info, b2)
    mixed, attn_weights, attn_scale, hat, inv, xin = attend(
        bucket, valid, qkvc, conv_out, hidden_in, out_weight, out_bias[None], norm_gain, norm_bias
    )
    if staged:
        *own, xin = fence(*own, xin)
        packs = own + [near_other] + [swap_core(v) for v in own[1:]]
    else:
        gathered = gather_relative(pack[0], size)
        packs = [
            pack[None]
            for v in (gathered, swap_core(gathered))
            for pack in repack(v, PARTS, hidden // PARTS)
        ]
    form = (shard, size) if staged else (hidden // PARTS, PARTS)
    (
        output, d_att, d_mixed, dback, act_a, dpre_a, sums, sums_a, grads_b, out_keep, out_send,
    ) = middle(
        group, packs, *form, hat, inv, xin, mixed, out_grad, out_weight, norm_gain, norm_bias, b2
    )
    from_core = swap_core(grads_b)
    grads_a = ffn_grad(group, dpre_a, act_a, xin, dback, sums_a, *form)
    grads_a, from_core, d_mixed = fence(grads_a, from_core, d_mixed)

    if not staged:
        ffn_grads = scatter_relative(
            repack(add_up([grads_a, from_core]), size, shard), size
        )
    else:
        per = size // PARTS
        xy, z = groups
        parts = [
            add_up([v[k * per : (k + 1) * per] for v in (grads_a, from_core)])
            for k in range(1, PARTS)
        ]
        *parts, d_mixed, out_send = fence(*parts, d_mixed, out_send)
        from_x, from_y = partner(parts[0], size, 1), partner(parts[1], size, 2)
        out_got = swap_core(out_send)
    dq, dkv, sums_v, kv_keep, kv_send = attend_back(
        info, attn_weights, attn_scale, qkvc, d_mixed, hidden_in
    )
    if staged:
        from_x, from_y, out_got, kv_send = fence(from_x, from_y, out_got, kv_send)
        kv_got = swap_core(kv_send)
        early = jnp.concatenate([add_up([out_keep, out_got]), add_up([kv_keep, kv_got])], axis=0)
        early = Sum(size, early, direct=True)
        early.value, dq = fence(early.value, dq)
        from_xy = partner(parts[2], size, 3)
        early.send(xy)
    dqc, dkc, late_keep, late_send = conv_back(
        info, qkvc, d_mixed, kc, ks, dq, hidden_in, dep, kernel_weight, point_weight, sums, sums_v
    )
    if staged:
        *early.parts, from_xy, late_send, dkc = fence(*early.parts, from_xy, late_send, dkc)
        late_got = swap_core(late_send)
        parts = [
            add_up([v[k] for v in (grads_a, from_core, from_x, from_y, from_xy)]) for k in range(PARTS)
        ]
        early.reduce()
        late = Sum(size, add_up([late_keep, late_got]))
        early.value, late.value, dkc = fence(early.value, late.value, dkc)
        late.send(xy)
        early.send(z)
    hidden_grad = hidden_back(
        info, dkc, d_att, dqc, dkv, depth_weight, point_weight, in_weight, 0, blocks
    )
    info = jnp.stack([core, lax.axis_index("wide").astype(jnp.int32) & (PARTS - 1)])
    if staged:
        late.parts[0], *early.parts, hidden_grad = fence(late.parts[0], *early.parts, hidden_grad)
        late.reduce()
        early.reduce()
        late.value, early.value = fence(late.value, early.value)
        late.send(z)
        early.spread(z)
        late.parts[0], *early.parts = fence(late.parts[0], *early.parts)
        late.reduce()
        early.join(z)
        early.value, late.value, *parts = fence(early.value, late.value, *parts)
        late.spread(z)
        early.spread(xy)
        from_z = [partner(parts[k], size, k << z[0]) for k in (1, 2)]
        late.parts[0], *rest = fence(late.parts[0], *early.parts, *from_z, parts[3])
        early.parts, from_z, last = rest[:PARTS], rest[PARTS : PARTS + 2], rest[-1]
        late.join(z)
        late.spread(xy)
        early_all = early.parts + [swap_core(v) for v in early.parts]
        from_z.append(partner(last, size, 3 << z[0]))
        in_weight_grad, out_weight_grad = unpack_early(info, early_all)
        late.parts[0], from_z[2], in_weight_grad = fence(late.parts[0], from_z[2], in_weight_grad)
        late.join(xy)
        late_all = [late.value, swap_core(late.value)]
        ffn_grads = add_up([parts[0]] + from_z, F32)
        late_all[1], ffn_grads = fence(late_all[1], ffn_grads)
    else:
        early_all = [
            sum_everywhere(
                jnp.concatenate([out_keep, kv_keep], axis=0),
                jnp.concatenate([out_send, kv_send], axis=0),
                size,
            )
        ]
        late_all = [sum_everywhere(late_keep, late_send, size)]
        in_weight_grad, out_weight_grad = unpack_early(info, early_all)
    (
        in_weight_grad, in_bias_grad, depth_weight_grad, point_weight_grad, kernel_weight_grad,
        kernel_bias_grad, out_bias_grad, gain_grad, shift_grad, ffn_out_bias_grad,
    ) = unpack_late(info, late_all, in_weight_grad)
    return (
        output,
        hidden_grad,
        in_weight_grad,
        in_bias_grad,
        depth_weight_grad,
        point_weight_grad,
        kernel_weight_grad.T,
        kernel_bias_grad[0],
        out_weight_grad,
        out_bias_grad,
        gain_grad,
        shift_grad,
        ffn_grads[None, :shard],
        ffn_grads[None, 2 * shard, :shard],
        ffn_grads[None, shard : 2 * shard],
        ffn_out_bias_grad,
    )


def solution(mesh):
    both = ("grp", "wide")
    return jax.shard_map(
        functools.partial(body, mesh.shape["wide"]),
        mesh=mesh,
        in_specs=(
            P(both, None),
            P(both),
            P(both),
            P(),
            P(),
            P(),
            P(),
            P(),
            P(),
            P(),
            P(),
            P(),
            P(),
            P("grp", "wide", None),
            P("grp", "wide"),
            P("grp", "wide", None),
            P("grp", None),
            P(both, None),
        ),
        out_specs=(
            P(both, None),
            P(both, None),
            P(),
            P(),
            P(),
            P(),
            P(),
            P(),
            P(),
            P(),
            P(),
            P(),
            P("grp", "wide", None),
            P("grp", "wide"),
            P("grp", "wide", None),
            P("grp", None),
        ),
        check_vma=False,
    )
```
